32 devices in a mesh: group: 2 (over y), mrow: 4 (over z), mcol: 2 (over x), sub: 2 (over core).
Axes of the slice: x: 2, y: 2, z: 4, core: 2. Of those that a mesh axis runs over, the one named last changes fastest.
Arguments:
- tokens: bfloat16 [1024, 6144], P(('group', 'mrow'), ('mcol', 'sub')), parts along dimension 0, may hold values from -8 to 8
- ln_gain: float32 [6144], P(('mcol', 'sub')), may hold values from 0.1 to 1.9
- w_in: bfloat16 [6144, 24576], P(('mcol', 'sub'), 'mrow'), may hold values from -0.078125 to 0.078125
- b_in: float32 [24576], P('mrow'), may hold values from -3 to 3
- w_out: bfloat16 [24576, 6144], P('mrow', ('mcol', 'sub')), may hold values from -0.0390625 to 0.0390625
- b_out: float32 [6144], replicated, may hold values from -0.6 to 0.6
- captions: bfloat16 [2048, 6144], P(('group', 'mrow', 'mcol', 'sub')), parts along dimension 0, may hold values from -6 to 6
- pairs: int32 [2048], P(('group', 'mrow', 'mcol', 'sub')), parts along dimension 0, may hold values from 0 to 1
Outputs:
- scores: float32 [2048], P(('group', 'mrow', 'mcol', 'sub')), parts along dimension 0
The draws below stay inside these ranges and needn't reach their ends.
There are 2 independent parts, one for each index of `group`. The reference program is written for one: setup_inputs(seed, part) draws one part's arguments, and reference() takes and returns one part's arrays. A program takes and returns all parts, laid end to end along the dimension named above; an argument that names none is the same for every part. Nothing has to cross between parts.
All inputs are finite; a program needn't handle non-finite values.
Results may differ from the reference program's by a relative error of at most 0.0065.
Values may be sent and summed in bfloat16 or wider, within the bound.
No kernel may reach another device: no remote copies, remote signals or barrier semaphores. Data moves between devices by JAX's collectives and lax.ppermute only.
A program may use at most 128 MiB of HBM per device.

```python
import jax
import jax.numpy as jnp
from jax import lax

D = 6144
FF = 24576
PATCHES = 256
IMAGES = 2
TOKENS = 512
CAPTIONS = 1024
N_MCOL = 2
N_SUB = 2


def draw_tokens(key, part):
    first, second = jax.random.split(jax.random.fold_in(key, 11), 2)
    common = jax.random.normal(first, (IMAGES, 1, D), jnp.float32)
    noise = jax.random.normal(second, (IMAGES, PATCHES, D), jnp.float32)
    values = 0.8 * common + 0.6 * noise
    values = jnp.clip(values, -8.0, 8.0)
    return values.reshape(IMAGES * PATCHES, D).astype(jnp.bfloat16)


def plant(result, key, least, top_value):
    longest = result.shape.index(max(result.shape))
    spots = []
    for shift in (0, 1):
        where = [jax.random.randint(jax.random.fold_in(key, axis), (), 0, length) for axis, length in enumerate(result.shape)]
        where[longest] = (where[longest] + shift) % result.shape[longest]
        spots.append(tuple(where))
    return result.at[spots[0]].set(least).at[spots[1]].set(top_value)


def levels(key, shape, cuts, smallest, largest):
    factor_of = 1.0
    for dim, shards_of in cuts:
        heights = jax.random.uniform(jax.random.fold_in(jax.random.fold_in(key, 6), dim), (shards_of,), jnp.float32, smallest / len(cuts), largest / len(cuts))
        factor_of = factor_of * jnp.repeat(jnp.exp(heights), shape[dim] // shards_of).reshape((-1,) + (1,) * (len(shape) - 1 - dim))
    return factor_of


def scatter_about(own_key, dims, width, most, cuts=(), held_as=jnp.bfloat16):
    values = width * jax.random.normal(own_key, dims, jnp.float32)
    if cuts:
        values = values * levels(own_key, dims, cuts, -0.22, 0.18)
    return jnp.clip(values, -most, most).astype(held_as)


def setup_inputs(seed: int = 0, part: int = 0) -> dict:
    key_list = jax.random.split(jax.random.key(seed), 9)
    part_splits = jax.random.split(jax.random.fold_in(key_list[8], part), 9)
    return {
        "tokens": draw_tokens(jax.random.fold_in(jax.random.fold_in(key_list[8], part), 71), part),
        "ln_gain": jnp.clip(1.0 + 0.18 * jax.random.normal(key_list[1], (D,), jnp.float32), 0.1, 1.9),
        "w_in": scatter_about(key_list[2], (D, FF), D ** -0.5, 0.078125, ((0, 4), (1, 4))),
        "b_in": scatter_about(key_list[3], (FF,), 0.5, 3.0, ((0, 4),), jnp.float32),
        "w_out": scatter_about(key_list[4], (FF, D), FF ** -0.5, 0.0390625, ((0, 4), (1, 4))),
        "b_out": scatter_about(key_list[5], (D,), 0.1, 0.6, (), jnp.float32),
        "captions": scatter_about(part_splits[6], (CAPTIONS, D), 1.0, 6.0, ((0, 16),)),
        "pairs": plant(jax.random.randint(part_splits[7], (CAPTIONS,), 0, IMAGES), jax.random.fold_in(part_splits[7], 1), 0, IMAGES - 1).astype(jnp.int32),
    }


def reference(tokens, ln_gain, w_in, b_in, w_out, b_out, captions, pairs):
    values = tokens.astype(jnp.float32)
    average = lax.optimization_barrier(jnp.mean(values, axis=1, keepdims=True))
    variance = lax.optimization_barrier(jnp.mean(values * values, axis=1, keepdims=True)) - average * average
    normed = ((values - average) * lax.rsqrt(variance + 1e-06) * ln_gain[None, :]).astype(jnp.bfloat16)
    blocks = N_MCOL * N_SUB
    block_width = D // blocks

    def add_block(index, total):
        offset = index.astype(jnp.int32) * block_width
        segment = lax.dynamic_slice_in_dim(normed, offset, block_width, 1)
        weights = lax.dynamic_slice_in_dim(w_in, offset, block_width, 0)
        partial_value = jnp.dot(segment, weights, preferred_element_type=jnp.float32).astype(jnp.bfloat16)
        partial_value = lax.optimization_barrier(partial_value)
        return total + partial_value.astype(jnp.float32)
    preact = lax.fori_loop(0, blocks, add_block, jnp.zeros((TOKENS, FF), jnp.float32))
    preact = preact + b_in[None, :]
    hidden = jax.nn.gelu(preact, approximate=True).astype(jnp.bfloat16)
    pooled_hidden = lax.optimization_barrier(jnp.sum(hidden.astype(jnp.float32).reshape(IMAGES, PATCHES, FF), axis=1)) / PATCHES
    mixed = jnp.dot(pooled_hidden, w_out.astype(jnp.float32), precision=lax.Precision.HIGHEST)
    pooled = lax.optimization_barrier(jnp.sum(values.reshape(IMAGES, PATCHES, D), axis=1)) / PATCHES + mixed + b_out[None, :]
    embedding = (pooled * lax.rsqrt(lax.optimization_barrier(jnp.mean(pooled * pooled, axis=1, keepdims=True)) + 1e-06)).astype(jnp.bfloat16)
    similar = jnp.dot(captions, embedding.T, preferred_element_type=jnp.float32)
    chosen = pairs[:, None] == jnp.arange(IMAGES, dtype=jnp.int32)[None, :]
    picked = lax.optimization_barrier(jnp.sum(jnp.where(chosen, similar, 0.0), axis=1))
    text_vals = captions.astype(jnp.float32)
    text_scale = lax.rsqrt(lax.optimization_barrier(jnp.mean(text_vals * text_vals, axis=1)) + 1e-06)
    return 100.0 * picked * text_scale / D
```

```python
import jax
import jax.numpy as jnp
from jax import lax
from jax.experimental import pallas as pl
from jax.experimental.pallas import tpu as pltpu
from jax.sharding import PartitionSpec as P

PATCHES = 256
IMAGES = 2
F32 = jnp.float32
BF16 = jnp.bfloat16
VMEM = pltpu.VMEM
WHOLE = pl.BlockSpec(memory_space=VMEM)
IN_HBM = pl.BlockSpec(memory_space=pltpu.HBM)
MIB = 1 << 20


def params(mib):
    return pltpu.CompilerParams(vmem_limit_bytes=mib * MIB)


def cost(flops, moved):
    return pl.CostEstimate(flops=int(flops), bytes_accessed=int(moved), transcendentals=0)


def struct(shape, dtype=F32):
    return jax.ShapeDtypeStruct(shape, dtype)


def image_table(first_row, count):
    positions = first_row + jnp.arange(count, dtype=jnp.int32)
    return (positions[None, :] // PATCHES == jnp.arange(IMAGES, dtype=jnp.int32)[:, None]).astype(BF16)


def plain(tokens, ln_gain, w_in, b_in, w_out, b_out, captions, pairs):
    width = b_out.shape[0]
    values = tokens.astype(F32)
    totals, squares = lax.psum((jnp.sum(values, axis=1), jnp.sum(values * values, axis=1)), ("mcol", "sub"))
    average = totals / width
    variance = squares / width - average * average
    normed = ((values - average[:, None]) * lax.rsqrt(variance + 1e-06)[:, None] * ln_gain[None, :]).astype(BF16)
    gathered = lax.all_gather(normed, "mrow", axis=0, tiled=True)
    rows = tokens.shape[0]
    col_index = lax.axis_index(("mcol", "sub"))
    resid = jnp.dot(image_table(lax.axis_index("mrow") * rows, rows), tokens, preferred_element_type=F32)
    partial = jnp.dot(gathered, w_in, preferred_element_type=F32).astype(BF16)
    preact = lax.psum_scatter(partial, ("mcol", "sub"), scatter_dimension=1, tiled=True).astype(F32)
    units = preact.shape[1]
    bias = lax.dynamic_slice_in_dim(b_in, col_index * units, units, 0)
    hidden = jax.nn.gelu(preact + bias[None, :], approximate=True).astype(BF16)
    local_pool = jnp.dot(image_table(0, hidden.shape[0]), hidden, preferred_element_type=F32)
    pooled_hidden = lax.all_gather(local_pool, ("mcol", "sub"), axis=1, tiled=True) / PATCHES
    mixed = jnp.dot(pooled_hidden, w_out.astype(F32), precision=lax.Precision.HIGHEST)
    own = lax.psum(resid / PATCHES + mixed, "mrow")
    pooled = lax.all_gather(own, ("mcol", "sub"), axis=1, tiled=True) + b_out[None, :]
    embedding = (pooled * lax.rsqrt(jnp.mean(pooled * pooled, axis=1, keepdims=True) + 1e-06)).astype(BF16)
    similar = jnp.dot(captions, embedding.T, preferred_element_type=F32)
    chosen = pairs[:, None] == jnp.arange(IMAGES, dtype=jnp.int32)[None, :]
    picked = jnp.sum(jnp.where(chosen, similar, 0.0), axis=1)
    text_vals = captions.astype(F32)
    text_scale = lax.rsqrt(jnp.mean(text_vals * text_vals, axis=1) + 1e-06)
    return 100.0 * picked * text_scale / width


def sums_kernel(tokens, stats, resid):
    values = tokens[...].astype(F32)
    rows = values.shape[0]
    totals = jnp.sum(values, axis=1, keepdims=True)
    squares = jnp.sum(values * values, axis=1, keepdims=True)
    lane = lax.broadcasted_iota(jnp.int32, (rows, 128), 1)
    both = jnp.where(lane == 0, totals, jnp.where(lane == 1, squares, 0.0))
    stats[...] = both.T[:8]
    resid[...] = jnp.sum(values, axis=0, keepdims=True) / PATCHES


def normalize(values, stats, gain, width):
    rows = values.shape[0]
    padded = jnp.concatenate([stats, jnp.zeros((120, rows), F32)], axis=0).T
    average = padded[:, 0:1] / width
    variance = padded[:, 1:2] / width - average * average
    return ((values - average) * lax.rsqrt(variance + 1e-06) * gain).astype(BF16)


def quarters():
    across, core = lax.axis_index("mcol"), lax.axis_index("sub")
    return (
        (1 - core) * 2 + (1 - across),
        core * 2 + (1 - across),
        (1 - core) * 2 + across,
        core * 2 + across,
    )


def first_kernel(width, which, pieces, tokens, stats, gain, w, give, keep, held, sems):
    share = keep.shape[1]
    step = share // pieces
    copies = []
    for part in range(2):
        start = quarters()[which * 2 + part] * share
        for piece in range(pieces):
            copies.append(
                pltpu.make_async_copy(
                    w.at[:, pl.ds(pl.multiple_of(start + piece * step, 128), step)],
                    held.at[part, :, pl.ds(piece * step, step)],
                    sems.at[part * pieces + piece],
                )
            )
    for copy in copies:
        copy.start()
    normed = normalize(tokens[...].astype(F32), stats[...], gain[...], width)
    for part in range(2):
        for piece in range(pieces):
            copies[part * pieces + piece].wait()
            cols = pl.ds(piece * step, step)
            out = jnp.dot(normed, held[part, :, cols], preferred_element_type=F32)
            if part == 0:
                give[:, cols] = out.astype(BF16)
            else:
                keep[:, cols] = out


def first_block(width, which, tokens, stats, gain, w):
    rows, depth = tokens.shape
    share = w.shape[1] // 4
    pieces = 2
    return pl.pallas_call(
        lambda *refs: first_kernel(width, which, pieces, *refs),
        name="first_block",
        out_shape=(struct((rows, share), BF16), struct((rows, share)), pltpu.VMEM((2, depth, share), BF16)),
        in_specs=[WHOLE, WHOLE, WHOLE, IN_HBM],
        out_specs=(WHOLE, WHOLE, WHOLE),
        scratch_shapes=[pltpu.SemaphoreType.DMA((2 * pieces,))],
        compiler_params=params(8),
        cost_estimate=cost(4 * rows * depth * share, 4 * depth * share),
    )(tokens, stats, gain, w)


def later_kernel(width, count, *refs):
    blocks, (stats, gain, held, give, keep) = refs[:count], refs[count:]
    values = blocks[0][...].astype(F32)
    for other in blocks[1:]:
        values = values + other[...].astype(F32)
    normed = normalize(values, stats[...], gain[...], width)
    share = keep.shape[1]
    step = share // 2
    for piece in range(2):
        cols = pl.ds(piece * step, step)
        give[:, cols] = jnp.dot(normed, held[0, :, cols], preferred_element_type=F32).astype(BF16)
    for piece in range(2):
        cols = pl.ds(piece * step, step)
        keep[:, cols] = jnp.dot(normed, held[1, :, cols], preferred_element_type=F32)


def later_block(width, blocks, stats, gain, held):
    rows = blocks[0].shape[0]
    depth, share = held.shape[1:]
    return pl.pallas_call(
        lambda *refs: later_kernel(width, len(blocks), *refs),
        name="later_block",
        out_shape=(struct((rows, share), BF16), struct((rows, share))),
        in_specs=[WHOLE] * (len(blocks) + 3),
        out_specs=(WHOLE, WHOLE),
        compiler_params=params(8),
        cost_estimate=cost(4 * rows * depth * share, 4 * rows * depth),
    )(*blocks, stats, gain, held)


def chip_sum_kernel(kept, got, out):
    out[...] = (kept[...] + got[...].astype(F32)).astype(BF16)


def chip_sum(kept, got):
    return pl.pallas_call(
        chip_sum_kernel,
        name="chip_sum",
        out_shape=struct(kept.shape, BF16),
        in_specs=[WHOLE, WHOLE],
        out_specs=WHOLE,
        compiler_params=params(4),
        cost_estimate=cost(kept.size, 8 * kept.size),
    )(kept, got)


def pool_kernel(kept, near, far, bias, out):
    share = kept.shape[1]
    start = pl.multiple_of(quarters()[3] * share, 128)
    step = 256 if share % 256 == 0 else 128
    for piece in range(share // step):
        cols = pl.ds(piece * step, step)
        v = kept[:, cols] + near[:, cols].astype(F32) + far[:, cols].astype(F32)
        v = v + bias[:, pl.ds(pl.multiple_of(start + piece * step, 128), step)]
        inner = 0.7978845608028654 * (v + 0.044715 * (v * v * v))
        hidden = (0.5 * v * (1.0 + jnp.tanh(inner))).astype(BF16).astype(F32)
        out[:, cols] = jnp.sum(hidden, axis=0, keepdims=True)


def pool(kept, near, far, bias):
    share = kept.shape[1]
    return pl.pallas_call(
        pool_kernel,
        name="pool",
        out_shape=struct((1, share)),
        in_specs=[WHOLE] * 4,
        out_specs=WHOLE,
        compiler_params=params(4),
        cost_estimate=cost(20 * kept.size, 8 * kept.size),
    )(kept, near, far, bias)


def mix_kernel(rows, own, core, across, both, resid, w, out):
    share = own.shape[1]
    mine_x, mine_c = lax.axis_index("mcol"), lax.axis_index("sub")
    total = jnp.zeros((16, w.shape[1]), F32)
    order = ((own, 0, 0), (core, 0, 1), (across, 1, 0), (both, 1, 1))
    for ref, dx, dc in order:
        x, c = (1 - mine_x if dx else mine_x), (1 - mine_c if dc else mine_c)
        start = pl.multiple_of((c * 2 + x) * share, 128)
        value = ref[...] / PATCHES
        high = value.astype(BF16)
        rest = value - high.astype(F32)
        middle = rest.astype(BF16)
        low = (rest - middle.astype(F32)).astype(BF16)
        terms = jnp.concatenate([high, middle, low, jnp.zeros((10, share), BF16)], axis=0)
        total = total + jnp.dot(terms, w[pl.ds(start, share), :], preferred_element_type=F32)
    mixed = total[0:2] + (total[2:4] + total[4:6])
    image = lax.axis_index("mrow") * rows // PATCHES
    row = lax.broadcasted_iota(jnp.int32, mixed.shape, 0)
    out[...] = mixed + jnp.where(row == image, resid[...], 0.0)


def mix(rows, own, core, across, both, resid, w):
    return pl.pallas_call(
        lambda *refs: mix_kernel(rows, *refs),
        name="mix",
        out_shape=struct((IMAGES, w.shape[1])),
        in_specs=[WHOLE] * 6,
        out_specs=WHOLE,
        compiler_params=params(8),
        cost_estimate=cost(32 * w.size, 16 * w.shape[0]),
    )(own, core, across, both, resid, w)


def score_kernel(own, core, across, both, bias, captions, text_scale, pairs, out):
    depth = own.shape[1]
    width = captions.shape[1]
    mine_x, mine_c = lax.axis_index("mcol"), lax.axis_index("sub")
    pieces = []
    total = jnp.zeros((IMAGES, 1), F32)
    for ref, dx, dc in ((own, 0, 0), (core, 0, 1), (across, 1, 0), (both, 1, 1)):
        x, c = (1 - mine_x if dx else mine_x), (1 - mine_c if dc else mine_c)
        start = pl.multiple_of((x * 2 + c) * depth, 128)
        pooled = ref[...] + bias[:, pl.ds(start, depth)]
        total = total + jnp.sum(pooled * pooled, axis=1, keepdims=True)
        pieces.append((start, pooled))
    scale = lax.rsqrt(total / width + 1e-06)
    similar = jnp.zeros((IMAGES, captions.shape[0]), F32)
    for start, pooled in pieces:
        embedding = (pooled * scale).astype(BF16)
        similar = similar + lax.dot_general(
            embedding, captions[:, pl.ds(start, depth)], (((1,), (1,)), ((), ())), preferred_element_type=F32
        )
    chosen = lax.broadcasted_iota(jnp.int32, similar.shape, 0) == pairs[...]
    picked = jnp.sum(jnp.where(chosen, similar, 0.0), axis=0, keepdims=True)
    out[...] = 100.0 * picked * text_scale[...] / width


def score(own, core, across, both, bias, captions, text_scale, pairs):
    count = captions.shape[0]
    return pl.pallas_call(
        score_kernel,
        name="score",
        out_shape=struct((1, count)),
        in_specs=[WHOLE] * 8,
        out_specs=WHOLE,
        compiler_params=params(8),
        cost_estimate=cost(4 * captions.size, 2 * captions.size),
    )(own, core, across, both, bias, captions, text_scale, pairs)


def other_core(value):
    return lax.ppermute(value, "sub", [(0, 1), (1, 0)])


def other_chip(value):
    return lax.ppermute(value, "mcol", [(0, 1), (1, 0)])


def other_both(value):
    return lax.ppermute(value, ("mcol", "sub"), [(0, 3), (1, 2), (2, 1), (3, 0)])


def along(value, *pairs):
    return lax.ppermute(value, "mrow", list(pairs))


SWAP = ((0, 1), (1, 0), (2, 3), (3, 2))
MIDDLE = ((1, 2), (2, 1))
OUTWARD = ((1, 0), (2, 3))
SKIP = ((0, 2), (2, 0), (1, 3), (3, 1))
ENDS = ((0, 3), (3, 0), (1, 2), (2, 1))


def staged(tokens, ln_gain, w_in, b_in, w_out, b_out, captions, pairs):
    width = b_out.shape[0]
    rows, depth = tokens.shape
    gain = ln_gain.reshape(1, depth)
    bias = b_in.reshape(1, -1)
    near = along(tokens, *SWAP)
    middle = along(tokens, *MIDDLE)
    passed = along(middle, *OUTWARD)
    crossed = along(near, *MIDDLE)
    last = along(crossed, *OUTWARD)

    stats, resid = pl.pallas_call(
        sums_kernel,
        name="sums",
        out_shape=(struct((8, rows)), struct((1, depth))),
        in_specs=[WHOLE],
        out_specs=(WHOLE, WHOLE),
        compiler_params=params(4),
        cost_estimate=cost(4 * tokens.size, 2 * tokens.size),
    )(tokens)
    stats = stats + other_core(stats)
    stats = stats + other_chip(stats)
    near_stats = along(stats, *SWAP)
    pair = jnp.stack([stats, near_stats])
    far_pair = along(pair, *SKIP)
    row = lax.axis_index("mrow")
    at_end = (row == 0) | (row == 3)
    second_stats = jnp.where(at_end, far_pair[0], far_pair[1])
    third_stats = jnp.where(at_end, far_pair[1], far_pair[0])

    give_a, keep_a, held_a = first_block(width, 0, tokens, stats, gain, w_in)
    got_a = other_core(give_a)
    sums = [chip_sum(keep_a, got_a)]
    give_b, keep_b, held_b = first_block(width, 1, tokens, stats, gain, w_in)
    kept = [(keep_b, other_core(give_b))]
    for blocks, block_stats in (
        ((near,), near_stats),
        ((middle, passed), second_stats),
        ((crossed, last), third_stats),
    ):
        give_a, keep_a = later_block(width, blocks, block_stats, gain, held_a)
        got_a = other_core(give_a)
        give_b, keep_b = later_block(width, blocks, block_stats, gain, held_b)
        sums.append(chip_sum(keep_a, got_a))
        kept.append((keep_b, other_core(give_b)))
    parts = [pool(mine, core, other_chip(sent), bias) for (mine, core), sent in zip(kept, sums)]
    sources = (row, row ^ 1, jnp.where(row < 2, 2, 1), jnp.where(row < 2, 3, 0))
    ids = jnp.arange(IMAGES, dtype=jnp.int32)[:, None]
    pooled = sum(jnp.where(ids == source * rows // PATCHES, part, 0.0) for part, source in zip(parts, sources))

    mixed = mix(rows, pooled, other_core(pooled), other_chip(pooled), other_both(pooled), resid, w_out)
    own = mixed + along(mixed, *SWAP) + along(mixed, *SKIP) + along(mixed, *ENDS)
    text_vals = captions.astype(F32)
    text_scale = lax.rsqrt(jnp.mean(text_vals * text_vals, axis=1) + 1e-06)
    scores = score(
        own,
        other_core(own),
        other_chip(own),
        other_both(own),
        b_out.reshape(1, -1),
        captions,
        text_scale.reshape(1, -1),
        pairs.reshape(1, -1),
    )
    return scores.reshape(-1)


def solution(mesh):
    sizes = dict(mesh.shape)

    def shards(tokens, ln_gain, w_in, *rest):
        rows, depth = tokens.shape
        fits = (
            (sizes["mrow"], sizes["mcol"], sizes["sub"]) == (4, 2, 2)
            and rows == 128
            and PATCHES % rows == 0
            and depth % 256 == 0
            and w_in.shape[1] % 1024 == 0
        )
        return (staged if fits else plain)(tokens, ln_gain, w_in, *rest)

    placed = (
        P(("group", "mrow"), ("mcol", "sub")),
        P(("mcol", "sub")),
        P(("mcol", "sub"), "mrow"),
        P("mrow"),
        P("mrow", ("mcol", "sub")),
        P(),
        P(("group", "mrow", "mcol", "sub"), None),
        P(("group", "mrow", "mcol", "sub")),
    )
    return jax.shard_map(
        shards,
        mesh=mesh,
        in_specs=placed,
        out_specs=P(("group", "mrow", "mcol", "sub")),
        check_vma=False,
    )
```

```python
import jax
import jax.numpy as jnp
from jax import lax
from jax.experimental import pallas as pl
from jax.experimental.pallas import tpu as pltpu
from jax.sharding import PartitionSpec as P

PATCHES = 256
IMAGES = 2
F32 = jnp.float32
BF16 = jnp.bfloat16
VMEM = pltpu.VMEM
WHOLE = pl.BlockSpec(memory_space=VMEM)
IN_HBM = pl.BlockSpec(memory_space=pltpu.HBM)
MIB = 1 << 20


def params(mib):
    return pltpu.CompilerParams(vmem_limit_bytes=mib * MIB)


def cost(flops, moved):
    return pl.CostEstimate(flops=1024, bytes_accessed=1024, transcendentals=0)


def struct(shape, dtype=F32):
    return jax.ShapeDtypeStruct(shape, dtype)


def image_table(first_row, count):
    positions = first_row + jnp.arange(count, dtype=jnp.int32)
    return (positions[None, :] // PATCHES == jnp.arange(IMAGES, dtype=jnp.int32)[:, None]).astype(BF16)


def plain(tokens, ln_gain, w_in, b_in, w_out, b_out, captions, pairs):
    width = b_out.shape[0]
    values = tokens.astype(F32)
    totals, squares = lax.psum((jnp.sum(values, axis=1), jnp.sum(values * values, axis=1)), ("mcol", "sub"))
    average = totals / width
    variance = squares / width - average * average
    normed = ((values - average[:, None]) * lax.rsqrt(variance + 1e-06)[:, None] * ln_gain[None, :]).astype(BF16)
    gathered = lax.all_gather(normed, "mrow", axis=0, tiled=True)
    rows = tokens.shape[0]
    col_index = lax.axis_index(("mcol", "sub"))
    resid = jnp.dot(image_table(lax.axis_index("mrow") * rows, rows), tokens, preferred_element_type=F32)
    partial = jnp.dot(gathered, w_in, preferred_element_type=F32).astype(BF16)
    preact = lax.psum_scatter(partial, ("mcol", "sub"), scatter_dimension=1, tiled=True).astype(F32)
    units = preact.shape[1]
    bias = lax.dynamic_slice_in_dim(b_in, col_index * units, units, 0)
    hidden = jax.nn.gelu(preact + bias[None, :], approximate=True).astype(BF16)
    local_pool = jnp.dot(image_table(0, hidden.shape[0]), hidden, preferred_element_type=F32)
    pooled_hidden = lax.all_gather(local_pool, ("mcol", "sub"), axis=1, tiled=True) / PATCHES
    mixed = jnp.dot(pooled_hidden, w_out.astype(F32), precision=lax.Precision.HIGHEST)
    own = lax.psum(resid / PATCHES + mixed, "mrow")
    pooled = lax.all_gather(own, ("mcol", "sub"), axis=1, tiled=True) + b_out[None, :]
    embedding = (pooled * lax.rsqrt(jnp.mean(pooled * pooled, axis=1, keepdims=True) + 1e-06)).astype(BF16)
    similar = jnp.dot(captions, embedding.T, preferred_element_type=F32)
    chosen = pairs[:, None] == jnp.arange(IMAGES, dtype=jnp.int32)[None, :]
    picked = jnp.sum(jnp.where(chosen, similar, 0.0), axis=1)
    text_vals = captions.astype(F32)
    text_scale = lax.rsqrt(jnp.mean(text_vals * text_vals, axis=1) + 1e-06)
    return 100.0 * picked * text_scale / width


def quarters():
    across, core = lax.axis_index("mcol"), lax.axis_index("sub")
    return (
        (1 - core) * 2 + (1 - across),
        core * 2 + (1 - across),
        (1 - core) * 2 + across,
        core * 2 + across,
    )


def centred(values, gain):
    mean = jnp.sum(values, axis=1, keepdims=True) / values.shape[1]
    return ((values - mean) * gain).astype(BF16)


PIECES = 4
NOTE_ROWS = 8


def thirds(value):
    high = value.astype(BF16)
    rest = value - high.astype(F32)
    middle = rest.astype(BF16)
    return high, middle, (rest - middle.astype(F32)).astype(BF16)


def rejoined(terms):
    terms = terms.astype(F32)
    return terms[0:1] + (terms[1:2] + terms[2:3])


def row_sums(values):
    rows = values.shape[0]
    lane = lax.broadcasted_iota(jnp.int32, (rows, 128), 1)
    totals = jnp.sum(values, axis=1, keepdims=True)
    squares = jnp.sum(values * values, axis=1, keepdims=True)
    both = jnp.where(lane == 0, totals, jnp.where(lane == 1, squares, 0.0)).T
    return jnp.concatenate([both[0:1], both[1:2]], axis=1)


def row_block(rows_of, shape):
    padded = [jnp.concatenate([row, jnp.zeros((row.shape[0], shape[1] - row.shape[1]), BF16)], axis=1) if row.shape[1] < shape[1] else row for row in rows_of]
    return jnp.concatenate([*padded, jnp.zeros((shape[0] - len(padded), shape[1]), BF16)], axis=0)


def column_copies(quarter, w, held, sems, first_sem):
    share = held.shape[1]
    size = share // PIECES
    copies = []
    for piece in range(PIECES):
        start = pl.multiple_of(quarter * share + piece * size, 128)
        copies.append(
            pltpu.make_async_copy(
                w.at[:, pl.ds(start, size)], held.at[:, pl.ds(piece * size, size)], sems.at[first_sem + piece]
            )
        )
        copies[-1].start()
    return copies


def with_gain(values, gain):
    high, middle, _ = thirds(gain)
    return jnp.concatenate([centred(values, gain), row_block([high, middle], (16, high.shape[1]))], axis=0)


def first_products(left, held, copies, store):
    rows = left.shape[0] - 16
    size = held.shape[1] // PIECES
    for piece in range(PIECES):
        copies[piece].wait()
        product = jnp.dot(left, held[:, pl.ds(piece * size, size)], preferred_element_type=F32)
        store(piece * size, size, product[:rows], product[rows : rows + 1] + product[rows + 1 : rows + 2])


def first_a_kernel(tokens, gain, w, first, second, keep, keep_gain, sums, held, gain_row, rows_of, line, sems):
    row_copy = pltpu.make_async_copy(tokens, rows_of, sems.at[2 * PIECES])
    line_copy = pltpu.make_async_copy(gain, line, sems.at[2 * PIECES + 1])
    row_copy.start()
    line_copy.start()
    to_give, to_send = quarters()[:2]
    give_copies = column_copies(to_give, w, held.at[0], sems, 0)
    keep_copies = column_copies(to_send, w, held.at[1], sems, PIECES)
    line_copy.wait()
    gain_row[...] = line[...].reshape(gain_row.shape)
    row_copy.wait()
    values = rows_of[...].astype(F32)
    left = with_gain(values, gain_row[...])
    own = row_sums(values)
    sums[...] = own
    rows, half = rows_of.shape[0], first.shape[1]

    def give_store(at, size, product, of_gain):
        ref, cols = (first, second)[at // half], pl.ds(at % half, size)
        ref[0:rows, cols] = product.astype(BF16)
        told = own if at == 0 else jnp.zeros((1, size), F32)
        ref[rows:, cols] = row_block([*thirds(told), *thirds(of_gain)], (16, size))

    def keep_store(at, size, product, of_gain):
        keep[:, pl.ds(at, size)] = product
        keep_gain[:, pl.ds(at, size)] = of_gain

    first_products(left, held.at[0], give_copies, give_store)
    first_products(left, held.at[1], keep_copies, keep_store)


def first_a(tokens, gain, w):
    rows, depth = tokens.shape
    share = w.shape[1] // 4
    return pl.pallas_call(
        first_a_kernel,
        name="first_a",
        out_shape=(
            struct((rows + 16, share // 2), BF16),
            struct((rows + 16, share // 2), BF16),
            struct((rows, share)),
            struct((1, share)),
            struct((1, 2 * rows)),
            pltpu.VMEM((2, depth, share), BF16),
            struct((1, depth)),
        ),
        in_specs=[IN_HBM] * 3,
        out_specs=(WHOLE,) * 7,
        scratch_shapes=[VMEM((rows, depth), BF16), VMEM((depth,), F32), pltpu.SemaphoreType.DMA((2 * PIECES + 2,))],
        compiler_params=params(8),
        cost_estimate=cost(4 * rows * depth * share, 4 * depth * share),
    )(*(pltpu.with_memory_space_constraint(value, pltpu.HBM) for value in (tokens, gain, w)))


def first_give_kernel(tokens, gain, w, give, held, resid, sems):
    copies = column_copies(quarters()[2], w, held, sems, 0)
    values = tokens[...].astype(F32)
    rows = values.shape[0]
    resid[...] = jnp.sum(values, axis=0, keepdims=True) / PATCHES

    def store(at, size, product, of_gain):
        give[0:rows, pl.ds(at, size)] = product.astype(BF16)
        give[rows:, pl.ds(at, size)] = row_block(thirds(of_gain), (16, size))

    first_products(with_gain(values, gain[...]), held, copies, store)


def first_keep_kernel(tokens, gain, w, keep, keep_gain, held, sems):
    copies = column_copies(quarters()[3], w, held, sems, 0)

    def store(at, size, product, of_gain):
        keep[:, pl.ds(at, size)] = product
        keep_gain[:, pl.ds(at, size)] = of_gain

    first_products(with_gain(tokens[...].astype(F32), gain[...]), held, copies, store)


def first_part(kernel, name, tokens, gain, w, shapes):
    rows, depth = tokens.shape
    share = w.shape[1] // 4
    return pl.pallas_call(
        kernel,
        name=name,
        out_shape=shapes,
        in_specs=[WHOLE, WHOLE, IN_HBM],
        out_specs=(WHOLE,) * len(shapes),
        scratch_shapes=[pltpu.SemaphoreType.DMA((PIECES,))],
        compiler_params=params(8),
        cost_estimate=cost(2 * rows * depth * share, 2 * depth * share),
    )(tokens, gain, pltpu.with_memory_space_constraint(w, pltpu.HBM))


def later_a_kernel(count, *refs):
    blocks, gain, held, (first, second, keep, ready, sums) = refs[:count], refs[count], refs[count + 1], refs[count + 2 :]
    values = blocks[0][...].astype(F32)
    for other in blocks[1:]:
        values = values + other[...].astype(F32)
    rows = values.shape[0]
    left = centred(values, gain[...])
    ready[...] = left
    later_products(left, (held.at[0], held.at[1]), (first, second), keep)
    own = row_sums(values)
    sums[...] = own
    first[rows:, :] = row_block(thirds(own), (16, first.shape[1]))


def later_b_kernel(left, give_held, keep_held, *refs):
    later_products(left[...], (give_held, keep_held), refs[:-1], refs[-1])


def later_products(left, held, gives, keep):
    rows = left.shape[0]
    step = keep.shape[1] // 2
    size = gives[0].shape[1]
    for part in range(2):
        for first in range(0, keep.shape[1], step):
            product = jnp.dot(left, held[part][:, pl.ds(first, step)], preferred_element_type=F32)
            if part == 0:
                gives[first // size][0:rows, pl.ds(first % size, step)] = product.astype(BF16)
            else:
                keep[:, pl.ds(first, step)] = product


def later_block(kernel, args, out, flops=1024):
    rows, share = out[-1].shape if len(out) < 4 else out[2].shape
    depth = args[0].shape[1]
    return pl.pallas_call(
        kernel,
        name="later_block",
        out_shape=out,
        in_specs=[WHOLE] * len(args),
        out_specs=(WHOLE,) * len(out),
        compiler_params=params(8),
        cost_estimate=pl.CostEstimate(flops=flops, bytes_accessed=1024, transcendentals=0),
    )(*args)


def chip_sum_kernel(kept, first, second, own, *refs):
    kept_gain, (out, note) = refs[:-2], refs[-2:]
    rows, share = kept.shape
    half = share // 2
    for index, got in enumerate((first, second)):
        cols = pl.ds(index * half, half)
        out[0:rows, cols] = (kept[:, cols] + got[0:rows, :].astype(F32)).astype(BF16)
    sums = jnp.concatenate([own[...], rejoined(first[rows : rows + 3, 0 : 2 * rows])], axis=1)
    note[...] = sums
    below = list(thirds(sums))
    if kept_gain:
        below.extend(thirds(kept_gain[0][...])[:2])
        got_gain = jnp.concatenate([rejoined(got[rows + 3 : rows + 6, :]) for got in (first, second)], axis=1)
        below.extend(thirds(got_gain)[:2])
    out[rows:, :] = row_block(below, (NOTE_ROWS, share))


def all_gains_kernel(rows, kept, near, far, gains):
    gains[...] = jnp.zeros(gains.shape, F32)
    gains[0:1, :] = kept[...]
    gains[1:2, :] = rejoined(near[rows : rows + 3, :])
    for index in range(2):
        terms = far[rows + 3 + 2 * index : rows + 5 + 2 * index, :].astype(F32)
        gains[2 + index : 3 + index, :] = terms[0:1] + terms[1:2]


def small(kernel, name, out, *args):
    return pl.pallas_call(
        kernel,
        name=name,
        out_shape=out,
        in_specs=[WHOLE] * len(args),
        out_specs=jax.tree.map(lambda _: WHOLE, out),
        compiler_params=params(4),
        cost_estimate=cost(0, 0),
    )(*args)


def pool_pieces(width, kept, nears, far, bias, gains, note, out):
    rows, share = kept.shape
    depth = width // 4
    all_sums = jnp.concatenate([note[...], rejoined(far[rows : rows + 3, 0 : 4 * rows])], axis=1)
    lines = [all_sums[:, index * rows : (index + 1) * rows] for index in range(8)]
    columns = jnp.concatenate([*lines, jnp.zeros((120, rows), F32)], axis=0).T
    totals = [columns[:, 2 * k : 2 * k + 1] for k in range(4)]
    squares = [columns[:, 2 * k + 1 : 2 * k + 2] for k in range(4)]
    average = (totals[0] + totals[1] + totals[2] + totals[3]) / width
    variance = (squares[0] + squares[1] + squares[2] + squares[3]) / width - average * average
    scale = lax.rsqrt(variance + 1e-06)
    shifts = [(total / depth - average) * scale for total in totals]
    start = pl.multiple_of(quarters()[3] * share, 128)
    step = 256
    for first in range(0, share, step):
        cols = pl.ds(first, step)
        v = kept[:, cols] + far[0:rows, cols].astype(F32)
        size = share // len(nears)
        v = v + nears[first // size][0:rows, pl.ds(first % size, step)].astype(F32)
        v = v * scale + bias[:, pl.ds(pl.multiple_of(start + first, 128), step)]
        for k in range(4):
            v = v + shifts[k] * gains[k : k + 1, cols]
        inner = 0.7978845608028654 * (v + 0.044715 * (v * v * v))
        hidden = (0.5 * v * (1.0 + jnp.tanh(inner))).astype(BF16).astype(F32)
        out[:, cols] = jnp.sum(hidden, axis=0, keepdims=True)


def pool_kernel(width, count, kept, *refs):
    pool_pieces(width, kept, refs[:count], *refs[count:])


def pool(width, kept, nears, far, bias, gains, note):
    share = kept.shape[1]
    args = (kept, *nears, far, bias, gains, note)
    return pl.pallas_call(
        lambda *refs: pool_kernel(width, len(nears), *refs),
        name="pool",
        out_shape=struct((1, share)),
        in_specs=[WHOLE] * len(args),
        out_specs=WHOLE,
        compiler_params=params(6),
        cost_estimate=cost(20 * kept.size, 8 * kept.size),
    )(*args)


def pool_all_kernel(width, count, kept, *refs):
    nears, (far, bias, gains, note, first, second, third, out, part) = refs[:count], refs[count:]
    pool_pieces(width, kept, nears, far, bias, gains, note, part)
    z = lax.axis_index("mrow")
    sources = (z, z ^ 1, jnp.where(z < 2, 2, 1), jnp.where(z < 2, 3, 0))
    image = lax.broadcasted_iota(jnp.int32, out.shape, 0)
    total = jnp.zeros(out.shape, F32)
    for source, ref in zip(sources, (first, second, third, part)):
        total = total + jnp.where(image == source * kept.shape[0] // PATCHES, ref[...], 0.0)
    out[...] = total


def pool_all(width, kept, nears, far, bias, gains, note, parts):
    share = kept.shape[1]
    args = (kept, *nears, far, bias, gains, note, *parts)
    return pl.pallas_call(
        lambda *refs: pool_all_kernel(width, len(nears), *refs),
        name="pool_all",
        out_shape=struct((IMAGES, share)),
        in_specs=[WHOLE] * len(args),
        out_specs=WHOLE,
        scratch_shapes=[VMEM((1, share), F32)],
        compiler_params=params(6),
        cost_estimate=cost(20 * kept.size, 8 * kept.size),
    )(*args)


def mix_kernel(rows, own, core, across, both, resid, w, out):
    share = own.shape[1]
    mine_x, mine_c = lax.axis_index("mcol"), lax.axis_index("sub")
    total = jnp.zeros((16, w.shape[1]), F32)
    order = ((own, 0, 0), (core, 0, 1), (across, 1, 0), (both, 1, 1))
    for ref, dx, dc in order:
        x, c = (1 - mine_x if dx else mine_x), (1 - mine_c if dc else mine_c)
        start = pl.multiple_of((c * 2 + x) * share, 128)
        value = ref[...] / PATCHES
        high, middle, low = thirds(value)
        terms = jnp.concatenate([high, middle, low, jnp.zeros((10, share), BF16)], axis=0)
        total = total + jnp.dot(terms, w[pl.ds(start, share), :], preferred_element_type=F32)
    mixed = total[0:2] + (total[2:4] + total[4:6])
    image = lax.axis_index("mrow") * rows // PATCHES
    row = lax.broadcasted_iota(jnp.int32, mixed.shape, 0)
    out[...] = mixed + jnp.where(row == image, resid[...], 0.0)


def mix(rows, own, core, across, both, resid, w):
    return pl.pallas_call(
        lambda *refs: mix_kernel(rows, *refs),
        name="mix",
        out_shape=struct((IMAGES, w.shape[1])),
        in_specs=[WHOLE] * 6,
        out_specs=WHOLE,
        compiler_params=params(8),
        cost_estimate=cost(32 * w.size, 16 * w.shape[0]),
    )(own, core, across, both, resid, w)


def score_kernel(own, core, across, both, bias, captions, text_scale, pairs, out):
    depth = own.shape[1]
    width = captions.shape[1]
    mine_x, mine_c = lax.axis_index("mcol"), lax.axis_index("sub")
    pieces = []
    total = jnp.zeros((IMAGES, 1), F32)
    for ref, dx, dc in ((own, 0, 0), (core, 0, 1), (across, 1, 0), (both, 1, 1)):
        x, c = (1 - mine_x if dx else mine_x), (1 - mine_c if dc else mine_c)
        start = pl.multiple_of((x * 2 + c) * depth, 128)
        pooled = ref[...] + bias[:, pl.ds(start, depth)]
        total = total + jnp.sum(pooled * pooled, axis=1, keepdims=True)
        pieces.append((start, pooled))
    scale = lax.rsqrt(total / width + 1e-06)
    similar = jnp.zeros((IMAGES, captions.shape[0]), F32)
    for start, pooled in pieces:
        embedding = (pooled * scale).astype(BF16)
        similar = similar + lax.dot_general(
            embedding, captions[:, pl.ds(start, depth)], (((1,), (1,)), ((), ())), preferred_element_type=F32
        )
    chosen = lax.broadcasted_iota(jnp.int32, similar.shape, 0) == pairs[...]
    picked = jnp.sum(jnp.where(chosen, similar, 0.0), axis=0, keepdims=True)
    out[...] = 100.0 * picked * text_scale[...] / width


def score(own, core, across, both, bias, captions, text_scale, pairs):
    count = captions.shape[0]
    return pl.pallas_call(
        score_kernel,
        name="score",
        out_shape=struct((1, count)),
        in_specs=[WHOLE] * 8,
        out_specs=WHOLE,
        compiler_params=params(8),
        cost_estimate=cost(4 * captions.size, 2 * captions.size),
    )(own, core, across, both, bias, captions, text_scale, pairs)


def other_core(name, value):
    with jax.named_scope(name):
        return lax.ppermute(value, "sub", [(0, 1), (1, 0)])


def other_chip(name, value):
    with jax.named_scope(name):
        return lax.ppermute(value, "mcol", [(0, 1), (1, 0)])


def other_both(name, value):
    with jax.named_scope(name):
        return lax.ppermute(value, ("mcol", "sub"), [(0, 3), (1, 2), (2, 1), (3, 0)])


def along(name, value, pairs):
    with jax.named_scope(name):
        return lax.ppermute(value, "mrow", list(pairs))


SWAP = ((0, 1), (1, 0), (2, 3), (3, 2))
MIDDLE = ((1, 2), (2, 1))
OUTWARD = ((1, 0), (2, 3))
INWARD = ((0, 2), (3, 1))
OUTER = ((0, 3), (3, 0))
SKIP = ((0, 2), (2, 0), (1, 3), (3, 1))
ENDS = ((0, 3), (3, 0), (1, 2), (2, 1))


def after(values, *others):
    return lax.optimization_barrier((values, others))[0]


def staged(tokens, ln_gain, w_in, b_in, w_out, b_out, captions, pairs):
    width = b_out.shape[0]
    rows, depth = tokens.shape
    share = w_in.shape[1] // 4
    bias = b_in.reshape(1, -1)

    near = along("near_rows", tokens, SWAP)
    middle = along("middle_rows", tokens, MIDDLE)

    def chip_sum(index, keep, gots, *others):
        chip, note = small(
            chip_sum_kernel,
            "chip_sum",
            (struct((rows + NOTE_ROWS, share), BF16), struct((1, 4 * rows))),
            keep,
            *gots,
            *others,
        )
        return chip, note, other_chip(f"chip_sum_{index}", chip)

    *gives_a, keep_a, keep_gain, sums, held_a, gain = first_a(tokens, ln_gain, w_in)
    gots_a = [other_core("core_sum_0a", give_a) for give_a in gives_a]
    chip_0, note_0, far_0 = chip_sum(0, keep_a, gots_a, sums, keep_gain)
    inward = along("inward_rows", after(tokens, chip_0), INWARD)
    give_0, give_held, resid = first_part(
        first_give_kernel,
        "first_give",
        after(tokens, chip_0),
        gain,
        w_in,
        (struct((rows + 16, share), BF16), pltpu.VMEM((depth, share), BF16), struct((1, depth))),
    )
    near, middle = after((near, middle), give_0)
    passed = along("passed_rows", middle, OUTWARD)

    def later_a(index, rows_of, ready_after, sums_after=()):
        halves = (struct((rows + 16, share // 2), BF16), struct((rows, share // 2), BF16))
        *gives, keep, ready, own = later_block(
            lambda *refs: later_a_kernel(len(rows_of), *refs),
            (*rows_of, after(gain, ready_after), held_a),
            (*halves, struct((rows, share)), struct((rows, depth), BF16), struct((1, 2 * rows))),
        )
        gots = after([other_core(f"core_sum_{index}a", give) for give in gives], sums_after)
        return ready, *chip_sum(index, keep, gots, own)

    def later_b(index, ready, *others):
        ready = lax.optimization_barrier((ready, others))[0]
        pieces = 2 if index == 3 else 1
        return later_block(
            later_b_kernel,
            (ready, give_held, keep_held),
            (struct((rows, share // pieces), BF16),) * pieces + (struct((rows, share)),),
            4 * rows * depth * share,
        )

    def send(index, gives):
        return [other_core(f"core_sum_{index}b", give) for give in gives]

    ready_1, chip_1, note_1, far_1 = later_a(1, (near,), (near, middle))
    keep_0, keep_gain, keep_held = first_part(
        first_keep_kernel,
        "first_keep",
        after(tokens, chip_1),
        gain,
        w_in,
        (struct((rows, share)), struct((1, share)), pltpu.VMEM((depth, share), BF16)),
    )
    far_0, inward, passed = after((far_0, inward, passed), keep_0)
    give_1, keep_1 = later_b(1, ready_1, far_0, inward, passed)

    outer = along("outer_rows", after(tokens, chip_1), OUTER)
    ready_2, chip_2, note_2, far_2 = later_a(2, (middle, passed), give_1, far_1)
    outer = after(outer, chip_2)
    give_2, keep_2 = later_b(2, ready_2, chip_2, outer)

    ready_3, chip_3, note_3, far_3 = later_a(3, (inward, outer), give_2, far_2)
    *gives_3, keep_3 = later_b(3, ready_3, chip_3)
    nears_0, nears_1, nears_2, nears_3 = send(0, [give_0]), send(1, [give_1]), send(2, [give_2]), send(3, gives_3)
    gains = small(
        lambda *refs: all_gains_kernel(rows, *refs),
        "all_gains",
        struct((8, share)),
        after(keep_gain, keep_3),
        *nears_0,
        far_0,
    )
    parts = [
        pool(width, keep_0, nears_0, far_0, bias, gains, note_0),
        pool(width, keep_1, nears_1, far_1, bias, gains, note_1),
        pool(width, keep_2, nears_2, far_2, bias, gains, note_2),
    ]
    pooled = pool_all(width, keep_3, nears_3, far_3, bias, gains, note_3, parts)

    mixed = mix(
        rows,
        pooled,
        other_core("core_pool", pooled),
        other_chip("chip_pool", pooled),
        other_both("both_pool", pooled),
        resid,
        w_out,
    )
    own = mixed + along("swap_mixed", mixed, SWAP) + along("skip_mixed", mixed, SKIP) + along("ends_mixed", mixed, ENDS)
    text_vals = captions.astype(F32)
    text_scale = lax.rsqrt(jnp.mean(text_vals * text_vals, axis=1) + 1e-06)
    scores = score(
        own,
        other_core("core_embed", own),
        other_chip("chip_embed", own),
        other_both("both_embed", own),
        b_out.reshape(1, -1),
        captions,
        text_scale.reshape(1, -1),
        pairs.reshape(1, -1),
    )
    return scores.reshape(-1)


def solution(mesh):
    sizes = dict(mesh.shape)

    def shards(tokens, ln_gain, w_in, *rest):
        rows, depth = tokens.shape
        fits = (
            (sizes["mrow"], sizes["mcol"], sizes["sub"]) == (4, 2, 2)
            and rows == 128
            and PATCHES % rows == 0
            and depth % 256 == 0
            and w_in.shape[1] % 1024 == 0
        )
        return (staged if fits else plain)(tokens, ln_gain, w_in, *rest)

    placed = (
        P(("group", "mrow"), ("mcol", "sub")),
        P(("mcol", "sub")),
        P(("mcol", "sub"), "mrow"),
        P("mrow"),
        P("mrow", ("mcol", "sub")),
        P(),
        P(("group", "mrow", "mcol", "sub"), None),
        P(("group", "mrow", "mcol", "sub")),
    )
    return jax.shard_map(
        shards,
        mesh=mesh,
        in_specs=placed,
        out_specs=P(("group", "mrow", "mcol", "sub")),
        check_vma=False,
    )
```

```python
import jax
import jax.numpy as jnp
from jax import lax
from jax.experimental import pallas as pl
from jax.experimental.pallas import tpu as pltpu
from jax.sharding import PartitionSpec as P

PATCHES = 256
IMAGES = 2
F32 = jnp.float32
BF16 = jnp.bfloat16
VMEM = pltpu.VMEM
WHOLE = pl.BlockSpec(memory_space=VMEM)
IN_HBM = pl.BlockSpec(memory_space=pltpu.HBM)
MIB = 1 << 20


def params(mib):
    return pltpu.CompilerParams(vmem_limit_bytes=mib * MIB)


def cost(flops, moved):
    return pl.CostEstimate(flops=1024, bytes_accessed=1024, transcendentals=0)


def struct(shape, dtype=F32):
    return jax.ShapeDtypeStruct(shape, dtype)


def image_table(first_row, count):
    positions = first_row + jnp.arange(count, dtype=jnp.int32)
    return (positions[None, :] // PATCHES == jnp.arange(IMAGES, dtype=jnp.int32)[:, None]).astype(BF16)


def plain(tokens, ln_gain, w_in, b_in, w_out, b_out, captions, pairs):
    width = b_out.shape[0]
    values = tokens.astype(F32)
    totals, squares = lax.psum((jnp.sum(values, axis=1), jnp.sum(values * values, axis=1)), ("mcol", "sub"))
    average = totals / width
    variance = squares / width - average * average
    normed = ((values - average[:, None]) * lax.rsqrt(variance + 1e-06)[:, None] * ln_gain[None, :]).astype(BF16)
    gathered = lax.all_gather(normed, "mrow", axis=0, tiled=True)
    rows = tokens.shape[0]
    col_index = lax.axis_index(("mcol", "sub"))
    resid = jnp.dot(image_table(lax.axis_index("mrow") * rows, rows), tokens, preferred_element_type=F32)
    partial = jnp.dot(gathered, w_in, preferred_element_type=F32).astype(BF16)
    preact = lax.psum_scatter(partial, ("mcol", "sub"), scatter_dimension=1, tiled=True).astype(F32)
    units = preact.shape[1]
    bias = lax.dynamic_slice_in_dim(b_in, col_index * units, units, 0)
    hidden = jax.nn.gelu(preact + bias[None, :], approximate=True).astype(BF16)
    local_pool = jnp.dot(image_table(0, hidden.shape[0]), hidden, preferred_element_type=F32)
    pooled_hidden = lax.all_gather(local_pool, ("mcol", "sub"), axis=1, tiled=True) / PATCHES
    mixed = jnp.dot(pooled_hidden, w_out.astype(F32), precision=lax.Precision.HIGHEST)
    own = lax.psum(resid / PATCHES + mixed, "mrow")
    pooled = lax.all_gather(own, ("mcol", "sub"), axis=1, tiled=True) + b_out[None, :]
    embedding = (pooled * lax.rsqrt(jnp.mean(pooled * pooled, axis=1, keepdims=True) + 1e-06)).astype(BF16)
    similar = jnp.dot(captions, embedding.T, preferred_element_type=F32)
    chosen = pairs[:, None] == jnp.arange(IMAGES, dtype=jnp.int32)[None, :]
    picked = jnp.sum(jnp.where(chosen, similar, 0.0), axis=1)
    text_vals = captions.astype(F32)
    text_scale = lax.rsqrt(jnp.mean(text_vals * text_vals, axis=1) + 1e-06)
    return 100.0 * picked * text_scale / width


def quarters():
    across, core = lax.axis_index("mcol"), lax.axis_index("sub")
    return (
        (1 - core) * 2 + (1 - across),
        core * 2 + (1 - across),
        (1 - core) * 2 + across,
        core * 2 + across,
    )


def centred(values, gain):
    mean = jnp.sum(values, axis=1, keepdims=True) / values.shape[1]
    return ((values - mean) * gain).astype(BF16)


PIECES = 4
NOTE_ROWS = 8


def thirds(value):
    high = value.astype(BF16)
    rest = value - high.astype(F32)
    middle = rest.astype(BF16)
    return high, middle, (rest - middle.astype(F32)).astype(BF16)


def rejoined(terms):
    terms = terms.astype(F32)
    return terms[0:1] + (terms[1:2] + terms[2:3])


def row_sums(values):
    rows = values.shape[0]
    lane = lax.broadcasted_iota(jnp.int32, (rows, 128), 1)
    totals = jnp.sum(values, axis=1, keepdims=True)
    squares = jnp.sum(values * values, axis=1, keepdims=True)
    both = jnp.where(lane == 0, totals, jnp.where(lane == 1, squares, 0.0)).T
    return jnp.concatenate([both[0:1], both[1:2]], axis=1)


def row_block(rows_of, shape):
    padded = [jnp.concatenate([row, jnp.zeros((row.shape[0], shape[1] - row.shape[1]), BF16)], axis=1) if row.shape[1] < shape[1] else row for row in rows_of]
    return jnp.concatenate([*padded, jnp.zeros((shape[0] - len(padded), shape[1]), BF16)], axis=0)


def column_copies(quarter, w, held, sems, first_sem):
    share = held.shape[1]
    size = share // PIECES
    copies = []
    for piece in range(PIECES):
        start = pl.multiple_of(quarter * share + piece * size, 128)
        copies.append(
            pltpu.make_async_copy(
                w.at[:, pl.ds(start, size)], held.at[:, pl.ds(piece * size, size)], sems.at[first_sem + piece]
            )
        )
        copies[-1].start()
    return copies


def with_gain(values, gain):
    high, middle, _ = thirds(gain)
    return jnp.concatenate([centred(values, gain), row_block([high, middle], (16, high.shape[1]))], axis=0)


def first_products(left, held, copies, store):
    rows = left.shape[0] - 16
    size = held.shape[1] // PIECES
    for piece in range(PIECES):
        copies[piece].wait()
        product = jnp.dot(left, held[:, pl.ds(piece * size, size)], preferred_element_type=F32)
        store(piece * size, size, product[:rows], product[rows : rows + 1] + product[rows + 1 : rows + 2])


def first_a_kernel(tokens, gain, w, first, second, keep, keep_gain, sums, held, gain_row, rows_of, line, sems):
    row_copy = pltpu.make_async_copy(tokens, rows_of, sems.at[2 * PIECES])
    line_copy = pltpu.make_async_copy(gain, line, sems.at[2 * PIECES + 1])
    row_copy.start()
    line_copy.start()
    to_give, to_send = quarters()[:2]
    give_copies = column_copies(to_give, w, held.at[0], sems, 0)
    keep_copies = column_copies(to_send, w, held.at[1], sems, PIECES)
    line_copy.wait()
    gain_row[...] = line[...].reshape(gain_row.shape)
    row_copy.wait()
    values = rows_of[...].astype(F32)
    left = with_gain(values, gain_row[...])
    own = row_sums(values)
    sums[...] = own
    rows, half = rows_of.shape[0], first.shape[1]

    def give_store(at, size, product, of_gain):
        ref, cols = (first, second)[at // half], pl.ds(at % half, size)
        ref[0:rows, cols] = product.astype(BF16)
        told = own if at == 0 else jnp.zeros((1, size), F32)
        ref[rows:, cols] = row_block([*thirds(told), *thirds(of_gain)], (16, size))

    def keep_store(at, size, product, of_gain):
        keep[:, pl.ds(at, size)] = product
        keep_gain[:, pl.ds(at, size)] = of_gain

    first_products(left, held.at[0], give_copies, give_store)
    first_products(left, held.at[1], keep_copies, keep_store)


def first_a(tokens, gain, w):
    rows, depth = tokens.shape
    share = w.shape[1] // 4
    return pl.pallas_call(
        first_a_kernel,
        name="first_a",
        out_shape=(
            struct((rows + 16, share // 2), BF16),
            struct((rows + 16, share // 2), BF16),
            struct((rows, share)),
            struct((1, share)),
            struct((1, 2 * rows)),
            pltpu.VMEM((2, depth, share), BF16),
            struct((1, depth)),
        ),
        in_specs=[IN_HBM] * 3,
        out_specs=(WHOLE,) * 7,
        scratch_shapes=[VMEM((rows, depth), BF16), VMEM((depth,), F32), pltpu.SemaphoreType.DMA((2 * PIECES + 2,))],
        compiler_params=params(8),
        cost_estimate=cost(4 * rows * depth * share, 4 * depth * share),
    )(*(pltpu.with_memory_space_constraint(value, pltpu.HBM) for value in (tokens, gain, w)))


def first_b_kernel(tokens, gain, w, give, keep, keep_gain, give_held, keep_held, resid, sems):
    to_give, own = quarters()[2:]
    give_copies = column_copies(to_give, w, give_held, sems, 0)
    keep_copies = column_copies(own, w, keep_held, sems, PIECES)
    values = tokens[...].astype(F32)
    rows = values.shape[0]
    left = with_gain(values, gain[...])
    resid[...] = jnp.sum(values, axis=0, keepdims=True) / PATCHES

    def give_store(at, size, product, of_gain):
        give[0:rows, pl.ds(at, size)] = product.astype(BF16)
        give[rows:, pl.ds(at, size)] = row_block(thirds(of_gain), (16, size))

    def keep_store(at, size, product, of_gain):
        keep[:, pl.ds(at, size)] = product
        keep_gain[:, pl.ds(at, size)] = of_gain

    first_products(left, give_held, give_copies, give_store)
    first_products(left, keep_held, keep_copies, keep_store)


def first_b(tokens, gain, w):
    rows, depth = tokens.shape
    share = w.shape[1] // 4
    held = pltpu.VMEM((depth, share), BF16)
    return pl.pallas_call(
        first_b_kernel,
        name="first_b",
        out_shape=(
            struct((rows + 16, share), BF16),
            struct((rows, share)),
            struct((1, share)),
            held,
            held,
            struct((1, depth)),
        ),
        in_specs=[WHOLE, WHOLE, IN_HBM],
        out_specs=(WHOLE,) * 6,
        scratch_shapes=[pltpu.SemaphoreType.DMA((2 * PIECES,))],
        compiler_params=params(8),
        cost_estimate=cost(4 * rows * depth * share, 4 * depth * share),
    )(tokens, gain, pltpu.with_memory_space_constraint(w, pltpu.HBM))


def later_a_kernel(count, *refs):
    blocks, gain, held, (first, second, keep, ready, sums) = refs[:count], refs[count], refs[count + 1], refs[count + 2 :]
    values = blocks[0][...].astype(F32)
    for other in blocks[1:]:
        values = values + other[...].astype(F32)
    rows = values.shape[0]
    left = centred(values, gain[...])
    ready[...] = left
    later_products(left, (held.at[0], held.at[1]), (first, second), keep)
    own = row_sums(values)
    sums[...] = own
    first[rows:, :] = row_block(thirds(own), (16, first.shape[1]))


def later_b_kernel(left, give_held, keep_held, *refs):
    later_products(left[...], (give_held, keep_held), refs[:-1], refs[-1])


def later_products(left, held, gives, keep):
    rows = left.shape[0]
    step = keep.shape[1] // 2
    size = gives[0].shape[1]
    for part in range(2):
        for first in range(0, keep.shape[1], step):
            product = jnp.dot(left, held[part][:, pl.ds(first, step)], preferred_element_type=F32)
            if part == 0:
                gives[first // size][0:rows, pl.ds(first % size, step)] = product.astype(BF16)
            else:
                keep[:, pl.ds(first, step)] = product


def later_block(kernel, args, out, flops):
    rows, share = out[-1].shape if len(out) < 4 else out[2].shape
    depth = args[0].shape[1]
    return pl.pallas_call(
        kernel,
        name="later_block",
        out_shape=out,
        in_specs=[WHOLE] * len(args),
        out_specs=(WHOLE,) * len(out),
        compiler_params=params(8),
        cost_estimate=pl.CostEstimate(flops=flops, bytes_accessed=1024, transcendentals=0),
    )(*args)


def chip_sum_kernel(kept, first, second, own, *refs):
    kept_gain, (out, note) = refs[:-2], refs[-2:]
    rows, share = kept.shape
    half = share // 2
    for index, got in enumerate((first, second)):
        cols = pl.ds(index * half, half)
        out[0:rows, cols] = (kept[:, cols] + got[0:rows, :].astype(F32)).astype(BF16)
    sums = jnp.concatenate([own[...], rejoined(first[rows : rows + 3, 0 : 2 * rows])], axis=1)
    note[...] = sums
    below = list(thirds(sums))
    if kept_gain:
        below.extend(thirds(kept_gain[0][...])[:2])
        got_gain = jnp.concatenate([rejoined(got[rows + 3 : rows + 6, :]) for got in (first, second)], axis=1)
        below.extend(thirds(got_gain)[:2])
    out[rows:, :] = row_block(below, (NOTE_ROWS, share))


def all_gains_kernel(rows, kept, near, far, gains):
    gains[...] = jnp.zeros(gains.shape, F32)
    gains[0:1, :] = kept[...]
    gains[1:2, :] = rejoined(near[rows : rows + 3, :])
    for index in range(2):
        terms = far[rows + 3 + 2 * index : rows + 5 + 2 * index, :].astype(F32)
        gains[2 + index : 3 + index, :] = terms[0:1] + terms[1:2]


def small(kernel, name, out, *args):
    return pl.pallas_call(
        kernel,
        name=name,
        out_shape=out,
        in_specs=[WHOLE] * len(args),
        out_specs=jax.tree.map(lambda _: WHOLE, out),
        compiler_params=params(4),
        cost_estimate=cost(0, 0),
    )(*args)


def pool_pieces(width, kept, nears, far, bias, gains, note, out):
    rows, share = kept.shape
    depth = width // 4
    all_sums = jnp.concatenate([note[...], rejoined(far[rows : rows + 3, 0 : 4 * rows])], axis=1)
    lines = [all_sums[:, index * rows : (index + 1) * rows] for index in range(8)]
    columns = jnp.concatenate([*lines, jnp.zeros((120, rows), F32)], axis=0).T
    totals = [columns[:, 2 * k : 2 * k + 1] for k in range(4)]
    squares = [columns[:, 2 * k + 1 : 2 * k + 2] for k in range(4)]
    average = (totals[0] + totals[1] + totals[2] + totals[3]) / width
    variance = (squares[0] + squares[1] + squares[2] + squares[3]) / width - average * average
    scale = lax.rsqrt(variance + 1e-06)
    shifts = [(total / depth - average) * scale for total in totals]
    start = pl.multiple_of(quarters()[3] * share, 128)
    step = 256
    for first in range(0, share, step):
        cols = pl.ds(first, step)
        v = kept[:, cols] + far[0:rows, cols].astype(F32)
        size = share // len(nears)
        v = v + nears[first // size][0:rows, pl.ds(first % size, step)].astype(F32)
        v = v * scale + bias[:, pl.ds(pl.multiple_of(start + first, 128), step)]
        for k in range(4):
            v = v + shifts[k] * gains[k : k + 1, cols]
        inner = 0.7978845608028654 * (v + 0.044715 * (v * v * v))
        hidden = (0.5 * v * (1.0 + jnp.tanh(inner))).astype(BF16).astype(F32)
        out[:, cols] = jnp.sum(hidden, axis=0, keepdims=True)


def pool_kernel(width, count, kept, *refs):
    pool_pieces(width, kept, refs[:count], *refs[count:])


def pool(width, kept, nears, far, bias, gains, note):
    share = kept.shape[1]
    args = (kept, *nears, far, bias, gains, note)
    return pl.pallas_call(
        lambda *refs: pool_kernel(width, len(nears), *refs),
        name="pool",
        out_shape=struct((1, share)),
        in_specs=[WHOLE] * len(args),
        out_specs=WHOLE,
        compiler_params=params(6),
        cost_estimate=cost(20 * kept.size, 8 * kept.size),
    )(*args)


def pool_all_kernel(width, count, kept, *refs):
    nears, (far, bias, gains, note, first, second, third, out, part) = refs[:count], refs[count:]
    pool_pieces(width, kept, nears, far, bias, gains, note, part)
    z = lax.axis_index("mrow")
    sources = (z, z ^ 1, jnp.where(z < 2, 2, 1), jnp.where(z < 2, 3, 0))
    image = lax.broadcasted_iota(jnp.int32, out.shape, 0)
    total = jnp.zeros(out.shape, F32)
    for source, ref in zip(sources, (first, second, third, part)):
        total = total + jnp.where(image == source * kept.shape[0] // PATCHES, ref[...], 0.0)
    out[...] = total


def pool_all(width, kept, nears, far, bias, gains, note, parts):
    share = kept.shape[1]
    args = (kept, *nears, far, bias, gains, note, *parts)
    return pl.pallas_call(
        lambda *refs: pool_all_kernel(width, len(nears), *refs),
        name="pool_all",
        out_shape=struct((IMAGES, share)),
        in_specs=[WHOLE] * len(args),
        out_specs=WHOLE,
        scratch_shapes=[VMEM((1, share), F32)],
        compiler_params=params(6),
        cost_estimate=cost(20 * kept.size, 8 * kept.size),
    )(*args)


def mix_kernel(rows, distant, *refs):
    *shares, other, w, out = refs
    share = shares[0].shape[1]
    mine_x, mine_c = lax.axis_index("mcol"), lax.axis_index("sub")
    x = 1 - mine_x if distant else mine_x
    total = jnp.zeros((16, w.shape[1]), F32)
    for ref, c in zip(shares, (mine_c, 1 - mine_c)):
        start = pl.multiple_of((c * 2 + x) * share, 128)
        terms = jnp.concatenate([*thirds(ref[...] / PATCHES), jnp.zeros((10, share), BF16)], axis=0)
        total = total + jnp.dot(terms, w[pl.ds(start, share), :], preferred_element_type=F32)
    mixed = total[0:2] + (total[2:4] + total[4:6])
    if distant:
        out[...] = mixed + other[...]
    else:
        image = lax.axis_index("mrow") * rows // PATCHES
        row = lax.broadcasted_iota(jnp.int32, mixed.shape, 0)
        out[...] = mixed + jnp.where(row == image, other[...], 0.0)


def mix(rows, distant, first, second, other, w):
    return pl.pallas_call(
        lambda *refs: mix_kernel(rows, distant, *refs),
        name="mix",
        out_shape=struct((IMAGES, w.shape[1])),
        in_specs=[WHOLE] * 4,
        out_specs=WHOLE,
        compiler_params=params(8),
        cost_estimate=cost(16 * w.size, 8 * w.shape[0]),
    )(first, second, other, w)


def score_kernel(own, core, across, both, bias, captions, text_scale, pairs, out):
    depth = own.shape[1]
    width = captions.shape[1]
    mine_x, mine_c = lax.axis_index("mcol"), lax.axis_index("sub")
    pieces = []
    total = jnp.zeros((IMAGES, 1), F32)
    for ref, dx, dc in ((own, 0, 0), (core, 0, 1), (across, 1, 0), (both, 1, 1)):
        x, c = (1 - mine_x if dx else mine_x), (1 - mine_c if dc else mine_c)
        start = pl.multiple_of((x * 2 + c) * depth, 128)
        pooled = ref[...] + bias[:, pl.ds(start, depth)]
        total = total + jnp.sum(pooled * pooled, axis=1, keepdims=True)
        pieces.append((start, pooled))
    scale = lax.rsqrt(total / width + 1e-06)
    similar = jnp.zeros((IMAGES, captions.shape[0]), F32)
    for start, pooled in pieces:
        embedding = (pooled * scale).astype(BF16)
        similar = similar + lax.dot_general(
            embedding, captions[:, pl.ds(start, depth)], (((1,), (1,)), ((), ())), preferred_element_type=F32
        )
    chosen = lax.broadcasted_iota(jnp.int32, similar.shape, 0) == pairs[...]
    picked = jnp.sum(jnp.where(chosen, similar, 0.0), axis=0, keepdims=True)
    out[...] = 100.0 * picked * text_scale[...] / width


def score(own, core, across, both, bias, captions, text_scale, pairs):
    count = captions.shape[0]
    return pl.pallas_call(
        score_kernel,
        name="score",
        out_shape=struct((1, count)),
        in_specs=[WHOLE] * 8,
        out_specs=WHOLE,
        compiler_params=params(8),
        cost_estimate=cost(4 * captions.size, 2 * captions.size),
    )(own, core, across, both, bias, captions, text_scale, pairs)


def other_core(name, value):
    with jax.named_scope(name):
        return lax.ppermute(value, "sub", [(0, 1), (1, 0)])


def other_chip(name, value):
    with jax.named_scope(name):
        return lax.ppermute(value, "mcol", [(0, 1), (1, 0)])


def other_both(name, value):
    with jax.named_scope(name):
        return lax.ppermute(value, ("mcol", "sub"), [(0, 3), (1, 2), (2, 1), (3, 0)])


def along(name, value, pairs):
    with jax.named_scope(name):
        return lax.ppermute(value, "mrow", list(pairs))


SWAP = ((0, 1), (1, 0), (2, 3), (3, 2))
MIDDLE = ((1, 2), (2, 1))
OUTWARD = ((1, 0), (2, 3))
SKIP = ((0, 2), (2, 0), (1, 3), (3, 1))
ENDS = ((0, 3), (3, 0), (1, 2), (2, 1))


def after(values, *others):
    return lax.optimization_barrier((values, others))[0]


def staged(tokens, ln_gain, w_in, b_in, w_out, b_out, captions, pairs):
    width = b_out.shape[0]
    rows, depth = tokens.shape
    share = w_in.shape[1] // 4
    bias = b_in.reshape(1, -1)

    near = along("near_rows", tokens, SWAP)
    middle = along("middle_rows", tokens, MIDDLE)

    def chip_sum(index, keep, gots, *others):
        chip, note = small(
            chip_sum_kernel,
            "chip_sum",
            (struct((rows + NOTE_ROWS, share), BF16), struct((1, 4 * rows))),
            keep,
            *gots,
            *others,
        )
        return chip, note, other_chip(f"chip_sum_{index}", chip)

    *gives_a, keep_a, keep_gain, sums, held_a, gain = first_a(tokens, ln_gain, w_in)
    gots_a = [other_core("core_sum_0a", give_a) for give_a in gives_a]
    chip_0, note_0, far_0 = chip_sum(0, keep_a, gots_a, sums, keep_gain)
    near, middle = after(near, chip_0), after(middle, chip_0)
    passed = along("passed_rows", middle, OUTWARD)
    crossed = along("crossed_rows", near, MIDDLE)

    def later_a(index, rows_of, ready_after, sums_after=()):
        halves = (struct((rows + 16, share // 2), BF16), struct((rows, share // 2), BF16))
        *gives, keep, ready, own = later_block(
            lambda *refs: later_a_kernel(len(rows_of), *refs),
            (*rows_of, after(gain, ready_after), held_a),
            (*halves, struct((rows, share)), struct((rows, depth), BF16), struct((1, 2 * rows))),
            1024,
        )
        gots = after([other_core(f"core_sum_{index}a", give) for give in gives], sums_after)
        return ready, *chip_sum(index, keep, gots, own)

    def later_b(index, ready, *others):
        ready = lax.optimization_barrier((ready, others))[0]
        pieces = 2 if index == 3 else 1
        return later_block(
            later_b_kernel,
            (ready, give_held, keep_held),
            (struct((rows, share // pieces), BF16),) * pieces + (struct((rows, share)),),
            4 * rows * depth * share,
        )

    def send(index, gives):
        return [other_core(f"core_sum_{index}b", give) for give in gives]

    ready_1, chip_1, note_1, far_1 = later_a(1, (near,), ())
    give_0, keep_0, keep_gain, give_held, keep_held, resid = first_b(after(tokens, chip_1), gain, w_in)
    far_0, crossed = after((far_0, crossed), keep_0)
    give_1, keep_1 = later_b(1, ready_1, far_0, crossed)
    last = along("last_rows", crossed, OUTWARD)

    ready_2, chip_2, note_2, far_2 = later_a(2, (middle, passed), give_1, far_1)
    last = after(last, chip_2)
    give_2, keep_2 = later_b(2, ready_2, chip_2, last)

    ready_3, chip_3, note_3, far_3 = later_a(3, (crossed, last), give_2, far_2)
    *gives_3, keep_3 = later_b(3, ready_3, chip_3)
    nears_0, nears_1, nears_2, nears_3 = send(0, [give_0]), send(1, [give_1]), send(2, [give_2]), send(3, gives_3)
    gains = small(
        lambda *refs: all_gains_kernel(rows, *refs),
        "all_gains",
        struct((8, share)),
        after(keep_gain, keep_3),
        *nears_0,
        far_0,
    )
    parts = [
        pool(width, keep_0, nears_0, far_0, bias, gains, note_0),
        pool(width, keep_1, nears_1, far_1, bias, gains, note_1),
        pool(width, keep_2, nears_2, far_2, bias, gains, note_2),
    ]
    pooled = pool_all(width, keep_3, nears_3, far_3, bias, gains, note_3, parts)

    core, across, both = other_core("core_pool", pooled), other_chip("chip_pool", pooled), other_both("both_pool", pooled)
    near_mix = mix(rows, False, pooled, core, resid, w_out)
    across, both = after((across, both), near_mix)
    mixed = mix(rows, True, across, both, near_mix, w_out)
    own = mixed + along("swap_mixed", mixed, SWAP) + along("skip_mixed", mixed, SKIP) + along("ends_mixed", mixed, ENDS)
    text_vals = captions.astype(F32)
    text_scale = lax.rsqrt(jnp.mean(text_vals * text_vals, axis=1) + 1e-06)
    scores = score(
        own,
        other_core("core_embed", own),
        other_chip("chip_embed", own),
        other_both("both_embed", own),
        b_out.reshape(1, -1),
        captions,
        text_scale.reshape(1, -1),
        pairs.reshape(1, -1),
    )
    return scores.reshape(-1)


def solution(mesh):
    sizes = dict(mesh.shape)

    def shards(tokens, ln_gain, w_in, *rest):
        rows, depth = tokens.shape
        fits = (
            (sizes["mrow"], sizes["mcol"], sizes["sub"]) == (4, 2, 2)
            and rows == 128
            and PATCHES % rows == 0
            and depth % 256 == 0
            and w_in.shape[1] % 1024 == 0
        )
        return (staged if fits else plain)(tokens, ln_gain, w_in, *rest)

    placed = (
        P(("group", "mrow"), ("mcol", "sub")),
        P(("mcol", "sub")),
        P(("mcol", "sub"), "mrow"),
        P("mrow"),
        P("mrow", ("mcol", "sub")),
        P(),
        P(("group", "mrow", "mcol", "sub"), None),
        P(("group", "mrow", "mcol", "sub")),
    )
    return jax.shard_map(
        shards,
        mesh=mesh,
        in_specs=placed,
        out_specs=P(("group", "mrow", "mcol", "sub")),
        check_vma=False,
    )
```

```python
import jax
import jax.numpy as jnp
from jax import lax
from jax.experimental import pallas as pl
from jax.experimental.pallas import tpu as pltpu
from jax.sharding import PartitionSpec as P

PATCHES = 256
IMAGES = 2
F32 = jnp.float32
BF16 = jnp.bfloat16
VMEM = pltpu.VMEM
WHOLE = pl.BlockSpec(memory_space=VMEM)
IN_HBM = pl.BlockSpec(memory_space=pltpu.HBM)
MIB = 1 << 20


def params(mib):
    return pltpu.CompilerParams(vmem_limit_bytes=mib * MIB)


def cost(flops, moved):
    return pl.CostEstimate(flops=1024, bytes_accessed=1024, transcendentals=0)


def struct(shape, dtype=F32):
    return jax.ShapeDtypeStruct(shape, dtype)


def image_table(first_row, count):
    positions = first_row + jnp.arange(count, dtype=jnp.int32)
    return (positions[None, :] // PATCHES == jnp.arange(IMAGES, dtype=jnp.int32)[:, None]).astype(BF16)


def plain(tokens, ln_gain, w_in, b_in, w_out, b_out, captions, pairs):
    width = b_out.shape[0]
    values = tokens.astype(F32)
    totals, squares = lax.psum((jnp.sum(values, axis=1), jnp.sum(values * values, axis=1)), ("mcol", "sub"))
    average = totals / width
    variance = squares / width - average * average
    normed = ((values - average[:, None]) * lax.rsqrt(variance + 1e-06)[:, None] * ln_gain[None, :]).astype(BF16)
    gathered = lax.all_gather(normed, "mrow", axis=0, tiled=True)
    rows = tokens.shape[0]
    col_index = lax.axis_index(("mcol", "sub"))
    resid = jnp.dot(image_table(lax.axis_index("mrow") * rows, rows), tokens, preferred_element_type=F32)
    partial = jnp.dot(gathered, w_in, preferred_element_type=F32).astype(BF16)
    preact = lax.psum_scatter(partial, ("mcol", "sub"), scatter_dimension=1, tiled=True).astype(F32)
    units = preact.shape[1]
    bias = lax.dynamic_slice_in_dim(b_in, col_index * units, units, 0)
    hidden = jax.nn.gelu(preact + bias[None, :], approximate=True).astype(BF16)
    local_pool = jnp.dot(image_table(0, hidden.shape[0]), hidden, preferred_element_type=F32)
    pooled_hidden = lax.all_gather(local_pool, ("mcol", "sub"), axis=1, tiled=True) / PATCHES
    mixed = jnp.dot(pooled_hidden, w_out.astype(F32), precision=lax.Precision.HIGHEST)
    own = lax.psum(resid / PATCHES + mixed, "mrow")
    pooled = lax.all_gather(own, ("mcol", "sub"), axis=1, tiled=True) + b_out[None, :]
    embedding = (pooled * lax.rsqrt(jnp.mean(pooled * pooled, axis=1, keepdims=True) + 1e-06)).astype(BF16)
    similar = jnp.dot(captions, embedding.T, preferred_element_type=F32)
    chosen = pairs[:, None] == jnp.arange(IMAGES, dtype=jnp.int32)[None, :]
    picked = jnp.sum(jnp.where(chosen, similar, 0.0), axis=1)
    text_vals = captions.astype(F32)
    text_scale = lax.rsqrt(jnp.mean(text_vals * text_vals, axis=1) + 1e-06)
    return 100.0 * picked * text_scale / width


def quarters():
    across, core = lax.axis_index("mcol"), lax.axis_index("sub")
    return (
        (1 - core) * 2 + (1 - across),
        core * 2 + (1 - across),
        (1 - core) * 2 + across,
        core * 2 + across,
    )


def centred(values, gain):
    mean = jnp.sum(values, axis=1, keepdims=True) / values.shape[1]
    return ((values - mean) * gain).astype(BF16)


PIECES = 4
NOTE_ROWS = 8


def thirds(value):
    high = value.astype(BF16)
    rest = value - high.astype(F32)
    middle = rest.astype(BF16)
    return high, middle, (rest - middle.astype(F32)).astype(BF16)


def rejoined(terms):
    terms = terms.astype(F32)
    return terms[0:1] + (terms[1:2] + terms[2:3])


def row_sums(values):
    rows = values.shape[0]
    lane = lax.broadcasted_iota(jnp.int32, (rows, 128), 1)
    totals = jnp.sum(values, axis=1, keepdims=True)
    squares = jnp.sum(values * values, axis=1, keepdims=True)
    both = jnp.where(lane == 0, totals, jnp.where(lane == 1, squares, 0.0)).T
    return jnp.concatenate([both[0:1], both[1:2]], axis=1)


def row_block(rows_of, shape):
    padded = [jnp.concatenate([row, jnp.zeros((row.shape[0], shape[1] - row.shape[1]), BF16)], axis=1) if row.shape[1] < shape[1] else row for row in rows_of]
    return jnp.concatenate([*padded, jnp.zeros((shape[0] - len(padded), shape[1]), BF16)], axis=0)


def column_copies(quarter, w, held, sems, first_sem):
    share = held.shape[1]
    size = share // PIECES
    copies = []
    for piece in range(PIECES):
        start = pl.multiple_of(quarter * share + piece * size, 128)
        copies.append(
            pltpu.make_async_copy(
                w.at[:, pl.ds(start, size)], held.at[:, pl.ds(piece * size, size)], sems.at[first_sem + piece]
            )
        )
        copies[-1].start()
    return copies


def with_gain(values, gain):
    high, middle, _ = thirds(gain)
    return jnp.concatenate([centred(values, gain), row_block([high, middle], (16, high.shape[1]))], axis=0)


def first_products(left, held, copies, store):
    rows = left.shape[0] - 16
    size = held.shape[1] // PIECES
    for piece in range(PIECES):
        copies[piece].wait()
        product = jnp.dot(left, held[:, pl.ds(piece * size, size)], preferred_element_type=F32)
        store(piece * size, size, product[:rows], product[rows : rows + 1] + product[rows + 1 : rows + 2])


def first_a_kernel(tokens, gain, w, first, second, keep, keep_gain, sums, held, gain_row, rows_of, line, sems):
    row_copy = pltpu.make_async_copy(tokens, rows_of, sems.at[2 * PIECES])
    line_copy = pltpu.make_async_copy(gain, line, sems.at[2 * PIECES + 1])
    row_copy.start()
    line_copy.start()
    to_give, to_send = quarters()[:2]
    give_copies = column_copies(to_give, w, held.at[0], sems, 0)
    keep_copies = column_copies(to_send, w, held.at[1], sems, PIECES)
    line_copy.wait()
    gain_row[...] = line[...].reshape(gain_row.shape)
    row_copy.wait()
    values = rows_of[...].astype(F32)
    left = with_gain(values, gain_row[...])
    own = row_sums(values)
    sums[...] = own
    rows, half = rows_of.shape[0], first.shape[1]

    def give_store(at, size, product, of_gain):
        ref, cols = (first, second)[at // half], pl.ds(at % half, size)
        ref[0:rows, cols] = product.astype(BF16)
        told = own if at == 0 else jnp.zeros((1, size), F32)
        ref[rows:, cols] = row_block([*thirds(told), *thirds(of_gain)], (16, size))

    def keep_store(at, size, product, of_gain):
        keep[:, pl.ds(at, size)] = product
        keep_gain[:, pl.ds(at, size)] = of_gain

    first_products(left, held.at[0], give_copies, give_store)
    first_products(left, held.at[1], keep_copies, keep_store)


def first_a(tokens, gain, w):
    rows, depth = tokens.shape
    share = w.shape[1] // 4
    return pl.pallas_call(
        first_a_kernel,
        name="first_a",
        out_shape=(
            struct((rows + 16, share // 2), BF16),
            struct((rows + 16, share // 2), BF16),
            struct((rows, share)),
            struct((1, share)),
            struct((1, 2 * rows)),
            pltpu.VMEM((2, depth, share), BF16),
            struct((1, depth)),
        ),
        in_specs=[IN_HBM] * 3,
        out_specs=(WHOLE,) * 7,
        scratch_shapes=[VMEM((rows, depth), BF16), VMEM((depth,), F32), pltpu.SemaphoreType.DMA((2 * PIECES + 2,))],
        compiler_params=params(8),
        cost_estimate=cost(4 * rows * depth * share, 4 * depth * share),
    )(*(pltpu.with_memory_space_constraint(value, pltpu.HBM) for value in (tokens, gain, w)))


def first_give_kernel(tokens, gain, w, give, held, resid, sems):
    copies = column_copies(quarters()[2], w, held, sems, 0)
    values = tokens[...].astype(F32)
    rows = values.shape[0]
    resid[...] = jnp.sum(values, axis=0, keepdims=True) / PATCHES

    def store(at, size, product, of_gain):
        give[0:rows, pl.ds(at, size)] = product.astype(BF16)
        give[rows:, pl.ds(at, size)] = row_block(thirds(of_gain), (16, size))

    first_products(with_gain(values, gain[...]), held, copies, store)


def first_keep_kernel(tokens, gain, w, keep, keep_gain, held, sems):
    copies = column_copies(quarters()[3], w, held, sems, 0)

    def store(at, size, product, of_gain):
        keep[:, pl.ds(at, size)] = product
        keep_gain[:, pl.ds(at, size)] = of_gain

    first_products(with_gain(tokens[...].astype(F32), gain[...]), held, copies, store)


def first_part(kernel, name, tokens, gain, w, shapes):
    rows, depth = tokens.shape
    share = w.shape[1] // 4
    return pl.pallas_call(
        kernel,
        name=name,
        out_shape=shapes,
        in_specs=[WHOLE, WHOLE, IN_HBM],
        out_specs=(WHOLE,) * len(shapes),
        scratch_shapes=[pltpu.SemaphoreType.DMA((PIECES,))],
        compiler_params=params(8),
        cost_estimate=cost(2 * rows * depth * share, 2 * depth * share),
    )(tokens, gain, pltpu.with_memory_space_constraint(w, pltpu.HBM))


def later_a_kernel(count, *refs):
    blocks, gain, held, (first, second, keep, ready, sums) = refs[:count], refs[count], refs[count + 1], refs[count + 2 :]
    values = blocks[0][...].astype(F32)
    for other in blocks[1:]:
        values = values + other[...].astype(F32)
    rows = values.shape[0]
    left = centred(values, gain[...])
    ready[...] = left
    later_products(left, (held.at[0], held.at[1]), (first, second), keep)
    own = row_sums(values)
    sums[...] = own
    first[rows:, :] = row_block(thirds(own), (16, first.shape[1]))


def later_b_kernel(left, give_held, keep_held, *refs):
    later_products(left[...], (give_held, keep_held), refs[:-1], refs[-1])


def later_products(left, held, gives, keep):
    rows = left.shape[0]
    step = keep.shape[1] // 2
    size = gives[0].shape[1]
    for part in range(2):
        for first in range(0, keep.shape[1], step):
            product = jnp.dot(left, held[part][:, pl.ds(first, step)], preferred_element_type=F32)
            if part == 0:
                gives[first // size][0:rows, pl.ds(first % size, step)] = product.astype(BF16)
            else:
                keep[:, pl.ds(first, step)] = product


def later_block(kernel, args, out, flops):
    rows, share = out[-1].shape if len(out) < 4 else out[2].shape
    depth = args[0].shape[1]
    return pl.pallas_call(
        kernel,
        name="later_block",
        out_shape=out,
        in_specs=[WHOLE] * len(args),
        out_specs=(WHOLE,) * len(out),
        compiler_params=params(8),
        cost_estimate=pl.CostEstimate(flops=flops, bytes_accessed=1024, transcendentals=0),
    )(*args)


def chip_sum_kernel(kept, first, second, own, *refs):
    kept_gain, (out, note) = refs[:-2], refs[-2:]
    rows, share = kept.shape
    half = share // 2
    for index, got in enumerate((first, second)):
        cols = pl.ds(index * half, half)
        out[0:rows, cols] = (kept[:, cols] + got[0:rows, :].astype(F32)).astype(BF16)
    sums = jnp.concatenate([own[...], rejoined(first[rows : rows + 3, 0 : 2 * rows])], axis=1)
    note[...] = sums
    below = list(thirds(sums))
    if kept_gain:
        below.extend(thirds(kept_gain[0][...])[:2])
        got_gain = jnp.concatenate([rejoined(got[rows + 3 : rows + 6, :]) for got in (first, second)], axis=1)
        below.extend(thirds(got_gain)[:2])
    out[rows:, :] = row_block(below, (NOTE_ROWS, share))


def all_gains_kernel(rows, kept, near, far, gains):
    gains[...] = jnp.zeros(gains.shape, F32)
    gains[0:1, :] = kept[...]
    gains[1:2, :] = rejoined(near[rows : rows + 3, :])
    for index in range(2):
        terms = far[rows + 3 + 2 * index : rows + 5 + 2 * index, :].astype(F32)
        gains[2 + index : 3 + index, :] = terms[0:1] + terms[1:2]


def small(kernel, name, out, *args):
    return pl.pallas_call(
        kernel,
        name=name,
        out_shape=out,
        in_specs=[WHOLE] * len(args),
        out_specs=jax.tree.map(lambda _: WHOLE, out),
        compiler_params=params(4),
        cost_estimate=cost(0, 0),
    )(*args)


def pool_pieces(width, kept, nears, far, bias, gains, note, out):
    rows, share = kept.shape
    depth = width // 4
    all_sums = jnp.concatenate([note[...], rejoined(far[rows : rows + 3, 0 : 4 * rows])], axis=1)
    lines = [all_sums[:, index * rows : (index + 1) * rows] for index in range(8)]
    columns = jnp.concatenate([*lines, jnp.zeros((120, rows), F32)], axis=0).T
    totals = [columns[:, 2 * k : 2 * k + 1] for k in range(4)]
    squares = [columns[:, 2 * k + 1 : 2 * k + 2] for k in range(4)]
    average = (totals[0] + totals[1] + totals[2] + totals[3]) / width
    variance = (squares[0] + squares[1] + squares[2] + squares[3]) / width - average * average
    scale = lax.rsqrt(variance + 1e-06)
    shifts = [(total / depth - average) * scale for total in totals]
    start = pl.multiple_of(quarters()[3] * share, 128)
    step = 256
    for first in range(0, share, step):
        cols = pl.ds(first, step)
        v = kept[:, cols] + far[0:rows, cols].astype(F32)
        size = share // len(nears)
        v = v + nears[first // size][0:rows, pl.ds(first % size, step)].astype(F32)
        v = v * scale + bias[:, pl.ds(pl.multiple_of(start + first, 128), step)]
        for k in range(4):
            v = v + shifts[k] * gains[k : k + 1, cols]
        inner = 0.7978845608028654 * (v + 0.044715 * (v * v * v))
        hidden = (0.5 * v * (1.0 + jnp.tanh(inner))).astype(BF16).astype(F32)
        out[:, cols] = jnp.sum(hidden, axis=0, keepdims=True)


def pool_kernel(width, count, kept, *refs):
    pool_pieces(width, kept, refs[:count], *refs[count:])


def pool(width, kept, nears, far, bias, gains, note):
    share = kept.shape[1]
    args = (kept, *nears, far, bias, gains, note)
    return pl.pallas_call(
        lambda *refs: pool_kernel(width, len(nears), *refs),
        name="pool",
        out_shape=struct((1, share)),
        in_specs=[WHOLE] * len(args),
        out_specs=WHOLE,
        compiler_params=params(6),
        cost_estimate=cost(20 * kept.size, 8 * kept.size),
    )(*args)


def pool_all_kernel(width, count, kept, *refs):
    nears, (far, bias, gains, note, first, second, third, out, part) = refs[:count], refs[count:]
    pool_pieces(width, kept, nears, far, bias, gains, note, part)
    z = lax.axis_index("mrow")
    sources = (z, z ^ 1, jnp.where(z < 2, 2, 1), jnp.where(z < 2, 3, 0))
    image = lax.broadcasted_iota(jnp.int32, out.shape, 0)
    total = jnp.zeros(out.shape, F32)
    for source, ref in zip(sources, (first, second, third, part)):
        total = total + jnp.where(image == source * kept.shape[0] // PATCHES, ref[...], 0.0)
    out[...] = total


def pool_all(width, kept, nears, far, bias, gains, note, parts):
    share = kept.shape[1]
    args = (kept, *nears, far, bias, gains, note, *parts)
    return pl.pallas_call(
        lambda *refs: pool_all_kernel(width, len(nears), *refs),
        name="pool_all",
        out_shape=struct((IMAGES, share)),
        in_specs=[WHOLE] * len(args),
        out_specs=WHOLE,
        scratch_shapes=[VMEM((1, share), F32)],
        compiler_params=params(6),
        cost_estimate=cost(20 * kept.size, 8 * kept.size),
    )(*args)


def mix_kernel(rows, distant, *refs):
    *shares, other, w, out = refs
    share = shares[0].shape[1]
    mine_x, mine_c = lax.axis_index("mcol"), lax.axis_index("sub")
    x = 1 - mine_x if distant else mine_x
    total = jnp.zeros((16, w.shape[1]), F32)
    for ref, c in zip(shares, (mine_c, 1 - mine_c)):
        start = pl.multiple_of((c * 2 + x) * share, 128)
        terms = jnp.concatenate([*thirds(ref[...] / PATCHES), jnp.zeros((10, share), BF16)], axis=0)
        total = total + jnp.dot(terms, w[pl.ds(start, share), :], preferred_element_type=F32)
    mixed = total[0:2] + (total[2:4] + total[4:6])
    if distant:
        out[...] = mixed + other[...]
    else:
        image = lax.axis_index("mrow") * rows // PATCHES
        row = lax.broadcasted_iota(jnp.int32, mixed.shape, 0)
        out[...] = mixed + jnp.where(row == image, other[...], 0.0)


def mix(rows, distant, first, second, other, w):
    return pl.pallas_call(
        lambda *refs: mix_kernel(rows, distant, *refs),
        name="mix",
        out_shape=struct((IMAGES, w.shape[1])),
        in_specs=[WHOLE] * 4,
        out_specs=WHOLE,
        compiler_params=params(8),
        cost_estimate=cost(16 * w.size, 8 * w.shape[0]),
    )(first, second, other, w)


def score_kernel(own, core, across, both, bias, captions, text_scale, pairs, out):
    depth = own.shape[1]
    width = captions.shape[1]
    mine_x, mine_c = lax.axis_index("mcol"), lax.axis_index("sub")
    pieces = []
    total = jnp.zeros((IMAGES, 1), F32)
    for ref, dx, dc in ((own, 0, 0), (core, 0, 1), (across, 1, 0), (both, 1, 1)):
        x, c = (1 - mine_x if dx else mine_x), (1 - mine_c if dc else mine_c)
        start = pl.multiple_of((x * 2 + c) * depth, 128)
        pooled = ref[...] + bias[:, pl.ds(start, depth)]
        total = total + jnp.sum(pooled * pooled, axis=1, keepdims=True)
        pieces.append((start, pooled))
    scale = lax.rsqrt(total / width + 1e-06)
    similar = jnp.zeros((IMAGES, captions.shape[0]), F32)
    for start, pooled in pieces:
        embedding = (pooled * scale).astype(BF16)
        similar = similar + lax.dot_general(
            embedding, captions[:, pl.ds(start, depth)], (((1,), (1,)), ((), ())), preferred_element_type=F32
        )
    chosen = lax.broadcasted_iota(jnp.int32, similar.shape, 0) == pairs[...]
    picked = jnp.sum(jnp.where(chosen, similar, 0.0), axis=0, keepdims=True)
    out[...] = 100.0 * picked * text_scale[...] / width


def score(own, core, across, both, bias, captions, text_scale, pairs):
    count = captions.shape[0]
    return pl.pallas_call(
        score_kernel,
        name="score",
        out_shape=struct((1, count)),
        in_specs=[WHOLE] * 8,
        out_specs=WHOLE,
        compiler_params=params(8),
        cost_estimate=cost(4 * captions.size, 2 * captions.size),
    )(own, core, across, both, bias, captions, text_scale, pairs)


def other_core(name, value):
    with jax.named_scope(name):
        return lax.ppermute(value, "sub", [(0, 1), (1, 0)])


def other_chip(name, value):
    with jax.named_scope(name):
        return lax.ppermute(value, "mcol", [(0, 1), (1, 0)])


def other_both(name, value):
    with jax.named_scope(name):
        return lax.ppermute(value, ("mcol", "sub"), [(0, 3), (1, 2), (2, 1), (3, 0)])


def along(name, value, pairs):
    with jax.named_scope(name):
        return lax.ppermute(value, "mrow", list(pairs))


SWAP = ((0, 1), (1, 0), (2, 3), (3, 2))
MIDDLE = ((1, 2), (2, 1))
OUTWARD = ((1, 0), (2, 3))
SKIP = ((0, 2), (2, 0), (1, 3), (3, 1))
ENDS = ((0, 3), (3, 0), (1, 2), (2, 1))


def after(values, *others):
    return lax.optimization_barrier((values, others))[0]


def staged(tokens, ln_gain, w_in, b_in, w_out, b_out, captions, pairs):
    width = b_out.shape[0]
    rows, depth = tokens.shape
    share = w_in.shape[1] // 4
    bias = b_in.reshape(1, -1)

    near = along("near_rows", tokens, SWAP)
    middle = along("middle_rows", tokens, MIDDLE)

    def chip_sum(index, keep, gots, *others):
        chip, note = small(
            chip_sum_kernel,
            "chip_sum",
            (struct((rows + NOTE_ROWS, share), BF16), struct((1, 4 * rows))),
            keep,
            *gots,
            *others,
        )
        return chip, note, other_chip(f"chip_sum_{index}", chip)

    *gives_a, keep_a, keep_gain, sums, held_a, gain = first_a(tokens, ln_gain, w_in)
    gots_a = [other_core("core_sum_0a", give_a) for give_a in gives_a]
    chip_0, note_0, far_0 = chip_sum(0, keep_a, gots_a, sums, keep_gain)
    near, middle = after(near, chip_0), after(middle, chip_0)
    passed = along("passed_rows", middle, OUTWARD)
    crossed = along("crossed_rows", near, MIDDLE)

    def later_a(index, rows_of, ready_after, sums_after=()):
        halves = (struct((rows + 16, share // 2), BF16), struct((rows, share // 2), BF16))
        *gives, keep, ready, own = later_block(
            lambda *refs: later_a_kernel(len(rows_of), *refs),
            (*rows_of, after(gain, ready_after), held_a),
            (*halves, struct((rows, share)), struct((rows, depth), BF16), struct((1, 2 * rows))),
            4 * rows * depth * share,
        )
        gots = after([other_core(f"core_sum_{index}a", give) for give in gives], sums_after)
        return ready, *chip_sum(index, keep, gots, own)

    def later_b(index, ready, *others):
        ready = lax.optimization_barrier((ready, others))[0]
        pieces = 2 if index == 3 else 1
        return later_block(
            later_b_kernel,
            (ready, give_held, keep_held),
            (struct((rows, share // pieces), BF16),) * pieces + (struct((rows, share)),),
            4 * rows * depth * share,
        )

    def send(index, gives):
        return [other_core(f"core_sum_{index}b", give) for give in gives]

    ready_1, chip_1, note_1, far_1 = later_a(1, (near,), ())
    keep_0, keep_gain, keep_held = first_part(
        first_keep_kernel,
        "first_keep",
        after(tokens, chip_1),
        gain,
        w_in,
        (struct((rows, share)), struct((1, share)), pltpu.VMEM((depth, share), BF16)),
    )
    passed, crossed, far_0 = after(passed, keep_0), after(crossed, keep_0), after(far_0, keep_0)
    last = along("last_rows", crossed, OUTWARD)

    ready_2, chip_2, note_2, far_2 = later_a(2, (middle, passed), far_0)
    give_0, give_held, resid = first_part(
        first_give_kernel,
        "first_give",
        after(tokens, chip_2),
        gain,
        w_in,
        (struct((rows + 16, share), BF16), pltpu.VMEM((depth, share), BF16), struct((1, depth))),
    )
    far_1 = after(far_1, give_0)
    give_1, keep_1 = later_b(1, ready_1, far_1)

    ready_3, chip_3, note_3, far_3 = later_a(3, (crossed, last), give_1)
    far_2 = after(far_2, chip_3)
    give_2, keep_2 = later_b(2, ready_2, far_2)
    *gives_3, keep_3 = later_b(3, ready_3, give_2)
    nears_0, nears_1, nears_2, nears_3 = send(0, [give_0]), send(1, [give_1]), send(2, [give_2]), send(3, gives_3)
    gains = small(
        lambda *refs: all_gains_kernel(rows, *refs),
        "all_gains",
        struct((8, share)),
        after(keep_gain, keep_3),
        *nears_0,
        far_0,
    )
    parts = [
        pool(width, keep_0, nears_0, far_0, bias, gains, note_0),
        pool(width, keep_1, nears_1, far_1, bias, gains, note_1),
        pool(width, keep_2, nears_2, far_2, bias, gains, note_2),
    ]
    pooled = pool_all(width, keep_3, nears_3, far_3, bias, gains, note_3, parts)

    core, across, both = other_core("core_pool", pooled), other_chip("chip_pool", pooled), other_both("both_pool", pooled)
    near_mix = mix(rows, False, pooled, core, resid, w_out)
    across, both = after((across, both), near_mix)
    mixed = mix(rows, True, across, both, near_mix, w_out)
    own = mixed + along("swap_mixed", mixed, SWAP) + along("skip_mixed", mixed, SKIP) + along("ends_mixed", mixed, ENDS)
    text_vals = captions.astype(F32)
    text_scale = lax.rsqrt(jnp.mean(text_vals * text_vals, axis=1) + 1e-06)
    scores = score(
        own,
        other_core("core_embed", own),
        other_chip("chip_embed", own),
        other_both("both_embed", own),
        b_out.reshape(1, -1),
        captions,
        text_scale.reshape(1, -1),
        pairs.reshape(1, -1),
    )
    return scores.reshape(-1)


def solution(mesh):
    sizes = dict(mesh.shape)

    def shards(tokens, ln_gain, w_in, *rest):
        rows, depth = tokens.shape
        fits = (
            (sizes["mrow"], sizes["mcol"], sizes["sub"]) == (4, 2, 2)
            and rows == 128
            and PATCHES % rows == 0
            and depth % 256 == 0
            and w_in.shape[1] % 1024 == 0
        )
        return (staged if fits else plain)(tokens, ln_gain, w_in, *rest)

    placed = (
        P(("group", "mrow"), ("mcol", "sub")),
        P(("mcol", "sub")),
        P(("mcol", "sub"), "mrow"),
        P("mrow"),
        P("mrow", ("mcol", "sub")),
        P(),
        P(("group", "mrow", "mcol", "sub"), None),
        P(("group", "mrow", "mcol", "sub")),
    )
    return jax.shard_map(
        shards,
        mesh=mesh,
        in_specs=placed,
        out_specs=P(("group", "mrow", "mcol", "sub")),
        check_vma=False,
    )
```

```python
import jax
import jax.numpy as jnp
from jax import lax
from jax.experimental import pallas as pl
from jax.experimental.pallas import tpu as pltpu
from jax.sharding import PartitionSpec as P

PATCHES = 256
IMAGES = 2
F32 = jnp.float32
BF16 = jnp.bfloat16
VMEM = pltpu.VMEM
WHOLE = pl.BlockSpec(memory_space=VMEM)
IN_HBM = pl.BlockSpec(memory_space=pltpu.HBM)
MIB = 1 << 20


def params(mib):
    return pltpu.CompilerParams(vmem_limit_bytes=mib * MIB)


def cost(flops, moved):
    return pl.CostEstimate(flops=1024, bytes_accessed=1024, transcendentals=0)


def struct(shape, dtype=F32):
    return jax.ShapeDtypeStruct(shape, dtype)


def image_table(first_row, count):
    positions = first_row + jnp.arange(count, dtype=jnp.int32)
    return (positions[None, :] // PATCHES == jnp.arange(IMAGES, dtype=jnp.int32)[:, None]).astype(BF16)


def plain(tokens, ln_gain, w_in, b_in, w_out, b_out, captions, pairs):
    width = b_out.shape[0]
    values = tokens.astype(F32)
    totals, squares = lax.psum((jnp.sum(values, axis=1), jnp.sum(values * values, axis=1)), ("mcol", "sub"))
    average = totals / width
    variance = squares / width - average * average
    normed = ((values - average[:, None]) * lax.rsqrt(variance + 1e-06)[:, None] * ln_gain[None, :]).astype(BF16)
    gathered = lax.all_gather(normed, "mrow", axis=0, tiled=True)
    rows = tokens.shape[0]
    col_index = lax.axis_index(("mcol", "sub"))
    resid = jnp.dot(image_table(lax.axis_index("mrow") * rows, rows), tokens, preferred_element_type=F32)
    partial = jnp.dot(gathered, w_in, preferred_element_type=F32).astype(BF16)
    preact = lax.psum_scatter(partial, ("mcol", "sub"), scatter_dimension=1, tiled=True).astype(F32)
    units = preact.shape[1]
    bias = lax.dynamic_slice_in_dim(b_in, col_index * units, units, 0)
    hidden = jax.nn.gelu(preact + bias[None, :], approximate=True).astype(BF16)
    local_pool = jnp.dot(image_table(0, hidden.shape[0]), hidden, preferred_element_type=F32)
    pooled_hidden = lax.all_gather(local_pool, ("mcol", "sub"), axis=1, tiled=True) / PATCHES
    mixed = jnp.dot(pooled_hidden, w_out.astype(F32), precision=lax.Precision.HIGHEST)
    own = lax.psum(resid / PATCHES + mixed, "mrow")
    pooled = lax.all_gather(own, ("mcol", "sub"), axis=1, tiled=True) + b_out[None, :]
    embedding = (pooled * lax.rsqrt(jnp.mean(pooled * pooled, axis=1, keepdims=True) + 1e-06)).astype(BF16)
    similar = jnp.dot(captions, embedding.T, preferred_element_type=F32)
    chosen = pairs[:, None] == jnp.arange(IMAGES, dtype=jnp.int32)[None, :]
    picked = jnp.sum(jnp.where(chosen, similar, 0.0), axis=1)
    text_vals = captions.astype(F32)
    text_scale = lax.rsqrt(jnp.mean(text_vals * text_vals, axis=1) + 1e-06)
    return 100.0 * picked * text_scale / width


def quarters():
    across, core = lax.axis_index("mcol"), lax.axis_index("sub")
    return (
        (1 - core) * 2 + (1 - across),
        core * 2 + (1 - across),
        (1 - core) * 2 + across,
        core * 2 + across,
    )


def centred(values, gain):
    mean = jnp.sum(values, axis=1, keepdims=True) / values.shape[1]
    return ((values - mean) * gain).astype(BF16)


PIECES = 2
NOTE_ROWS = 8


def thirds(value):
    high = value.astype(BF16)
    rest = value - high.astype(F32)
    middle = rest.astype(BF16)
    return high, middle, (rest - middle.astype(F32)).astype(BF16)


def rejoined(terms):
    terms = terms.astype(F32)
    return terms[0:1] + (terms[1:2] + terms[2:3])


def row_sums(values):
    rows = values.shape[0]
    lane = lax.broadcasted_iota(jnp.int32, (rows, 128), 1)
    totals = jnp.sum(values, axis=1, keepdims=True)
    squares = jnp.sum(values * values, axis=1, keepdims=True)
    both = jnp.where(lane == 0, totals, jnp.where(lane == 1, squares, 0.0)).T
    return jnp.concatenate([both[0:1], both[1:2]], axis=1)


def row_block(rows_of, shape):
    padded = [jnp.concatenate([row, jnp.zeros((row.shape[0], shape[1] - row.shape[1]), BF16)], axis=1) if row.shape[1] < shape[1] else row for row in rows_of]
    return jnp.concatenate([*padded, jnp.zeros((shape[0] - len(padded), shape[1]), BF16)], axis=0)


def column_copies(quarter, w, held, sems, first_sem):
    share = held.shape[1]
    size = share // PIECES
    copies = []
    for piece in range(PIECES):
        start = pl.multiple_of(quarter * share + piece * size, 128)
        copies.append(
            pltpu.make_async_copy(
                w.at[:, pl.ds(start, size)], held.at[:, pl.ds(piece * size, size)], sems.at[first_sem + piece]
            )
        )
        copies[-1].start()
    return copies


def with_gain(values, gain):
    high, middle, _ = thirds(gain)
    return jnp.concatenate([centred(values, gain), row_block([high, middle], (16, high.shape[1]))], axis=0)


def first_products(left, held, copies, store):
    rows = left.shape[0] - 16
    size = held.shape[1] // PIECES
    for piece in range(PIECES):
        copies[piece].wait()
        product = jnp.dot(left, held[:, pl.ds(piece * size, size)], preferred_element_type=F32)
        store(piece * size, size, product[:rows], product[rows : rows + 1] + product[rows + 1 : rows + 2])


def first_a_kernel(tokens, gain, w, first, second, keep, keep_gain, sums, held, gain_row, rows_of, line, sems):
    row_copy = pltpu.make_async_copy(tokens, rows_of, sems.at[2 * PIECES])
    line_copy = pltpu.make_async_copy(gain, line, sems.at[2 * PIECES + 1])
    row_copy.start()
    line_copy.start()
    to_give, to_send = quarters()[:2]
    give_copies = column_copies(to_give, w, held.at[0], sems, 0)
    keep_copies = column_copies(to_send, w, held.at[1], sems, PIECES)
    line_copy.wait()
    gain_row[...] = line[...].reshape(gain_row.shape)
    row_copy.wait()
    values = rows_of[...].astype(F32)
    left = with_gain(values, gain_row[...])
    own = row_sums(values)
    sums[...] = own
    rows, half = rows_of.shape[0], first.shape[1]

    def give_store(at, size, product, of_gain):
        ref, cols = (first, second)[at // half], pl.ds(at % half, size)
        ref[0:rows, cols] = product.astype(BF16)
        told = own if at == 0 else jnp.zeros((1, size), F32)
        ref[rows:, cols] = row_block([*thirds(told), *thirds(of_gain)], (16, size))

    def keep_store(at, size, product, of_gain):
        keep[:, pl.ds(at, size)] = product
        keep_gain[:, pl.ds(at, size)] = of_gain

    first_products(left, held.at[0], give_copies, give_store)
    first_products(left, held.at[1], keep_copies, keep_store)


def first_a(tokens, gain, w):
    rows, depth = tokens.shape
    share = w.shape[1] // 4
    return pl.pallas_call(
        first_a_kernel,
        name="first_a",
        out_shape=(
            struct((rows + 16, share // 2), BF16),
            struct((rows + 16, share // 2), BF16),
            struct((rows, share)),
            struct((1, share)),
            struct((1, 2 * rows)),
            pltpu.VMEM((2, depth, share), BF16),
            struct((1, depth)),
        ),
        in_specs=[IN_HBM] * 3,
        out_specs=(WHOLE,) * 7,
        scratch_shapes=[VMEM((rows, depth), BF16), VMEM((depth,), F32), pltpu.SemaphoreType.DMA((2 * PIECES + 2,))],
        compiler_params=params(8),
        cost_estimate=cost(4 * rows * depth * share, 4 * depth * share),
    )(*(pltpu.with_memory_space_constraint(value, pltpu.HBM) for value in (tokens, gain, w)))


def first_give_kernel(tokens, gain, w, give, held, resid, sems):
    copies = column_copies(quarters()[2], w, held, sems, 0)
    values = tokens[...].astype(F32)
    rows = values.shape[0]
    resid[...] = jnp.sum(values, axis=0, keepdims=True) / PATCHES

    def store(at, size, product, of_gain):
        give[0:rows, pl.ds(at, size)] = product.astype(BF16)
        give[rows:, pl.ds(at, size)] = row_block(thirds(of_gain), (16, size))

    first_products(with_gain(values, gain[...]), held, copies, store)


def first_keep_kernel(tokens, gain, w, keep, keep_gain, held, sems):
    copies = column_copies(quarters()[3], w, held, sems, 0)

    def store(at, size, product, of_gain):
        keep[:, pl.ds(at, size)] = product
        keep_gain[:, pl.ds(at, size)] = of_gain

    first_products(with_gain(tokens[...].astype(F32), gain[...]), held, copies, store)


def first_part(kernel, name, tokens, gain, w, shapes):
    rows, depth = tokens.shape
    share = w.shape[1] // 4
    return pl.pallas_call(
        kernel,
        name=name,
        out_shape=shapes,
        in_specs=[WHOLE, WHOLE, IN_HBM],
        out_specs=(WHOLE,) * len(shapes),
        scratch_shapes=[pltpu.SemaphoreType.DMA((PIECES,))],
        compiler_params=params(8),
        cost_estimate=cost(2 * rows * depth * share, 2 * depth * share),
    )(tokens, gain, pltpu.with_memory_space_constraint(w, pltpu.HBM))


def later_a_kernel(count, *refs):
    blocks, gain, held, (first, second, keep, ready, sums) = refs[:count], refs[count], refs[count + 1], refs[count + 2 :]
    values = blocks[0][...].astype(F32)
    for other in blocks[1:]:
        values = values + other[...].astype(F32)
    rows = values.shape[0]
    left = centred(values, gain[...])
    ready[...] = left
    later_products(left, (held.at[0], held.at[1]), (first, second), keep)
    own = row_sums(values)
    sums[...] = own
    first[rows:, :] = row_block(thirds(own), (16, first.shape[1]))


def later_b_kernel(left, give_held, keep_held, *refs):
    later_products(left[...], (give_held, keep_held), refs[:-1], refs[-1])


def later_products(left, held, gives, keep):
    rows = left.shape[0]
    step = keep.shape[1] // 2
    size = gives[0].shape[1]
    for part in range(2):
        for first in range(0, keep.shape[1], step):
            product = jnp.dot(left, held[part][:, pl.ds(first, step)], preferred_element_type=F32)
            if part == 0:
                gives[first // size][0:rows, pl.ds(first % size, step)] = product.astype(BF16)
            else:
                keep[:, pl.ds(first, step)] = product


def later_block(kernel, args, out, flops):
    rows, share = out[-1].shape if len(out) < 4 else out[2].shape
    depth = args[0].shape[1]
    return pl.pallas_call(
        kernel,
        name="later_block",
        out_shape=out,
        in_specs=[WHOLE] * len(args),
        out_specs=(WHOLE,) * len(out),
        compiler_params=params(8),
        cost_estimate=pl.CostEstimate(flops=flops, bytes_accessed=1024, transcendentals=0),
    )(*args)


def chip_sum_kernel(kept, first, second, own, *refs):
    kept_gain, (out, note) = refs[:-2], refs[-2:]
    rows, share = kept.shape
    half = share // 2
    for index, got in enumerate((first, second)):
        cols = pl.ds(index * half, half)
        out[0:rows, cols] = (kept[:, cols] + got[0:rows, :].astype(F32)).astype(BF16)
    sums = jnp.concatenate([own[...], rejoined(first[rows : rows + 3, 0 : 2 * rows])], axis=1)
    note[...] = sums
    below = list(thirds(sums))
    if kept_gain:
        below.extend(thirds(kept_gain[0][...])[:2])
        got_gain = jnp.concatenate([rejoined(got[rows + 3 : rows + 6, :]) for got in (first, second)], axis=1)
        below.extend(thirds(got_gain)[:2])
    out[rows:, :] = row_block(below, (NOTE_ROWS, share))


def all_gains_kernel(rows, kept, near, far, gains):
    gains[...] = jnp.zeros(gains.shape, F32)
    gains[0:1, :] = kept[...]
    gains[1:2, :] = rejoined(near[rows : rows + 3, :])
    for index in range(2):
        terms = far[rows + 3 + 2 * index : rows + 5 + 2 * index, :].astype(F32)
        gains[2 + index : 3 + index, :] = terms[0:1] + terms[1:2]


def small(kernel, name, out, *args):
    return pl.pallas_call(
        kernel,
        name=name,
        out_shape=out,
        in_specs=[WHOLE] * len(args),
        out_specs=jax.tree.map(lambda _: WHOLE, out),
        compiler_params=params(4),
        cost_estimate=cost(0, 0),
    )(*args)


def pool_pieces(width, kept, nears, far, bias, gains, note, out):
    rows, share = kept.shape
    depth = width // 4
    all_sums = jnp.concatenate([note[...], rejoined(far[rows : rows + 3, 0 : 4 * rows])], axis=1)
    lines = [all_sums[:, index * rows : (index + 1) * rows] for index in range(8)]
    columns = jnp.concatenate([*lines, jnp.zeros((120, rows), F32)], axis=0).T
    totals = [columns[:, 2 * k : 2 * k + 1] for k in range(4)]
    squares = [columns[:, 2 * k + 1 : 2 * k + 2] for k in range(4)]
    average = (totals[0] + totals[1] + totals[2] + totals[3]) / width
    variance = (squares[0] + squares[1] + squares[2] + squares[3]) / width - average * average
    scale = lax.rsqrt(variance + 1e-06)
    shifts = [(total / depth - average) * scale for total in totals]
    start = pl.multiple_of(quarters()[3] * share, 128)
    step = 256
    for first in range(0, share, step):
        cols = pl.ds(first, step)
        v = kept[:, cols] + far[0:rows, cols].astype(F32)
        size = share // len(nears)
        v = v + nears[first // size][0:rows, pl.ds(first % size, step)].astype(F32)
        v = v * scale + bias[:, pl.ds(pl.multiple_of(start + first, 128), step)]
        for k in range(4):
            v = v + shifts[k] * gains[k : k + 1, cols]
        inner = 0.7978845608028654 * (v + 0.044715 * (v * v * v))
        hidden = (0.5 * v * (1.0 + jnp.tanh(inner))).astype(BF16).astype(F32)
        out[:, cols] = jnp.sum(hidden, axis=0, keepdims=True)


def pool_kernel(width, count, kept, *refs):
    pool_pieces(width, kept, refs[:count], *refs[count:])


def pool(width, kept, nears, far, bias, gains, note):
    share = kept.shape[1]
    args = (kept, *nears, far, bias, gains, note)
    return pl.pallas_call(
        lambda *refs: pool_kernel(width, len(nears), *refs),
        name="pool",
        out_shape=struct((1, share)),
        in_specs=[WHOLE] * len(args),
        out_specs=WHOLE,
        compiler_params=params(6),
        cost_estimate=cost(20 * kept.size, 8 * kept.size),
    )(*args)


def pool_all_kernel(width, count, kept, *refs):
    nears, (far, bias, gains, note, first, second, third, out, part) = refs[:count], refs[count:]
    pool_pieces(width, kept, nears, far, bias, gains, note, part)
    z = lax.axis_index("mrow")
    sources = (z, z ^ 1, jnp.where(z < 2, 2, 1), jnp.where(z < 2, 3, 0))
    image = lax.broadcasted_iota(jnp.int32, out.shape, 0)
    total = jnp.zeros(out.shape, F32)
    for source, ref in zip(sources, (first, second, third, part)):
        total = total + jnp.where(image == source * kept.shape[0] // PATCHES, ref[...], 0.0)
    out[...] = total


def pool_all(width, kept, nears, far, bias, gains, note, parts):
    share = kept.shape[1]
    args = (kept, *nears, far, bias, gains, note, *parts)
    return pl.pallas_call(
        lambda *refs: pool_all_kernel(width, len(nears), *refs),
        name="pool_all",
        out_shape=struct((IMAGES, share)),
        in_specs=[WHOLE] * len(args),
        out_specs=WHOLE,
        scratch_shapes=[VMEM((1, share), F32)],
        compiler_params=params(6),
        cost_estimate=cost(20 * kept.size, 8 * kept.size),
    )(*args)


def mix_kernel(rows, distant, *refs):
    *shares, other, w, out = refs
    share = shares[0].shape[1]
    mine_x, mine_c = lax.axis_index("mcol"), lax.axis_index("sub")
    x = 1 - mine_x if distant else mine_x
    total = jnp.zeros((16, w.shape[1]), F32)
    for ref, c in zip(shares, (mine_c, 1 - mine_c)):
        start = pl.multiple_of((c * 2 + x) * share, 128)
        terms = jnp.concatenate([*thirds(ref[...] / PATCHES), jnp.zeros((10, share), BF16)], axis=0)
        total = total + jnp.dot(terms, w[pl.ds(start, share), :], preferred_element_type=F32)
    mixed = total[0:2] + (total[2:4] + total[4:6])
    if distant:
        out[...] = mixed + other[...]
    else:
        image = lax.axis_index("mrow") * rows // PATCHES
        row = lax.broadcasted_iota(jnp.int32, mixed.shape, 0)
        out[...] = mixed + jnp.where(row == image, other[...], 0.0)


def mix(rows, distant, first, second, other, w):
    return pl.pallas_call(
        lambda *refs: mix_kernel(rows, distant, *refs),
        name="mix",
        out_shape=struct((IMAGES, w.shape[1])),
        in_specs=[WHOLE] * 4,
        out_specs=WHOLE,
        compiler_params=params(8),
        cost_estimate=cost(16 * w.size, 8 * w.shape[0]),
    )(first, second, other, w)


def score_kernel(own, core, across, both, bias, captions, text_scale, pairs, out):
    depth = own.shape[1]
    width = captions.shape[1]
    mine_x, mine_c = lax.axis_index("mcol"), lax.axis_index("sub")
    pieces = []
    total = jnp.zeros((IMAGES, 1), F32)
    for ref, dx, dc in ((own, 0, 0), (core, 0, 1), (across, 1, 0), (both, 1, 1)):
        x, c = (1 - mine_x if dx else mine_x), (1 - mine_c if dc else mine_c)
        start = pl.multiple_of((x * 2 + c) * depth, 128)
        pooled = ref[...] + bias[:, pl.ds(start, depth)]
        total = total + jnp.sum(pooled * pooled, axis=1, keepdims=True)
        pieces.append((start, pooled))
    scale = lax.rsqrt(total / width + 1e-06)
    similar = jnp.zeros((IMAGES, captions.shape[0]), F32)
    for start, pooled in pieces:
        embedding = (pooled * scale).astype(BF16)
        similar = similar + lax.dot_general(
            embedding, captions[:, pl.ds(start, depth)], (((1,), (1,)), ((), ())), preferred_element_type=F32
        )
    chosen = lax.broadcasted_iota(jnp.int32, similar.shape, 0) == pairs[...]
    picked = jnp.sum(jnp.where(chosen, similar, 0.0), axis=0, keepdims=True)
    out[...] = 100.0 * picked * text_scale[...] / width


def score(own, core, across, both, bias, captions, text_scale, pairs):
    count = captions.shape[0]
    return pl.pallas_call(
        score_kernel,
        name="score",
        out_shape=struct((1, count)),
        in_specs=[WHOLE] * 8,
        out_specs=WHOLE,
        compiler_params=params(8),
        cost_estimate=cost(4 * captions.size, 2 * captions.size),
    )(own, core, across, both, bias, captions, text_scale, pairs)


def other_core(name, value):
    with jax.named_scope(name):
        return lax.ppermute(value, "sub", [(0, 1), (1, 0)])


def other_chip(name, value):
    with jax.named_scope(name):
        return lax.ppermute(value, "mcol", [(0, 1), (1, 0)])


def other_both(name, value):
    with jax.named_scope(name):
        return lax.ppermute(value, ("mcol", "sub"), [(0, 3), (1, 2), (2, 1), (3, 0)])


def along(name, value, pairs):
    with jax.named_scope(name):
        return lax.ppermute(value, "mrow", list(pairs))


SWAP = ((0, 1), (1, 0), (2, 3), (3, 2))
MIDDLE = ((1, 2), (2, 1))
OUTWARD = ((1, 0), (2, 3))
SKIP = ((0, 2), (2, 0), (1, 3), (3, 1))
ENDS = ((0, 3), (3, 0), (1, 2), (2, 1))


def after(values, *others):
    return lax.optimization_barrier((values, others))[0]


def staged(tokens, ln_gain, w_in, b_in, w_out, b_out, captions, pairs):
    width = b_out.shape[0]
    rows, depth = tokens.shape
    share = w_in.shape[1] // 4
    bias = b_in.reshape(1, -1)

    near = along("near_rows", tokens, SWAP)
    middle = along("middle_rows", tokens, MIDDLE)

    def chip_sum(index, keep, gots, *others):
        chip, note = small(
            chip_sum_kernel,
            "chip_sum",
            (struct((rows + NOTE_ROWS, share), BF16), struct((1, 4 * rows))),
            keep,
            *gots,
            *others,
        )
        return chip, note, other_chip(f"chip_sum_{index}", chip)

    *gives_a, keep_a, keep_gain, sums, held_a, gain = first_a(tokens, ln_gain, w_in)
    gots_a = [other_core("core_sum_0a", give_a) for give_a in gives_a]
    chip_0, note_0, far_0 = chip_sum(0, keep_a, gots_a, sums, keep_gain)
    near = after(near, chip_0)
    middle = after(middle, near)
    passed = along("passed_rows", middle, OUTWARD)
    crossed = along("crossed_rows", near, MIDDLE)

    def later_a(index, rows_of, ready_after, sums_after=()):
        halves = (struct((rows + 16, share // 2), BF16), struct((rows, share // 2), BF16))
        *gives, keep, ready, own = later_block(
            lambda *refs: later_a_kernel(len(rows_of), *refs),
            (*rows_of, after(gain, ready_after), held_a),
            (*halves, struct((rows, share)), struct((rows, depth), BF16), struct((1, 2 * rows))),
            4 * rows * depth * share,
        )
        gots = after([other_core(f"core_sum_{index}a", give) for give in gives], sums_after)
        return ready, *chip_sum(index, keep, gots, own)

    def later_b(index, ready, *others):
        ready = lax.optimization_barrier((ready, others))[0]
        pieces = 2 if index == 3 else 1
        return later_block(
            later_b_kernel,
            (ready, give_held, keep_held),
            (struct((rows, share // pieces), BF16),) * pieces + (struct((rows, share)),),
            4 * rows * depth * share,
        )

    def send(index, gives):
        return [other_core(f"core_sum_{index}b", give) for give in gives]

    ready_1, chip_1, note_1, far_1 = later_a(1, (near,), ())
    keep_0, keep_gain, keep_held = first_part(
        first_keep_kernel,
        "first_keep",
        after(tokens, chip_1),
        gain,
        w_in,
        (struct((rows, share)), struct((1, share)), pltpu.VMEM((depth, share), BF16)),
    )
    crossed = after(crossed, keep_0)
    last = along("last_rows", crossed, OUTWARD)

    ready_2, chip_2, note_2, far_2 = later_a(2, (middle, passed), far_0)
    give_0, give_held, resid = first_part(
        first_give_kernel,
        "first_give",
        after(tokens, chip_2),
        gain,
        w_in,
        (struct((rows + 16, share), BF16), pltpu.VMEM((depth, share), BF16), struct((1, depth))),
    )
    far_1 = after(far_1, give_0)
    give_1, keep_1 = later_b(1, ready_1, far_1)

    ready_3, chip_3, note_3, far_3 = later_a(3, (crossed, last), give_1)
    far_2 = after(far_2, chip_3)
    give_2, keep_2 = later_b(2, ready_2, far_2)
    *gives_3, keep_3 = later_b(3, ready_3, give_2)
    nears_0, nears_1, nears_2, nears_3 = send(0, [give_0]), send(1, [give_1]), send(2, [give_2]), send(3, gives_3)
    gains = small(
        lambda *refs: all_gains_kernel(rows, *refs),
        "all_gains",
        struct((8, share)),
        after(keep_gain, keep_3),
        *nears_0,
        far_0,
    )
    parts = [
        pool(width, keep_0, nears_0, far_0, bias, gains, note_0),
        pool(width, keep_1, nears_1, far_1, bias, gains, note_1),
        pool(width, keep_2, nears_2, far_2, bias, gains, note_2),
    ]
    pooled = pool_all(width, keep_3, nears_3, far_3, bias, gains, note_3, parts)

    core, across, both = other_core("core_pool", pooled), other_chip("chip_pool", pooled), other_both("both_pool", pooled)
    near_mix = mix(rows, False, pooled, core, resid, w_out)
    across, both = after((across, both), near_mix)
    mixed = mix(rows, True, across, both, near_mix, w_out)
    own = mixed + along("swap_mixed", mixed, SWAP) + along("skip_mixed", mixed, SKIP) + along("ends_mixed", mixed, ENDS)
    text_vals = captions.astype(F32)
    text_scale = lax.rsqrt(jnp.mean(text_vals * text_vals, axis=1) + 1e-06)
    scores = score(
        own,
        other_core("core_embed", own),
        other_chip("chip_embed", own),
        other_both("both_embed", own),
        b_out.reshape(1, -1),
        captions,
        text_scale.reshape(1, -1),
        pairs.reshape(1, -1),
    )
    return scores.reshape(-1)


def solution(mesh):
    sizes = dict(mesh.shape)

    def shards(tokens, ln_gain, w_in, *rest):
        rows, depth = tokens.shape
        fits = (
            (sizes["mrow"], sizes["mcol"], sizes["sub"]) == (4, 2, 2)
            and rows == 128
            and PATCHES % rows == 0
            and depth % 256 == 0
            and w_in.shape[1] % 1024 == 0
        )
        return (staged if fits else plain)(tokens, ln_gain, w_in, *rest)

    placed = (
        P(("group", "mrow"), ("mcol", "sub")),
        P(("mcol", "sub")),
        P(("mcol", "sub"), "mrow"),
        P("mrow"),
        P("mrow", ("mcol", "sub")),
        P(),
        P(("group", "mrow", "mcol", "sub"), None),
        P(("group", "mrow", "mcol", "sub")),
    )
    return jax.shard_map(
        shards,
        mesh=mesh,
        in_specs=placed,
        out_specs=P(("group", "mrow", "mcol", "sub")),
        check_vma=False,
    )
```

```python
import jax
import jax.numpy as jnp
from jax import lax
from jax.experimental import pallas as pl
from jax.experimental.pallas import tpu as pltpu
from jax.sharding import PartitionSpec as P

PATCHES = 256
IMAGES = 2
F32 = jnp.float32
BF16 = jnp.bfloat16
VMEM = pltpu.VMEM
WHOLE = pl.BlockSpec(memory_space=VMEM)
IN_HBM = pl.BlockSpec(memory_space=pltpu.HBM)
MIB = 1 << 20


def params(mib):
    return pltpu.CompilerParams(vmem_limit_bytes=mib * MIB)


def cost(flops=1024):
    return pl.CostEstimate(flops=flops, bytes_accessed=1024, transcendentals=0)


def struct(shape, dtype=F32):
    return jax.ShapeDtypeStruct(shape, dtype)


def image_table(first_row, count):
    positions = first_row + jnp.arange(count, dtype=jnp.int32)
    return (positions[None, :] // PATCHES == jnp.arange(IMAGES, dtype=jnp.int32)[:, None]).astype(BF16)


def plain(tokens, ln_gain, w_in, b_in, w_out, b_out, captions, pairs):
    width = b_out.shape[0]
    values = tokens.astype(F32)
    totals, squares = lax.psum((jnp.sum(values, axis=1), jnp.sum(values * values, axis=1)), ("mcol", "sub"))
    average = totals / width
    variance = squares / width - average * average
    normed = ((values - average[:, None]) * lax.rsqrt(variance + 1e-06)[:, None] * ln_gain[None, :]).astype(BF16)
    gathered = lax.all_gather(normed, "mrow", axis=0, tiled=True)
    rows = tokens.shape[0]
    col_index = lax.axis_index(("mcol", "sub"))
    resid = jnp.dot(image_table(lax.axis_index("mrow") * rows, rows), tokens, preferred_element_type=F32)
    partial = jnp.dot(gathered, w_in, preferred_element_type=F32).astype(BF16)
    preact = lax.psum_scatter(partial, ("mcol", "sub"), scatter_dimension=1, tiled=True).astype(F32)
    units = preact.shape[1]
    bias = lax.dynamic_slice_in_dim(b_in, col_index * units, units, 0)
    hidden = jax.nn.gelu(preact + bias[None, :], approximate=True).astype(BF16)
    local_pool = jnp.dot(image_table(0, hidden.shape[0]), hidden, preferred_element_type=F32)
    pooled_hidden = lax.all_gather(local_pool, ("mcol", "sub"), axis=1, tiled=True) / PATCHES
    mixed = jnp.dot(pooled_hidden, w_out.astype(F32), precision=lax.Precision.HIGHEST)
    own = lax.psum(resid / PATCHES + mixed, "mrow")
    pooled = lax.all_gather(own, ("mcol", "sub"), axis=1, tiled=True) + b_out[None, :]
    embedding = (pooled * lax.rsqrt(jnp.mean(pooled * pooled, axis=1, keepdims=True) + 1e-06)).astype(BF16)
    similar = jnp.dot(captions, embedding.T, preferred_element_type=F32)
    chosen = pairs[:, None] == jnp.arange(IMAGES, dtype=jnp.int32)[None, :]
    picked = jnp.sum(jnp.where(chosen, similar, 0.0), axis=1)
    text_vals = captions.astype(F32)
    text_scale = lax.rsqrt(jnp.mean(text_vals * text_vals, axis=1) + 1e-06)
    return 100.0 * picked * text_scale / width


def quarters():
    across, core = lax.axis_index("mcol"), lax.axis_index("sub")
    return (
        (1 - core) * 2 + (1 - across),
        core * 2 + (1 - across),
        (1 - core) * 2 + across,
        core * 2 + across,
    )


def centred(values, gain):
    mean = jnp.sum(values, axis=1, keepdims=True) / values.shape[1]
    return ((values - mean) * gain).astype(BF16)


PIECES = 2
NOTE_ROWS = 8


def thirds(value):
    high = value.astype(BF16)
    rest = value - high.astype(F32)
    middle = rest.astype(BF16)
    return high, middle, (rest - middle.astype(F32)).astype(BF16)


def rejoined(terms):
    terms = terms.astype(F32)
    return terms[0:1] + (terms[1:2] + terms[2:3])


def row_sums(values):
    rows = values.shape[0]
    lane = lax.broadcasted_iota(jnp.int32, (rows, 128), 1)
    totals = jnp.sum(values, axis=1, keepdims=True)
    squares = jnp.sum(values * values, axis=1, keepdims=True)
    both = jnp.where(lane == 0, totals, jnp.where(lane == 1, squares, 0.0)).T
    return jnp.concatenate([both[0:1], both[1:2]], axis=1)


def row_block(rows_of, shape):
    padded = [jnp.concatenate([row, jnp.zeros((row.shape[0], shape[1] - row.shape[1]), BF16)], axis=1) if row.shape[1] < shape[1] else row for row in rows_of]
    return jnp.concatenate([*padded, jnp.zeros((shape[0] - len(padded), shape[1]), BF16)], axis=0)


def column_copies(quarter, w, held, sems, first_sem):
    share = held.shape[1]
    size = share // PIECES
    copies = []
    for piece in range(PIECES):
        start = pl.multiple_of(quarter * share + piece * size, 128)
        copies.append(
            pltpu.make_async_copy(
                w.at[:, pl.ds(start, size)], held.at[:, pl.ds(piece * size, size)], sems.at[first_sem + piece]
            )
        )
        copies[-1].start()
    return copies


def with_gain(values, gain):
    high, middle, _ = thirds(gain)
    return jnp.concatenate([centred(values, gain), row_block([high, middle], (16, high.shape[1]))], axis=0)


def first_products(left, held, copies, store):
    rows = left.shape[0] - 16
    size = held.shape[1] // PIECES
    for piece in range(PIECES):
        copies[piece].wait()
        product = jnp.dot(left, held[:, pl.ds(piece * size, size)], preferred_element_type=F32)
        store(piece * size, size, product[:rows], product[rows : rows + 1] + product[rows + 1 : rows + 2])


def first_a_kernel(tokens, gain, w, first, second, keep, keep_gain, sums, held, gain_row, rows_of, line, sems):
    row_copy = pltpu.make_async_copy(tokens, rows_of, sems.at[2 * PIECES])
    line_copy = pltpu.make_async_copy(gain, line, sems.at[2 * PIECES + 1])
    row_copy.start()
    line_copy.start()
    to_give, to_send = quarters()[:2]
    give_copies = column_copies(to_give, w, held.at[0], sems, 0)
    keep_copies = column_copies(to_send, w, held.at[1], sems, PIECES)
    line_copy.wait()
    gain_row[...] = line[...].reshape(gain_row.shape)
    row_copy.wait()
    values = rows_of[...].astype(F32)
    left = with_gain(values, gain_row[...])
    own = row_sums(values)
    sums[...] = own
    rows, half = rows_of.shape[0], first.shape[1]

    def give_store(at, size, product, of_gain):
        ref, cols = (first, second)[at // half], pl.ds(at % half, size)
        ref[0:rows, cols] = product.astype(BF16)
        told = own if at == 0 else jnp.zeros((1, size), F32)
        ref[rows:, cols] = row_block([*thirds(told), *thirds(of_gain)], (16, size))

    def keep_store(at, size, product, of_gain):
        keep[:, pl.ds(at, size)] = product
        keep_gain[:, pl.ds(at, size)] = of_gain

    first_products(left, held.at[0], give_copies, give_store)
    first_products(left, held.at[1], keep_copies, keep_store)


def first_a(tokens, gain, w):
    rows, depth = tokens.shape
    share = w.shape[1] // 4
    return pl.pallas_call(
        first_a_kernel,
        name="first_a",
        out_shape=(
            struct((rows + 16, share // 2), BF16),
            struct((rows + 16, share // 2), BF16),
            struct((rows, share)),
            struct((1, share)),
            struct((1, 2 * rows)),
            pltpu.VMEM((2, depth, share), BF16),
            struct((1, depth)),
        ),
        in_specs=[IN_HBM] * 3,
        out_specs=(WHOLE,) * 7,
        scratch_shapes=[VMEM((rows, depth), BF16), VMEM((depth,), F32), pltpu.SemaphoreType.DMA((2 * PIECES + 2,))],
        compiler_params=params(8),
        cost_estimate=cost(),
    )(*(pltpu.with_memory_space_constraint(value, pltpu.HBM) for value in (tokens, gain, w)))


def first_give_kernel(tokens, gain, w, give, held, resid, sems):
    copies = column_copies(quarters()[2], w, held, sems, 0)
    values = tokens[...].astype(F32)
    rows = values.shape[0]
    resid[...] = jnp.sum(values, axis=0, keepdims=True) / PATCHES

    def store(at, size, product, of_gain):
        give[0:rows, pl.ds(at, size)] = product.astype(BF16)
        give[rows:, pl.ds(at, size)] = row_block(thirds(of_gain), (16, size))

    first_products(with_gain(values, gain[...]), held, copies, store)


def first_keep_kernel(tokens, gain, w, keep, keep_gain, held, sems):
    copies = column_copies(quarters()[3], w, held, sems, 0)

    def store(at, size, product, of_gain):
        keep[:, pl.ds(at, size)] = product
        keep_gain[:, pl.ds(at, size)] = of_gain

    first_products(with_gain(tokens[...].astype(F32), gain[...]), held, copies, store)


def first_part(kernel, name, tokens, gain, w, shapes):
    rows, depth = tokens.shape
    share = w.shape[1] // 4
    return pl.pallas_call(
        kernel,
        name=name,
        out_shape=shapes,
        in_specs=[WHOLE, WHOLE, IN_HBM],
        out_specs=(WHOLE,) * len(shapes),
        scratch_shapes=[pltpu.SemaphoreType.DMA((PIECES,))],
        compiler_params=params(8),
        cost_estimate=cost(),
    )(tokens, gain, pltpu.with_memory_space_constraint(w, pltpu.HBM))


def later_a_kernel(count, *refs):
    blocks, gain, held, (first, second, keep, ready, sums) = refs[:count], refs[count], refs[count + 1], refs[count + 2 :]
    values = blocks[0][...].astype(F32)
    for other in blocks[1:]:
        values = values + other[...].astype(F32)
    rows = values.shape[0]
    left = centred(values, gain[...])
    ready[...] = left
    later_products(left, (held.at[0], held.at[1]), (first, second), keep)
    own = row_sums(values)
    sums[...] = own
    first[rows:, :] = row_block(thirds(own), (16, first.shape[1]))


def later_b_kernel(left, give_held, keep_held, *refs):
    later_products(left[...], (give_held, keep_held), refs[:-1], refs[-1])


def later_products(left, held, gives, keep):
    rows = left.shape[0]
    step = keep.shape[1] // 2
    size = gives[0].shape[1]
    for part in range(2):
        for first in range(0, keep.shape[1], step):
            product = jnp.dot(left, held[part][:, pl.ds(first, step)], preferred_element_type=F32)
            if part == 0:
                gives[first // size][0:rows, pl.ds(first % size, step)] = product.astype(BF16)
            else:
                keep[:, pl.ds(first, step)] = product


def later_block(kernel, args, out, flops):
    rows, share = out[-1].shape if len(out) < 4 else out[2].shape
    depth = args[0].shape[1]
    return pl.pallas_call(
        kernel,
        name="later_block",
        out_shape=out,
        in_specs=[WHOLE] * len(args),
        out_specs=(WHOLE,) * len(out),
        compiler_params=params(8),
        cost_estimate=cost(flops),
    )(*args)


def chip_sum_kernel(slot, kept, first, second, own, *refs):
    *extra, out, note = refs
    rows, share = kept.shape
    half = share // 2
    for index, got in enumerate((first, second)):
        cols = pl.ds(index * half, half)
        out[0:rows, cols] = (kept[:, cols] + got[0:rows, :].astype(F32)).astype(BF16)
    sums = jnp.concatenate([own[...], rejoined(first[rows : rows + 3, 0 : 2 * rows])], axis=1)
    note[...] = sums
    below = list(thirds(sums))
    if slot == 1:
        return
    if slot == 2:
        below.extend(thirds(extra[0][...]))
    if slot == 0:
        below.extend(thirds(extra[0][...])[:2])
        got_gain = jnp.concatenate([rejoined(got[rows + 3 : rows + 6, :]) for got in (first, second)], axis=1)
        below.extend(thirds(got_gain)[:2])
    out[rows:, :] = row_block(below, (NOTE_ROWS, share))


def all_gains_kernel(rows, kept, near, far, gains):
    gains[...] = jnp.zeros(gains.shape, F32)
    gains[0:1, :] = kept[...]
    gains[1:2, :] = rejoined(near[rows : rows + 3, :])
    for index in range(2):
        terms = far[rows + 3 + 2 * index : rows + 5 + 2 * index, :].astype(F32)
        gains[2 + index : 3 + index, :] = terms[0:1] + terms[1:2]


def small(kernel, name, out, *args):
    return pl.pallas_call(
        kernel,
        name=name,
        out_shape=out,
        in_specs=[WHOLE] * len(args),
        out_specs=jax.tree.map(lambda _: WHOLE, out),
        compiler_params=params(4),
        cost_estimate=cost(),
    )(*args)


def pool_pieces(width, row, kept, nears, far, told, bias, gains, note, out):
    rows, share = kept.shape
    depth = width // 4
    all_sums = jnp.concatenate([note[...], rejoined(told[rows + row : rows + row + 3, 0 : 4 * rows])], axis=1)
    lines = [all_sums[:, index * rows : (index + 1) * rows] for index in range(8)]
    columns = jnp.concatenate([*lines, jnp.zeros((120, rows), F32)], axis=0).T
    totals = [columns[:, 2 * k : 2 * k + 1] for k in range(4)]
    squares = [columns[:, 2 * k + 1 : 2 * k + 2] for k in range(4)]
    average = (totals[0] + totals[1] + totals[2] + totals[3]) / width
    variance = (squares[0] + squares[1] + squares[2] + squares[3]) / width - average * average
    scale = lax.rsqrt(variance + 1e-06)
    shifts = [(total / depth - average) * scale for total in totals]
    start = pl.multiple_of(quarters()[3] * share, 128)
    step = 256
    for first in range(0, share, step):
        cols = pl.ds(first, step)
        v = kept[:, cols] + far[0:rows, cols].astype(F32)
        size = share // len(nears)
        v = v + nears[first // size][0:rows, pl.ds(first % size, step)].astype(F32)
        v = v * scale + bias[:, pl.ds(pl.multiple_of(start + first, 128), step)]
        for k in range(4):
            v = v + shifts[k] * gains[k : k + 1, cols]
        inner = 0.7978845608028654 * (v + 0.044715 * (v * v * v))
        hidden = (0.5 * v * (1.0 + jnp.tanh(inner))).astype(BF16).astype(F32)
        out[:, cols] = jnp.sum(hidden, axis=0, keepdims=True)


def pool_kernel(width, row, count, kept, *refs):
    pool_pieces(width, row, kept, refs[:count], *refs[count:])


def pool(width, row, kept, nears, far, told, bias, gains, note):
    share = kept.shape[1]
    args = (kept, *nears, far, told, bias, gains, note)
    return pl.pallas_call(
        lambda *refs: pool_kernel(width, row, len(nears), *refs),
        name="pool",
        out_shape=struct((1, share)),
        in_specs=[WHOLE] * len(args),
        out_specs=WHOLE,
        compiler_params=params(6),
        cost_estimate=cost(),
    )(*args)


def pool_all_kernel(width, count, kept, *refs):
    nears, (far, bias, gains, note, first, second, third, out, part) = refs[:count], refs[count:]
    pool_pieces(width, 0, kept, nears, far, far, bias, gains, note, part)
    z = lax.axis_index("mrow")
    sources = (z, z ^ 1, jnp.where(z < 2, 2, 1), jnp.where(z < 2, 3, 0))
    image = lax.broadcasted_iota(jnp.int32, out.shape, 0)
    total = jnp.zeros(out.shape, F32)
    for source, ref in zip(sources, (first, second, third, part)):
        total = total + jnp.where(image == source * kept.shape[0] // PATCHES, ref[...], 0.0)
    out[...] = total


def pool_all(width, kept, nears, far, bias, gains, note, parts):
    share = kept.shape[1]
    args = (kept, *nears, far, bias, gains, note, *parts)
    return pl.pallas_call(
        lambda *refs: pool_all_kernel(width, len(nears), *refs),
        name="pool_all",
        out_shape=struct((IMAGES, share)),
        in_specs=[WHOLE] * len(args),
        out_specs=WHOLE,
        scratch_shapes=[VMEM((1, share), F32)],
        compiler_params=params(6),
        cost_estimate=cost(),
    )(*args)


def mix_kernel(rows, distant, *refs):
    *shares, other, w, out = refs
    share = shares[0].shape[1]
    mine_x, mine_c = lax.axis_index("mcol"), lax.axis_index("sub")
    x = 1 - mine_x if distant else mine_x
    total = jnp.zeros((16, w.shape[1]), F32)
    for ref, c in zip(shares, (mine_c, 1 - mine_c)):
        start = pl.multiple_of((c * 2 + x) * share, 128)
        terms = jnp.concatenate([*thirds(ref[...] / PATCHES), jnp.zeros((10, share), BF16)], axis=0)
        total = total + jnp.dot(terms, w[pl.ds(start, share), :], preferred_element_type=F32)
    mixed = total[0:2] + (total[2:4] + total[4:6])
    if distant:
        out[...] = mixed + other[...]
    else:
        image = lax.axis_index("mrow") * rows // PATCHES
        row = lax.broadcasted_iota(jnp.int32, mixed.shape, 0)
        out[...] = mixed + jnp.where(row == image, other[...], 0.0)


def mix(rows, distant, first, second, other, w):
    return pl.pallas_call(
        lambda *refs: mix_kernel(rows, distant, *refs),
        name="mix",
        out_shape=struct((IMAGES, w.shape[1])),
        in_specs=[WHOLE] * 4,
        out_specs=WHOLE,
        compiler_params=params(8),
        cost_estimate=cost(),
    )(first, second, other, w)


def score_kernel(own, core, across, both, bias, captions, text_scale, pairs, out):
    depth = own.shape[1]
    width = captions.shape[1]
    mine_x, mine_c = lax.axis_index("mcol"), lax.axis_index("sub")
    pieces = []
    total = jnp.zeros((IMAGES, 1), F32)
    for ref, dx, dc in ((own, 0, 0), (core, 0, 1), (across, 1, 0), (both, 1, 1)):
        x, c = (1 - mine_x if dx else mine_x), (1 - mine_c if dc else mine_c)
        start = pl.multiple_of((x * 2 + c) * depth, 128)
        pooled = ref[...] + bias[:, pl.ds(start, depth)]
        total = total + jnp.sum(pooled * pooled, axis=1, keepdims=True)
        pieces.append((start, pooled))
    scale = lax.rsqrt(total / width + 1e-06)
    similar = jnp.zeros((IMAGES, captions.shape[0]), F32)
    for start, pooled in pieces:
        embedding = (pooled * scale).astype(BF16)
        similar = similar + lax.dot_general(
            embedding, captions[:, pl.ds(start, depth)], (((1,), (1,)), ((), ())), preferred_element_type=F32
        )
    chosen = lax.broadcasted_iota(jnp.int32, similar.shape, 0) == pairs[...]
    picked = jnp.sum(jnp.where(chosen, similar, 0.0), axis=0, keepdims=True)
    out[...] = 100.0 * picked * text_scale[...] / width


def score(own, core, across, both, bias, captions, text_scale, pairs):
    count = captions.shape[0]
    return pl.pallas_call(
        score_kernel,
        name="score",
        out_shape=struct((1, count)),
        in_specs=[WHOLE] * 8,
        out_specs=WHOLE,
        compiler_params=params(8),
        cost_estimate=cost(),
    )(own, core, across, both, bias, captions, text_scale, pairs)


def other_core(name, value):
    with jax.named_scope(name):
        return lax.ppermute(value, "sub", [(0, 1), (1, 0)])


def other_chip(name, value):
    with jax.named_scope(name):
        return lax.ppermute(value, "mcol", [(0, 1), (1, 0)])


def other_both(name, value):
    with jax.named_scope(name):
        return lax.ppermute(value, ("mcol", "sub"), [(0, 3), (1, 2), (2, 1), (3, 0)])


def along(name, value, pairs):
    with jax.named_scope(name):
        return lax.ppermute(value, "mrow", list(pairs))


SWAP = ((0, 1), (1, 0), (2, 3), (3, 2))
MIDDLE = ((1, 2), (2, 1))
OUTWARD = ((1, 0), (2, 3))
SKIP = ((0, 2), (2, 0), (1, 3), (3, 1))
ENDS = ((0, 3), (3, 0), (1, 2), (2, 1))


def after(values, *others):
    return lax.optimization_barrier((values, others))[0]


def staged(tokens, ln_gain, w_in, b_in, w_out, b_out, captions, pairs):
    width = b_out.shape[0]
    rows, depth = tokens.shape
    share = w_in.shape[1] // 4
    bias = b_in.reshape(1, -1)

    near = along("near_rows", tokens, SWAP)
    middle = along("middle_rows", tokens, MIDDLE)

    def chip_sum(index, keep, gots, *others):
        chip, note = small(
            lambda *refs: chip_sum_kernel(index, *refs),
            "chip_sum",
            (struct((rows + (0 if index == 1 else NOTE_ROWS), share), BF16), struct((1, 4 * rows))),
            keep,
            *gots,
            *others,
        )
        return chip, note, other_chip(f"chip_sum_{index}", chip)

    *gives_a, keep_a, keep_gain, sums, held_a, gain = first_a(tokens, ln_gain, w_in)
    gots_a = [other_core("core_sum_0a", give_a) for give_a in gives_a]
    chip_0, note_0, far_0 = chip_sum(0, keep_a, gots_a, sums, keep_gain)
    near = after(near, chip_0)
    middle = after(middle, near)
    passed = along("passed_rows", middle, OUTWARD)
    crossed = along("crossed_rows", near, MIDDLE)

    def later_a(index, rows_of, ready_after, *others):
        halves = (struct((rows + 16, share // 2), BF16), struct((rows, share // 2), BF16))
        *gives, keep, ready, own = later_block(
            lambda *refs: later_a_kernel(len(rows_of), *refs),
            (*rows_of, after(gain, ready_after), held_a),
            (*halves, struct((rows, share)), struct((rows, depth), BF16), struct((1, 2 * rows))),
            4 * rows * depth * share,
        )
        gots = [other_core(f"core_sum_{index}a", give) for give in gives]
        return ready, *chip_sum(index, keep, gots, own, *others)

    def later_b(index, ready, *others):
        ready = lax.optimization_barrier((ready, others))[0]
        pieces = 2 if index == 3 else 1
        return later_block(
            later_b_kernel,
            (ready, give_held, keep_held),
            (struct((rows, share // pieces), BF16),) * pieces + (struct((rows, share)),),
            4 * rows * depth * share,
        )

    def send(index, gives):
        return [other_core(f"core_sum_{index}b", give) for give in gives]

    ready_1, chip_1, note_1, far_1 = later_a(1, (near,), ())
    keep_0, keep_gain, keep_held = first_part(
        first_keep_kernel,
        "first_keep",
        after(tokens, chip_1),
        gain,
        w_in,
        (struct((rows, share)), struct((1, share)), pltpu.VMEM((depth, share), BF16)),
    )
    crossed = after(crossed, keep_0)
    last = along("last_rows", crossed, OUTWARD)

    ready_2, chip_2, note_2, far_2 = later_a(2, (middle, passed), far_0, note_1)
    give_0, give_held, resid = first_part(
        first_give_kernel,
        "first_give",
        after(tokens, chip_2),
        gain,
        w_in,
        (struct((rows + 16, share), BF16), pltpu.VMEM((depth, share), BF16), struct((1, depth))),
    )
    far_1 = after(far_1, give_0)
    give_1, keep_1 = later_b(1, ready_1, far_1)

    ready_3, chip_3, note_3, far_3 = later_a(3, (crossed, last), give_1)
    far_2 = after(far_2, chip_3)
    give_2, keep_2 = later_b(2, ready_2, far_2)
    *gives_3, keep_3 = later_b(3, ready_3, give_2)
    nears_0, nears_1, nears_2, nears_3 = send(0, [give_0]), send(1, [give_1]), send(2, [give_2]), send(3, gives_3)
    gains = small(
        lambda *refs: all_gains_kernel(rows, *refs),
        "all_gains",
        struct((8, share)),
        after(keep_gain, keep_3),
        *nears_0,
        far_0,
    )
    parts = [
        pool(width, 0, keep_0, nears_0, far_0, far_0, bias, gains, note_0),
        pool(width, 3, keep_1, nears_1, far_1, far_2, bias, gains, note_1),
        pool(width, 0, keep_2, nears_2, far_2, far_2, bias, gains, note_2),
    ]
    pooled = pool_all(width, keep_3, nears_3, far_3, bias, gains, note_3, parts)

    core, across, both = other_core("core_pool", pooled), other_chip("chip_pool", pooled), other_both("both_pool", pooled)
    near_mix = mix(rows, False, pooled, core, resid, w_out)
    across, both = after((across, both), near_mix)
    mixed = mix(rows, True, across, both, near_mix, w_out)
    own = mixed + along("swap_mixed", mixed, SWAP) + along("skip_mixed", mixed, SKIP) + along("ends_mixed", mixed, ENDS)
    text_vals = captions.astype(F32)
    text_scale = lax.rsqrt(jnp.mean(text_vals * text_vals, axis=1) + 1e-06)
    scores = score(
        own,
        other_core("core_embed", own),
        other_chip("chip_embed", own),
        other_both("both_embed", own),
        b_out.reshape(1, -1),
        captions,
        text_scale.reshape(1, -1),
        pairs.reshape(1, -1),
    )
    return scores.reshape(-1)


def solution(mesh):
    sizes = dict(mesh.shape)

    def shards(tokens, ln_gain, w_in, *rest):
        rows, depth = tokens.shape
        fits = (
            (sizes["mrow"], sizes["mcol"], sizes["sub"]) == (4, 2, 2)
            and rows == 128
            and PATCHES % rows == 0
            and depth % 256 == 0
            and w_in.shape[1] % 1024 == 0
            and w_in.shape[1] >= 16 * rows
        )
        return (staged if fits else plain)(tokens, ln_gain, w_in, *rest)

    placed = (
        P(("group", "mrow"), ("mcol", "sub")),
        P(("mcol", "sub")),
        P(("mcol", "sub"), "mrow"),
        P("mrow"),
        P("mrow", ("mcol", "sub")),
        P(),
        P(("group", "mrow", "mcol", "sub"), None),
        P(("group", "mrow", "mcol", "sub")),
    )
    return jax.shard_map(
        shards,
        mesh=mesh,
        in_specs=placed,
        out_specs=P(("group", "mrow", "mcol", "sub")),
        check_vma=False,
    )
```

```python
import jax
import jax.numpy as jnp
from jax import lax
from jax.experimental import pallas as pl
from jax.experimental.pallas import tpu as pltpu
from jax.sharding import PartitionSpec as P

PATCHES = 256
IMAGES = 2
F32 = jnp.float32
BF16 = jnp.bfloat16
VMEM = pltpu.VMEM
WHOLE = pl.BlockSpec(memory_space=VMEM)
IN_HBM = pl.BlockSpec(memory_space=pltpu.HBM)
MIB = 1 << 20


def params(mib):
    return pltpu.CompilerParams(vmem_limit_bytes=mib * MIB)


def cost(flops=1024):
    return pl.CostEstimate(flops=flops, bytes_accessed=1024, transcendentals=0)


def struct(shape, dtype=F32):
    return jax.ShapeDtypeStruct(shape, dtype)


def image_table(first_row, count):
    positions = first_row + jnp.arange(count, dtype=jnp.int32)
    return (positions[None, :] // PATCHES == jnp.arange(IMAGES, dtype=jnp.int32)[:, None]).astype(BF16)


def plain(tokens, ln_gain, w_in, b_in, w_out, b_out, captions, pairs):
    width = b_out.shape[0]
    values = tokens.astype(F32)
    totals, squares = lax.psum((jnp.sum(values, axis=1), jnp.sum(values * values, axis=1)), ("mcol", "sub"))
    average = totals / width
    variance = squares / width - average * average
    normed = ((values - average[:, None]) * lax.rsqrt(variance + 1e-06)[:, None] * ln_gain[None, :]).astype(BF16)
    gathered = lax.all_gather(normed, "mrow", axis=0, tiled=True)
    rows = tokens.shape[0]
    col_index = lax.axis_index(("mcol", "sub"))
    resid = jnp.dot(image_table(lax.axis_index("mrow") * rows, rows), tokens, preferred_element_type=F32)
    partial = jnp.dot(gathered, w_in, preferred_element_type=F32).astype(BF16)
    preact = lax.psum_scatter(partial, ("mcol", "sub"), scatter_dimension=1, tiled=True).astype(F32)
    units = preact.shape[1]
    bias = lax.dynamic_slice_in_dim(b_in, col_index * units, units, 0)
    hidden = jax.nn.gelu(preact + bias[None, :], approximate=True).astype(BF16)
    local_pool = jnp.dot(image_table(0, hidden.shape[0]), hidden, preferred_element_type=F32)
    pooled_hidden = lax.all_gather(local_pool, ("mcol", "sub"), axis=1, tiled=True) / PATCHES
    mixed = jnp.dot(pooled_hidden, w_out.astype(F32), precision=lax.Precision.HIGHEST)
    own = lax.psum(resid / PATCHES + mixed, "mrow")
    pooled = lax.all_gather(own, ("mcol", "sub"), axis=1, tiled=True) + b_out[None, :]
    embedding = (pooled * lax.rsqrt(jnp.mean(pooled * pooled, axis=1, keepdims=True) + 1e-06)).astype(BF16)
    similar = jnp.dot(captions, embedding.T, preferred_element_type=F32)
    chosen = pairs[:, None] == jnp.arange(IMAGES, dtype=jnp.int32)[None, :]
    picked = jnp.sum(jnp.where(chosen, similar, 0.0), axis=1)
    text_vals = captions.astype(F32)
    text_scale = lax.rsqrt(jnp.mean(text_vals * text_vals, axis=1) + 1e-06)
    return 100.0 * picked * text_scale / width


def quarters():
    across, core = lax.axis_index("mcol"), lax.axis_index("sub")
    return (
        (1 - core) * 2 + (1 - across),
        core * 2 + (1 - across),
        (1 - core) * 2 + across,
        core * 2 + across,
    )


def centred(values, gain):
    mean = jnp.sum(values, axis=1, keepdims=True) / values.shape[1]
    return ((values - mean) * gain).astype(BF16)


PIECES = 2
NOTE_ROWS = 8


def thirds(value):
    high = value.astype(BF16)
    rest = value - high.astype(F32)
    middle = rest.astype(BF16)
    return high, middle, (rest - middle.astype(F32)).astype(BF16)


def rejoined(terms):
    terms = terms.astype(F32)
    return terms[0:1] + (terms[1:2] + terms[2:3])


def row_sums(values):
    rows = values.shape[0]
    lane = lax.broadcasted_iota(jnp.int32, (rows, 128), 1)
    totals = jnp.sum(values, axis=1, keepdims=True)
    squares = jnp.sum(values * values, axis=1, keepdims=True)
    both = jnp.where(lane == 0, totals, jnp.where(lane == 1, squares, 0.0)).T
    return jnp.concatenate([both[0:1], both[1:2]], axis=1)


def row_block(rows_of, shape):
    padded = [jnp.concatenate([row, jnp.zeros((row.shape[0], shape[1] - row.shape[1]), BF16)], axis=1) if row.shape[1] < shape[1] else row for row in rows_of]
    return jnp.concatenate([*padded, jnp.zeros((shape[0] - len(padded), shape[1]), BF16)], axis=0)


def column_copies(quarter, w, held, sems, first_sem):
    share = held.shape[1]
    size = share // PIECES
    copies = []
    for piece in range(PIECES):
        start = pl.multiple_of(quarter * share + piece * size, 128)
        copies.append(
            pltpu.make_async_copy(
                w.at[:, pl.ds(start, size)], held.at[:, pl.ds(piece * size, size)], sems.at[first_sem + piece]
            )
        )
        copies[-1].start()
    return copies


def with_gain(values, gain):
    high, middle, _ = thirds(gain)
    return jnp.concatenate([centred(values, gain), row_block([high, middle], (16, high.shape[1]))], axis=0)


def first_products(left, held, copies, store):
    rows = left.shape[0] - 16
    size = held.shape[1] // PIECES
    for piece in range(PIECES):
        copies[piece].wait()
        product = jnp.dot(left, held[:, pl.ds(piece * size, size)], preferred_element_type=F32)
        store(piece * size, size, product[:rows], product[rows : rows + 1] + product[rows + 1 : rows + 2])


def first_a_kernel(tokens, gain, w, first, second, keep, keep_gain, sums, held, gain_row, rows_of, line, sems):
    row_copy = pltpu.make_async_copy(tokens, rows_of, sems.at[2 * PIECES])
    line_copy = pltpu.make_async_copy(gain, line, sems.at[2 * PIECES + 1])
    row_copy.start()
    line_copy.start()
    to_give, to_send = quarters()[:2]
    give_copies = column_copies(to_give, w, held.at[0], sems, 0)
    keep_copies = column_copies(to_send, w, held.at[1], sems, PIECES)
    line_copy.wait()
    gain_row[...] = line[...].reshape(gain_row.shape)
    row_copy.wait()
    values = rows_of[...].astype(F32)
    left = with_gain(values, gain_row[...])
    own = row_sums(values)
    sums[...] = own
    rows, half = rows_of.shape[0], first.shape[1]

    def give_store(at, size, product, of_gain):
        ref, cols = (first, second)[at // half], pl.ds(at % half, size)
        ref[0:rows, cols] = product.astype(BF16)
        told = own if at == 0 else jnp.zeros((1, size), F32)
        ref[rows:, cols] = row_block([*thirds(told), *thirds(of_gain)], (16, size))

    def keep_store(at, size, product, of_gain):
        keep[:, pl.ds(at, size)] = product
        keep_gain[:, pl.ds(at, size)] = of_gain

    first_products(left, held.at[0], give_copies, give_store)
    first_products(left, held.at[1], keep_copies, keep_store)


def first_a(tokens, gain, w):
    rows, depth = tokens.shape
    share = w.shape[1] // 4
    return pl.pallas_call(
        first_a_kernel,
        name="first_a",
        out_shape=(
            struct((rows + 16, share // 2), BF16),
            struct((rows + 16, share // 2), BF16),
            struct((rows, share)),
            struct((1, share)),
            struct((1, 2 * rows)),
            pltpu.VMEM((2, depth, share), BF16),
            struct((1, depth)),
        ),
        in_specs=[IN_HBM] * 3,
        out_specs=(WHOLE,) * 7,
        scratch_shapes=[VMEM((rows, depth), BF16), VMEM((depth,), F32), pltpu.SemaphoreType.DMA((2 * PIECES + 2,))],
        compiler_params=params(8),
        cost_estimate=cost(),
    )(*(pltpu.with_memory_space_constraint(value, pltpu.HBM) for value in (tokens, gain, w)))


def first_give_kernel(tokens, gain, w, give, held, resid, sems):
    copies = column_copies(quarters()[2], w, held, sems, 0)
    values = tokens[...].astype(F32)
    rows = values.shape[0]
    resid[...] = jnp.sum(values, axis=0, keepdims=True) / PATCHES

    def store(at, size, product, of_gain):
        give[0:rows, pl.ds(at, size)] = product.astype(BF16)
        give[rows:, pl.ds(at, size)] = row_block(thirds(of_gain), (16, size))

    first_products(with_gain(values, gain[...]), held, copies, store)


def first_keep_kernel(tokens, gain, w, keep, keep_gain, held, sems):
    copies = column_copies(quarters()[3], w, held, sems, 0)

    def store(at, size, product, of_gain):
        keep[:, pl.ds(at, size)] = product
        keep_gain[:, pl.ds(at, size)] = of_gain

    first_products(with_gain(tokens[...].astype(F32), gain[...]), held, copies, store)


def first_part(kernel, name, tokens, gain, w, shapes):
    rows, depth = tokens.shape
    share = w.shape[1] // 4
    return pl.pallas_call(
        kernel,
        name=name,
        out_shape=shapes,
        in_specs=[WHOLE, WHOLE, IN_HBM],
        out_specs=(WHOLE,) * len(shapes),
        scratch_shapes=[pltpu.SemaphoreType.DMA((PIECES,))],
        compiler_params=params(8),
        cost_estimate=cost(),
    )(tokens, gain, pltpu.with_memory_space_constraint(w, pltpu.HBM))


def later_a_kernel(count, *refs):
    blocks, gain, held, (first, second, keep, ready, sums) = refs[:count], refs[count], refs[count + 1], refs[count + 2 :]
    values = blocks[0][...].astype(F32)
    for other in blocks[1:]:
        values = values + other[...].astype(F32)
    rows = values.shape[0]
    left = centred(values, gain[...])
    ready[...] = left
    later_products(left, (held.at[0], held.at[1]), (first, second), keep)
    own = row_sums(values)
    sums[...] = own
    first[rows:, :] = row_block(thirds(own), (16, first.shape[1]))


def later_b_kernel(left, give_held, keep_held, *refs):
    later_products(left[...], (give_held, keep_held), refs[:-1], refs[-1])


def later_products(left, held, gives, keep):
    rows = left.shape[0]
    step = keep.shape[1] // 2
    size = gives[0].shape[1]
    for part in range(2):
        for first in range(0, keep.shape[1], step):
            product = jnp.dot(left, held[part][:, pl.ds(first, step)], preferred_element_type=F32)
            if part == 0:
                gives[first // size][0:rows, pl.ds(first % size, step)] = product.astype(BF16)
            else:
                keep[:, pl.ds(first, step)] = product


def later_block(kernel, args, out, flops):
    rows, share = out[-1].shape if len(out) < 4 else out[2].shape
    depth = args[0].shape[1]
    return pl.pallas_call(
        kernel,
        name="later_block",
        out_shape=out,
        in_specs=[WHOLE] * len(args),
        out_specs=(WHOLE,) * len(out),
        compiler_params=params(8),
        cost_estimate=cost(flops),
    )(*args)


def chip_sum_kernel(slot, kept, first, second, own, *refs):
    *extra, out, note = refs
    rows, share = kept.shape
    half = share // 2
    for index, got in enumerate((first, second)):
        cols = pl.ds(index * half, half)
        out[0:rows, cols] = (kept[:, cols] + got[0:rows, :].astype(F32)).astype(BF16)
    sums = jnp.concatenate([own[...], rejoined(first[rows : rows + 3, 0 : 2 * rows])], axis=1)
    note[...] = sums
    below = list(thirds(sums))
    if slot == 1:
        return
    if slot == 2:
        below.extend(thirds(extra[0][...]))
    if slot == 0:
        below.extend(thirds(extra[0][...])[:2])
        got_gain = jnp.concatenate([rejoined(got[rows + 3 : rows + 6, :]) for got in (first, second)], axis=1)
        below.extend(thirds(got_gain)[:2])
    out[rows:, :] = row_block(below, (NOTE_ROWS, share))


def all_gains_kernel(rows, kept, near, far, gains):
    gains[...] = jnp.zeros(gains.shape, F32)
    gains[0:1, :] = kept[...]
    gains[1:2, :] = rejoined(near[rows : rows + 3, :])
    for index in range(2):
        terms = far[rows + 3 + 2 * index : rows + 5 + 2 * index, :].astype(F32)
        gains[2 + index : 3 + index, :] = terms[0:1] + terms[1:2]


def small(kernel, name, out, *args):
    return pl.pallas_call(
        kernel,
        name=name,
        out_shape=out,
        in_specs=[WHOLE] * len(args),
        out_specs=jax.tree.map(lambda _: WHOLE, out),
        compiler_params=params(4),
        cost_estimate=cost(),
    )(*args)


def pool_pieces(width, row, kept, nears, far, told, bias, gains, note, out):
    rows, share = kept.shape
    depth = width // 4
    all_sums = jnp.concatenate([note[...], rejoined(told[rows + row : rows + row + 3, 0 : 4 * rows])], axis=1)
    lines = [all_sums[:, index * rows : (index + 1) * rows] for index in range(8)]
    columns = jnp.concatenate([*lines, jnp.zeros((120, rows), F32)], axis=0).T
    totals = [columns[:, 2 * k : 2 * k + 1] for k in range(4)]
    squares = [columns[:, 2 * k + 1 : 2 * k + 2] for k in range(4)]
    average = (totals[0] + totals[1] + totals[2] + totals[3]) / width
    variance = (squares[0] + squares[1] + squares[2] + squares[3]) / width - average * average
    scale = lax.rsqrt(variance + 1e-06)
    shifts = [(total / depth - average) * scale for total in totals]
    start = pl.multiple_of(quarters()[3] * share, 128)
    step = 256
    for first in range(0, share, step):
        cols = pl.ds(first, step)
        v = kept[:, cols] + far[0:rows, cols].astype(F32)
        size = share // len(nears)
        v = v + nears[first // size][0:rows, pl.ds(first % size, step)].astype(F32)
        v = v * scale + bias[:, pl.ds(pl.multiple_of(start + first, 128), step)]
        for k in range(4):
            v = v + shifts[k] * gains[k : k + 1, cols]
        inner = 0.7978845608028654 * (v + 0.044715 * (v * v * v))
        hidden = (0.5 * v * (1.0 + jnp.tanh(inner))).astype(BF16).astype(F32)
        out[:, cols] = jnp.sum(hidden, axis=0, keepdims=True)


def pool_kernel(width, row, count, kept, *refs):
    pool_pieces(width, row, kept, refs[:count], *refs[count:])


def pool(width, row, kept, nears, far, told, bias, gains, note):
    share = kept.shape[1]
    args = (kept, *nears, far, told, bias, gains, note)
    return pl.pallas_call(
        lambda *refs: pool_kernel(width, row, len(nears), *refs),
        name="pool",
        out_shape=struct((1, share)),
        in_specs=[WHOLE] * len(args),
        out_specs=WHOLE,
        compiler_params=params(6),
        cost_estimate=cost(),
    )(*args)


def pool_all_kernel(width, count, kept, *refs):
    nears, (far, bias, gains, note, first, second, third, out, part) = refs[:count], refs[count:]
    pool_pieces(width, 0, kept, nears, far, far, bias, gains, note, part)
    z = lax.axis_index("mrow")
    sources = (z, z ^ 1, jnp.where(z < 2, 2, 1), jnp.where(z < 2, 3, 0))
    image = lax.broadcasted_iota(jnp.int32, out.shape, 0)
    total = jnp.zeros(out.shape, F32)
    for source, ref in zip(sources, (first, second, third, part)):
        total = total + jnp.where(image == source * kept.shape[0] // PATCHES, ref[...], 0.0)
    out[...] = total


def pool_all(width, kept, nears, far, bias, gains, note, parts):
    share = kept.shape[1]
    args = (kept, *nears, far, bias, gains, note, *parts)
    return pl.pallas_call(
        lambda *refs: pool_all_kernel(width, len(nears), *refs),
        name="pool_all",
        out_shape=struct((IMAGES, share)),
        in_specs=[WHOLE] * len(args),
        out_specs=WHOLE,
        scratch_shapes=[VMEM((1, share), F32)],
        compiler_params=params(6),
        cost_estimate=cost(),
    )(*args)


def mix_kernel(rows, distant, *refs):
    *shares, other, w, out = refs
    share = shares[0].shape[1]
    mine_x, mine_c = lax.axis_index("mcol"), lax.axis_index("sub")
    x = 1 - mine_x if distant else mine_x
    total = jnp.zeros((16, w.shape[1]), F32)
    for ref, c in zip(shares, (mine_c, 1 - mine_c)):
        start = pl.multiple_of((c * 2 + x) * share, 128)
        terms = jnp.concatenate([*thirds(ref[...] / PATCHES), jnp.zeros((10, share), BF16)], axis=0)
        total = total + jnp.dot(terms, w[pl.ds(start, share), :], preferred_element_type=F32)
    mixed = total[0:2] + (total[2:4] + total[4:6])
    if distant:
        out[...] = mixed + other[...]
    else:
        image = lax.axis_index("mrow") * rows // PATCHES
        row = lax.broadcasted_iota(jnp.int32, mixed.shape, 0)
        out[...] = mixed + jnp.where(row == image, other[...], 0.0)


def mix(rows, distant, first, second, other, w):
    return pl.pallas_call(
        lambda *refs: mix_kernel(rows, distant, *refs),
        name="mix",
        out_shape=struct((IMAGES, w.shape[1])),
        in_specs=[WHOLE] * 4,
        out_specs=WHOLE,
        compiler_params=params(8),
        cost_estimate=cost(),
    )(first, second, other, w)


def score_kernel(own, core, across, both, bias, captions, text_scale, pairs, out):
    depth = own.shape[1]
    width = captions.shape[1]
    mine_x, mine_c = lax.axis_index("mcol"), lax.axis_index("sub")
    pieces = []
    total = jnp.zeros((IMAGES, 1), F32)
    for ref, dx, dc in ((own, 0, 0), (core, 0, 1), (across, 1, 0), (both, 1, 1)):
        x, c = (1 - mine_x if dx else mine_x), (1 - mine_c if dc else mine_c)
        start = pl.multiple_of((x * 2 + c) * depth, 128)
        pooled = ref[...] + bias[:, pl.ds(start, depth)]
        total = total + jnp.sum(pooled * pooled, axis=1, keepdims=True)
        pieces.append((start, pooled))
    terms = jnp.zeros((16, captions.shape[0]), F32)
    for start, pooled in pieces:
        left = jnp.concatenate([*thirds(pooled), jnp.zeros((10, depth), BF16)], axis=0)
        terms = terms + lax.dot_general(
            left, captions[:, pl.ds(start, depth)], (((1,), (1,)), ((), ())), preferred_element_type=F32
        )
    scale = lax.rsqrt(total / width + 1e-06)
    similar = (terms[0:2] + (terms[2:4] + terms[4:6])) * scale
    chosen = lax.broadcasted_iota(jnp.int32, similar.shape, 0) == pairs[...]
    picked = jnp.sum(jnp.where(chosen, similar, 0.0), axis=0, keepdims=True)
    out[...] = 100.0 * picked * text_scale[...] / width


def score(own, core, across, both, bias, captions, text_scale, pairs):
    count = captions.shape[0]
    return pl.pallas_call(
        score_kernel,
        name="score",
        out_shape=struct((1, count)),
        in_specs=[WHOLE] * 8,
        out_specs=WHOLE,
        compiler_params=params(8),
        cost_estimate=cost(),
    )(own, core, across, both, bias, captions, text_scale, pairs)


def other_core(name, value):
    with jax.named_scope(name):
        return lax.ppermute(value, "sub", [(0, 1), (1, 0)])


def other_chip(name, value):
    with jax.named_scope(name):
        return lax.ppermute(value, "mcol", [(0, 1), (1, 0)])


def other_both(name, value):
    with jax.named_scope(name):
        return lax.ppermute(value, ("mcol", "sub"), [(0, 3), (1, 2), (2, 1), (3, 0)])


def along(name, value, pairs):
    with jax.named_scope(name):
        return lax.ppermute(value, "mrow", list(pairs))


SWAP = ((0, 1), (1, 0), (2, 3), (3, 2))
MIDDLE = ((1, 2), (2, 1))
OUTWARD = ((1, 0), (2, 3))
SKIP = ((0, 2), (2, 0), (1, 3), (3, 1))
ENDS = ((0, 3), (3, 0), (1, 2), (2, 1))


def after(values, *others):
    return lax.optimization_barrier((values, others))[0]


def staged(tokens, ln_gain, w_in, b_in, w_out, b_out, captions, pairs):
    width = b_out.shape[0]
    rows, depth = tokens.shape
    share = w_in.shape[1] // 4
    bias = b_in.reshape(1, -1)

    near = along("near_rows", tokens, SWAP)
    middle = along("middle_rows", tokens, MIDDLE)

    def chip_sum(index, keep, gots, *others):
        chip, note = small(
            lambda *refs: chip_sum_kernel(index, *refs),
            "chip_sum",
            (struct((rows + (0 if index == 1 else NOTE_ROWS), share), BF16), struct((1, 4 * rows))),
            keep,
            *gots,
            *others,
        )
        return chip, note, other_chip(f"chip_sum_{index}", chip)

    *gives_a, keep_a, keep_gain, sums, held_a, gain = first_a(tokens, ln_gain, w_in)
    gots_a = [other_core("core_sum_0a", give_a) for give_a in gives_a]
    chip_0, note_0, far_0 = chip_sum(0, keep_a, gots_a, sums, keep_gain)
    near = after(near, chip_0)
    middle = after(middle, near)
    passed = along("passed_rows", middle, OUTWARD)
    crossed = along("crossed_rows", near, MIDDLE)

    def later_a(index, rows_of, ready_after, *others):
        halves = (struct((rows + 16, share // 2), BF16), struct((rows, share // 2), BF16))
        *gives, keep, ready, own = later_block(
            lambda *refs: later_a_kernel(len(rows_of), *refs),
            (*rows_of, after(gain, ready_after), held_a),
            (*halves, struct((rows, share)), struct((rows, depth), BF16), struct((1, 2 * rows))),
            4 * rows * depth * share,
        )
        gots = [other_core(f"core_sum_{index}a", give) for give in gives]
        return ready, *chip_sum(index, keep, gots, own, *others)

    def later_b(index, ready, *others):
        ready = lax.optimization_barrier((ready, others))[0]
        pieces = 2 if index == 3 else 1
        return later_block(
            later_b_kernel,
            (ready, give_held, keep_held),
            (struct((rows, share // pieces), BF16),) * pieces + (struct((rows, share)),),
            4 * rows * depth * share,
        )

    def send(index, gives):
        return [other_core(f"core_sum_{index}b", give) for give in gives]

    ready_1, chip_1, note_1, far_1 = later_a(1, (near,), ())
    keep_0, keep_gain, keep_held = first_part(
        first_keep_kernel,
        "first_keep",
        after(tokens, chip_1),
        gain,
        w_in,
        (struct((rows, share)), struct((1, share)), pltpu.VMEM((depth, share), BF16)),
    )
    crossed = after(crossed, keep_0)
    last = along("last_rows", crossed, OUTWARD)

    ready_2, chip_2, note_2, far_2 = later_a(2, (middle, passed), far_0, note_1)
    give_0, give_held, resid = first_part(
        first_give_kernel,
        "first_give",
        after(tokens, chip_2),
        gain,
        w_in,
        (struct((rows + 16, share), BF16), pltpu.VMEM((depth, share), BF16), struct((1, depth))),
    )
    far_1 = after(far_1, give_0)
    give_1, keep_1 = later_b(1, ready_1, far_1)

    ready_3, chip_3, note_3, far_3 = later_a(3, (crossed, last), give_1)
    far_2 = after(far_2, chip_3)
    give_2, keep_2 = later_b(2, ready_2, far_2)
    *gives_3, keep_3 = later_b(3, ready_3, give_2)
    nears_0, nears_1, nears_2, nears_3 = send(0, [give_0]), send(1, [give_1]), send(2, [give_2]), send(3, gives_3)
    gains = small(
        lambda *refs: all_gains_kernel(rows, *refs),
        "all_gains",
        struct((8, share)),
        after(keep_gain, keep_3),
        *nears_0,
        far_0,
    )
    parts = [
        pool(width, 0, keep_0, nears_0, far_0, far_0, bias, gains, note_0),
        pool(width, 3, keep_1, nears_1, far_1, far_2, bias, gains, note_1),
        pool(width, 0, keep_2, nears_2, far_2, far_2, bias, gains, note_2),
    ]
    pooled = pool_all(width, keep_3, nears_3, far_3, bias, gains, note_3, parts)

    core, across, both = other_core("core_pool", pooled), other_chip("chip_pool", pooled), other_both("both_pool", pooled)
    near_mix = mix(rows, False, pooled, core, resid, w_out)
    across, both = after((across, both), near_mix)
    mixed = mix(rows, True, across, both, near_mix, w_out)
    own = mixed + along("swap_mixed", mixed, SWAP) + along("skip_mixed", mixed, SKIP) + along("ends_mixed", mixed, ENDS)
    text_vals = captions.astype(F32)
    text_scale = lax.rsqrt(jnp.mean(text_vals * text_vals, axis=1) + 1e-06)
    scores = score(
        own,
        other_core("core_embed", own),
        other_chip("chip_embed", own),
        other_both("both_embed", own),
        b_out.reshape(1, -1),
        captions,
        text_scale.reshape(1, -1),
        pairs.reshape(1, -1),
    )
    return scores.reshape(-1)


def solution(mesh):
    sizes = dict(mesh.shape)

    def shards(tokens, ln_gain, w_in, *rest):
        rows, depth = tokens.shape
        fits = (
            (sizes["mrow"], sizes["mcol"], sizes["sub"]) == (4, 2, 2)
            and rows == 128
            and PATCHES % rows == 0
            and depth % 256 == 0
            and w_in.shape[1] % 1024 == 0
            and w_in.shape[1] >= 16 * rows
        )
        return (staged if fits else plain)(tokens, ln_gain, w_in, *rest)

    placed = (
        P(("group", "mrow"), ("mcol", "sub")),
        P(("mcol", "sub")),
        P(("mcol", "sub"), "mrow"),
        P("mrow"),
        P("mrow", ("mcol", "sub")),
        P(),
        P(("group", "mrow", "mcol", "sub"), None),
        P(("group", "mrow", "mcol", "sub")),
    )
    return jax.shard_map(
        shards,
        mesh=mesh,
        in_specs=placed,
        out_specs=P(("group", "mrow", "mcol", "sub")),
        check_vma=False,
    )
```

```python
import jax
import jax.numpy as jnp
from jax import lax
from jax.experimental import pallas as pl
from jax.experimental.pallas import tpu as pltpu
from jax.sharding import PartitionSpec as P

PATCHES = 256
IMAGES = 2
F32 = jnp.float32
BF16 = jnp.bfloat16
VMEM = pltpu.VMEM
WHOLE = pl.BlockSpec(memory_space=VMEM)
IN_HBM = pl.BlockSpec(memory_space=pltpu.HBM)
MIB = 1 << 20


def params(mib):
    return pltpu.CompilerParams(vmem_limit_bytes=mib * MIB)


def cost(flops=1024):
    return pl.CostEstimate(flops=flops, bytes_accessed=1024, transcendentals=0)


def struct(shape, dtype=F32):
    return jax.ShapeDtypeStruct(shape, dtype)


def image_table(first_row, count):
    positions = first_row + jnp.arange(count, dtype=jnp.int32)
    return (positions[None, :] // PATCHES == jnp.arange(IMAGES, dtype=jnp.int32)[:, None]).astype(BF16)


def plain(tokens, ln_gain, w_in, b_in, w_out, b_out, captions, pairs):
    width = b_out.shape[0]
    values = tokens.astype(F32)
    totals, squares = lax.psum((jnp.sum(values, axis=1), jnp.sum(values * values, axis=1)), ("mcol", "sub"))
    average = totals / width
    variance = squares / width - average * average
    normed = ((values - average[:, None]) * lax.rsqrt(variance + 1e-06)[:, None] * ln_gain[None, :]).astype(BF16)
    gathered = lax.all_gather(normed, "mrow", axis=0, tiled=True)
    rows = tokens.shape[0]
    col_index = lax.axis_index(("mcol", "sub"))
    resid = jnp.dot(image_table(lax.axis_index("mrow") * rows, rows), tokens, preferred_element_type=F32)
    partial = jnp.dot(gathered, w_in, preferred_element_type=F32).astype(BF16)
    preact = lax.psum_scatter(partial, ("mcol", "sub"), scatter_dimension=1, tiled=True).astype(F32)
    units = preact.shape[1]
    bias = lax.dynamic_slice_in_dim(b_in, col_index * units, units, 0)
    hidden = jax.nn.gelu(preact + bias[None, :], approximate=True).astype(BF16)
    local_pool = jnp.dot(image_table(0, hidden.shape[0]), hidden, preferred_element_type=F32)
    pooled_hidden = lax.all_gather(local_pool, ("mcol", "sub"), axis=1, tiled=True) / PATCHES
    mixed = jnp.dot(pooled_hidden, w_out.astype(F32), precision=lax.Precision.HIGHEST)
    own = lax.psum(resid / PATCHES + mixed, "mrow")
    pooled = lax.all_gather(own, ("mcol", "sub"), axis=1, tiled=True) + b_out[None, :]
    embedding = (pooled * lax.rsqrt(jnp.mean(pooled * pooled, axis=1, keepdims=True) + 1e-06)).astype(BF16)
    similar = jnp.dot(captions, embedding.T, preferred_element_type=F32)
    chosen = pairs[:, None] == jnp.arange(IMAGES, dtype=jnp.int32)[None, :]
    picked = jnp.sum(jnp.where(chosen, similar, 0.0), axis=1)
    text_vals = captions.astype(F32)
    text_scale = lax.rsqrt(jnp.mean(text_vals * text_vals, axis=1) + 1e-06)
    return 100.0 * picked * text_scale / width


def quarters():
    across, core = lax.axis_index("mcol"), lax.axis_index("sub")
    return (
        (1 - core) * 2 + (1 - across),
        core * 2 + (1 - across),
        (1 - core) * 2 + across,
        core * 2 + across,
    )


def centred(values, gain):
    mean = jnp.sum(values, axis=1, keepdims=True) / values.shape[1]
    return ((values - mean) * gain).astype(BF16)


PIECES = 2
NOTE_ROWS = 8


def thirds(value):
    high = value.astype(BF16)
    rest = value - high.astype(F32)
    middle = rest.astype(BF16)
    return high, middle, (rest - middle.astype(F32)).astype(BF16)


def rejoined(terms):
    terms = terms.astype(F32)
    return terms[0:1] + (terms[1:2] + terms[2:3])


def row_sums(values):
    rows = values.shape[0]
    lane = lax.broadcasted_iota(jnp.int32, (rows, 128), 1)
    totals = jnp.sum(values, axis=1, keepdims=True)
    squares = jnp.sum(values * values, axis=1, keepdims=True)
    both = jnp.where(lane == 0, totals, jnp.where(lane == 1, squares, 0.0)).T
    return jnp.concatenate([both[0:1], both[1:2]], axis=1)


def row_block(rows_of, shape):
    padded = [jnp.concatenate([row, jnp.zeros((row.shape[0], shape[1] - row.shape[1]), BF16)], axis=1) if row.shape[1] < shape[1] else row for row in rows_of]
    return jnp.concatenate([*padded, jnp.zeros((shape[0] - len(padded), shape[1]), BF16)], axis=0)


def column_copies(quarter, w, held, sems, first_sem):
    share = held.shape[1]
    size = share // PIECES
    copies = []
    for piece in range(PIECES):
        start = pl.multiple_of(quarter * share + piece * size, 128)
        copies.append(
            pltpu.make_async_copy(
                w.at[:, pl.ds(start, size)], held.at[:, pl.ds(piece * size, size)], sems.at[first_sem + piece]
            )
        )
        copies[-1].start()
    return copies


def with_gain(values, gain):
    high, middle, _ = thirds(gain)
    return jnp.concatenate([centred(values, gain), row_block([high, middle], (16, high.shape[1]))], axis=0)


def first_products(left, held, copies, store):
    rows = left.shape[0] - 16
    size = held.shape[1] // PIECES
    for piece in range(PIECES):
        copies[piece].wait()
        product = jnp.dot(left, held[:, pl.ds(piece * size, size)], preferred_element_type=F32)
        store(piece * size, size, product[:rows], product[rows : rows + 1] + product[rows + 1 : rows + 2])


def first_a_kernel(tokens, gain, w, first, second, keep, keep_gain, sums, held, gain_row, rows_of, line, sems):
    row_copy = pltpu.make_async_copy(tokens, rows_of, sems.at[2 * PIECES])
    line_copy = pltpu.make_async_copy(gain, line, sems.at[2 * PIECES + 1])
    row_copy.start()
    line_copy.start()
    to_give, to_send = quarters()[:2]
    give_copies = column_copies(to_give, w, held.at[0], sems, 0)
    keep_copies = column_copies(to_send, w, held.at[1], sems, PIECES)
    line_copy.wait()
    gain_row[...] = line[...].reshape(gain_row.shape)
    row_copy.wait()
    values = rows_of[...].astype(F32)
    left = with_gain(values, gain_row[...])
    own = row_sums(values)
    sums[...] = own
    rows, half = rows_of.shape[0], first.shape[1]

    def give_store(at, size, product, of_gain):
        ref, cols = (first, second)[at // half], pl.ds(at % half, size)
        ref[0:rows, cols] = product.astype(BF16)
        told = own if at == 0 else jnp.zeros((1, size), F32)
        ref[rows:, cols] = row_block([*thirds(told), *thirds(of_gain)], (16, size))

    def keep_store(at, size, product, of_gain):
        keep[:, pl.ds(at, size)] = product
        keep_gain[:, pl.ds(at, size)] = of_gain

    first_products(left, held.at[0], give_copies, give_store)
    first_products(left, held.at[1], keep_copies, keep_store)


def first_a(tokens, gain, w):
    rows, depth = tokens.shape
    share = w.shape[1] // 4
    return pl.pallas_call(
        first_a_kernel,
        name="first_a",
        out_shape=(
            struct((rows + 16, share // 2), BF16),
            struct((rows + 16, share // 2), BF16),
            struct((rows, share)),
            struct((1, share)),
            struct((1, 2 * rows)),
            pltpu.VMEM((2, depth, share), BF16),
            struct((1, depth)),
        ),
        in_specs=[IN_HBM] * 3,
        out_specs=(WHOLE,) * 7,
        scratch_shapes=[VMEM((rows, depth), BF16), VMEM((depth,), F32), pltpu.SemaphoreType.DMA((2 * PIECES + 2,))],
        compiler_params=params(8),
        cost_estimate=cost(),
    )(*(pltpu.with_memory_space_constraint(value, pltpu.HBM) for value in (tokens, gain, w)))


def first_give_kernel(tokens, gain, w, give, held, resid, sems):
    copies = column_copies(quarters()[2], w, held, sems, 0)
    values = tokens[...].astype(F32)
    rows = values.shape[0]
    resid[...] = jnp.sum(values, axis=0, keepdims=True) / PATCHES

    def store(at, size, product, of_gain):
        give[0:rows, pl.ds(at, size)] = product.astype(BF16)
        give[rows:, pl.ds(at, size)] = row_block(thirds(of_gain), (16, size))

    first_products(with_gain(values, gain[...]), held, copies, store)


def first_keep_kernel(tokens, gain, w, keep, keep_gain, held, sems):
    copies = column_copies(quarters()[3], w, held, sems, 0)

    def store(at, size, product, of_gain):
        keep[:, pl.ds(at, size)] = product
        keep_gain[:, pl.ds(at, size)] = of_gain

    first_products(with_gain(tokens[...].astype(F32), gain[...]), held, copies, store)


def first_part(kernel, name, tokens, gain, w, shapes):
    rows, depth = tokens.shape
    share = w.shape[1] // 4
    return pl.pallas_call(
        kernel,
        name=name,
        out_shape=shapes,
        in_specs=[WHOLE, WHOLE, IN_HBM],
        out_specs=(WHOLE,) * len(shapes),
        scratch_shapes=[pltpu.SemaphoreType.DMA((PIECES,))],
        compiler_params=params(8),
        cost_estimate=cost(),
    )(tokens, gain, pltpu.with_memory_space_constraint(w, pltpu.HBM))


def later_a_kernel(count, *refs):
    blocks, gain, held, (first, second, keep, ready, sums) = refs[:count], refs[count], refs[count + 1], refs[count + 2 :]
    values = blocks[0][...].astype(F32)
    for other in blocks[1:]:
        values = values + other[...].astype(F32)
    rows = values.shape[0]
    left = centred(values, gain[...])
    ready[...] = left
    later_products(left, (held.at[0], held.at[1]), (first, second), keep)
    own = row_sums(values)
    sums[...] = own
    first[rows:, :] = row_block(thirds(own), (16, first.shape[1]))


def later_b_kernel(left, give_held, keep_held, *refs):
    later_products(left[...], (give_held, keep_held), refs[:-1], refs[-1])


def later_products(left, held, gives, keep):
    rows = left.shape[0]
    step = keep.shape[1] // 2
    size = gives[0].shape[1]
    for part in range(2):
        for first in range(0, keep.shape[1], step):
            product = jnp.dot(left, held[part][:, pl.ds(first, step)], preferred_element_type=F32)
            if part == 0:
                gives[first // size][0:rows, pl.ds(first % size, step)] = product.astype(BF16)
            else:
                keep[:, pl.ds(first, step)] = product


def later_block(kernel, args, out, flops):
    rows, share = out[-1].shape if len(out) < 4 else out[2].shape
    depth = args[0].shape[1]
    return pl.pallas_call(
        kernel,
        name="later_block",
        out_shape=out,
        in_specs=[WHOLE] * len(args),
        out_specs=(WHOLE,) * len(out),
        compiler_params=params(8),
        cost_estimate=cost(flops),
    )(*args)


def chip_sum_kernel(slot, kept, first, second, own, *refs):
    *extra, out, note = refs
    rows, share = kept.shape
    half = share // 2
    for index, got in enumerate((first, second)):
        cols = pl.ds(index * half, half)
        out[0:rows, cols] = (kept[:, cols] + got[0:rows, :].astype(F32)).astype(BF16)
    sums = jnp.concatenate([own[...], rejoined(first[rows : rows + 3, 0 : 2 * rows])], axis=1)
    note[...] = sums
    below = list(thirds(sums))
    if slot == 1:
        return
    if slot == 2:
        below.extend(thirds(extra[0][...]))
    if slot == 0:
        below.extend(thirds(extra[0][...])[:2])
        got_gain = jnp.concatenate([rejoined(got[rows + 3 : rows + 6, :]) for got in (first, second)], axis=1)
        below.extend(thirds(got_gain)[:2])
    out[rows:, :] = row_block(below, (NOTE_ROWS, share))


def all_gains_kernel(rows, kept, near, far, gains):
    gains[...] = jnp.zeros(gains.shape, F32)
    gains[0:1, :] = kept[...]
    gains[1:2, :] = rejoined(near[rows : rows + 3, :])
    for index in range(2):
        terms = far[rows + 3 + 2 * index : rows + 5 + 2 * index, :].astype(F32)
        gains[2 + index : 3 + index, :] = terms[0:1] + terms[1:2]


def small(kernel, name, out, *args):
    return pl.pallas_call(
        kernel,
        name=name,
        out_shape=out,
        in_specs=[WHOLE] * len(args),
        out_specs=jax.tree.map(lambda _: WHOLE, out),
        compiler_params=params(4),
        cost_estimate=cost(),
    )(*args)


def pool_pieces(width, row, kept, nears, far, told, bias, gains, note, out):
    rows, share = kept.shape
    depth = width // 4
    all_sums = jnp.concatenate([note[...], rejoined(told[rows + row : rows + row + 3, 0 : 4 * rows])], axis=1)
    lines = [all_sums[:, index * rows : (index + 1) * rows] for index in range(8)]
    columns = jnp.concatenate([*lines, jnp.zeros((120, rows), F32)], axis=0).T
    totals = [columns[:, 2 * k : 2 * k + 1] for k in range(4)]
    squares = [columns[:, 2 * k + 1 : 2 * k + 2] for k in range(4)]
    average = (totals[0] + totals[1] + totals[2] + totals[3]) / width
    variance = (squares[0] + squares[1] + squares[2] + squares[3]) / width - average * average
    scale = lax.rsqrt(variance + 1e-06)
    shifts = [(total / depth - average) * scale for total in totals]
    start = pl.multiple_of(quarters()[3] * share, 128)
    step = 256
    for first in range(0, share, step):
        cols = pl.ds(first, step)
        v = kept[:, cols] + far[0:rows, cols].astype(F32)
        size = share // len(nears)
        v = v + nears[first // size][0:rows, pl.ds(first % size, step)].astype(F32)
        v = v * scale + bias[:, pl.ds(pl.multiple_of(start + first, 128), step)]
        for k in range(4):
            v = v + shifts[k] * gains[k : k + 1, cols]
        inner = 0.7978845608028654 * (v + 0.044715 * (v * v * v))
        hidden = (0.5 * v * (1.0 + jnp.tanh(inner))).astype(BF16).astype(F32)
        out[:, cols] = jnp.sum(hidden, axis=0, keepdims=True)


def pool_kernel(width, row, count, kept, *refs):
    pool_pieces(width, row, kept, refs[:count], *refs[count:])


def pool(width, row, kept, nears, far, told, bias, gains, note):
    share = kept.shape[1]
    args = (kept, *nears, far, told, bias, gains, note)
    return pl.pallas_call(
        lambda *refs: pool_kernel(width, row, len(nears), *refs),
        name="pool",
        out_shape=struct((1, share)),
        in_specs=[WHOLE] * len(args),
        out_specs=WHOLE,
        compiler_params=params(6),
        cost_estimate=cost(),
    )(*args)


def pool_all_kernel(width, count, kept, *refs):
    nears, (far, bias, gains, note, first, second, third, out, part) = refs[:count], refs[count:]
    pool_pieces(width, 0, kept, nears, far, far, bias, gains, note, part)
    z = lax.axis_index("mrow")
    sources = (z, z ^ 1, jnp.where(z < 2, 2, 1), jnp.where(z < 2, 3, 0))
    image = lax.broadcasted_iota(jnp.int32, out.shape, 0)
    total = jnp.zeros(out.shape, F32)
    for source, ref in zip(sources, (first, second, third, part)):
        total = total + jnp.where(image == source * kept.shape[0] // PATCHES, ref[...], 0.0)
    out[...] = total


def pool_all(width, kept, nears, far, bias, gains, note, parts):
    share = kept.shape[1]
    args = (kept, *nears, far, bias, gains, note, *parts)
    return pl.pallas_call(
        lambda *refs: pool_all_kernel(width, len(nears), *refs),
        name="pool_all",
        out_shape=struct((IMAGES, share)),
        in_specs=[WHOLE] * len(args),
        out_specs=WHOLE,
        scratch_shapes=[VMEM((1, share), F32)],
        compiler_params=params(6),
        cost_estimate=cost(),
    )(*args)


def mix_kernel(rows, places, *refs):
    *shares, other, w, out = refs
    share = shares[0].shape[1]
    mine_x, mine_c = lax.axis_index("mcol"), lax.axis_index("sub")
    total = jnp.zeros((16, w.shape[1]), F32)
    for ref, (dx, dc) in zip(shares, places):
        x, c = (1 - mine_x if dx else mine_x), (1 - mine_c if dc else mine_c)
        start = pl.multiple_of((c * 2 + x) * share, 128)
        terms = jnp.concatenate([*thirds(ref[...] / PATCHES), jnp.zeros((10, share), BF16)], axis=0)
        total = total + jnp.dot(terms, w[pl.ds(start, share), :], preferred_element_type=F32)
    mixed = total[0:2] + (total[2:4] + total[4:6])
    if places[0] == (0, 0):
        image = lax.axis_index("mrow") * rows // PATCHES
        row = lax.broadcasted_iota(jnp.int32, mixed.shape, 0)
        out[...] = mixed + jnp.where(row == image, other[...], 0.0)
    else:
        out[...] = mixed + other[...]


def mix(rows, places, shares, other, w):
    return pl.pallas_call(
        lambda *refs: mix_kernel(rows, places, *refs),
        name="mix",
        out_shape=struct((IMAGES, w.shape[1])),
        in_specs=[WHOLE] * (len(shares) + 2),
        out_specs=WHOLE,
        compiler_params=params(8),
        cost_estimate=cost(),
    )(*shares, other, w)


def score_kernel(own, core, across, both, bias, captions, text_scale, pairs, out):
    depth = own.shape[1]
    width = captions.shape[1]
    mine_x, mine_c = lax.axis_index("mcol"), lax.axis_index("sub")
    pieces = []
    total = jnp.zeros((IMAGES, 1), F32)
    for ref, dx, dc in ((own, 0, 0), (core, 0, 1), (across, 1, 0), (both, 1, 1)):
        x, c = (1 - mine_x if dx else mine_x), (1 - mine_c if dc else mine_c)
        start = pl.multiple_of((x * 2 + c) * depth, 128)
        pooled = ref[...] + bias[:, pl.ds(start, depth)]
        total = total + jnp.sum(pooled * pooled, axis=1, keepdims=True)
        pieces.append((start, pooled))
    scale = lax.rsqrt(total / width + 1e-06)
    similar = jnp.zeros((IMAGES, captions.shape[0]), F32)
    for start, pooled in pieces:
        embedding = (pooled * scale).astype(BF16)
        similar = similar + lax.dot_general(
            embedding, captions[:, pl.ds(start, depth)], (((1,), (1,)), ((), ())), preferred_element_type=F32
        )
    chosen = lax.broadcasted_iota(jnp.int32, similar.shape, 0) == pairs[...]
    picked = jnp.sum(jnp.where(chosen, similar, 0.0), axis=0, keepdims=True)
    out[...] = 100.0 * picked * text_scale[...] / width


def score(own, core, across, both, bias, captions, text_scale, pairs):
    count = captions.shape[0]
    return pl.pallas_call(
        score_kernel,
        name="score",
        out_shape=struct((1, count)),
        in_specs=[WHOLE] * 8,
        out_specs=WHOLE,
        compiler_params=params(8),
        cost_estimate=cost(),
    )(own, core, across, both, bias, captions, text_scale, pairs)


def other_core(name, value):
    with jax.named_scope(name):
        return lax.ppermute(value, "sub", [(0, 1), (1, 0)])


def other_chip(name, value):
    with jax.named_scope(name):
        return lax.ppermute(value, "mcol", [(0, 1), (1, 0)])


def other_both(name, value):
    with jax.named_scope(name):
        return lax.ppermute(value, ("mcol", "sub"), [(0, 3), (1, 2), (2, 1), (3, 0)])


def along(name, value, pairs):
    with jax.named_scope(name):
        return lax.ppermute(value, "mrow", list(pairs))


SWAP = ((0, 1), (1, 0), (2, 3), (3, 2))
MIDDLE = ((1, 2), (2, 1))
OUTWARD = ((1, 0), (2, 3))
SKIP = ((0, 2), (2, 0), (1, 3), (3, 1))
ENDS = ((0, 3), (3, 0), (1, 2), (2, 1))


def after(values, *others):
    return lax.optimization_barrier((values, others))[0]


def staged(tokens, ln_gain, w_in, b_in, w_out, b_out, captions, pairs):
    width = b_out.shape[0]
    rows, depth = tokens.shape
    share = w_in.shape[1] // 4
    bias = b_in.reshape(1, -1)

    near = along("near_rows", tokens, SWAP)
    middle = along("middle_rows", tokens, MIDDLE)

    def chip_sum(index, keep, gots, *others):
        chip, note = small(
            lambda *refs: chip_sum_kernel(index, *refs),
            "chip_sum",
            (struct((rows + (0 if index == 1 else NOTE_ROWS), share), BF16), struct((1, 4 * rows))),
            keep,
            *gots,
            *others,
        )
        return chip, note, other_chip(f"chip_sum_{index}", chip)

    *gives_a, keep_a, keep_gain, sums, held_a, gain = first_a(tokens, ln_gain, w_in)
    gots_a = [other_core("core_sum_0a", give_a) for give_a in gives_a]
    chip_0, note_0, far_0 = chip_sum(0, keep_a, gots_a, sums, keep_gain)
    near = after(near, chip_0)
    middle = after(middle, near)
    passed = along("passed_rows", middle, OUTWARD)
    crossed = along("crossed_rows", near, MIDDLE)

    def later_a(index, rows_of, ready_after, *others):
        halves = (struct((rows + 16, share // 2), BF16), struct((rows, share // 2), BF16))
        *gives, keep, ready, own = later_block(
            lambda *refs: later_a_kernel(len(rows_of), *refs),
            (*rows_of, after(gain, ready_after), held_a),
            (*halves, struct((rows, share)), struct((rows, depth), BF16), struct((1, 2 * rows))),
            4 * rows * depth * share,
        )
        gots = [other_core(f"core_sum_{index}a", give) for give in gives]
        return ready, *chip_sum(index, keep, gots, own, *others)

    def later_b(index, ready, *others):
        ready = lax.optimization_barrier((ready, others))[0]
        pieces = 2 if index == 3 else 1
        return later_block(
            later_b_kernel,
            (ready, give_held, keep_held),
            (struct((rows, share // pieces), BF16),) * pieces + (struct((rows, share)),),
            4 * rows * depth * share,
        )

    def send(index, gives):
        return [other_core(f"core_sum_{index}b", give) for give in gives]

    ready_1, chip_1, note_1, far_1 = later_a(1, (near,), ())
    keep_0, keep_gain, keep_held = first_part(
        first_keep_kernel,
        "first_keep",
        after(tokens, chip_1),
        gain,
        w_in,
        (struct((rows, share)), struct((1, share)), pltpu.VMEM((depth, share), BF16)),
    )
    crossed = after(crossed, keep_0)
    last = along("last_rows", crossed, OUTWARD)

    ready_2, chip_2, note_2, far_2 = later_a(2, (middle, passed), far_0, note_1)
    give_0, give_held, resid = first_part(
        first_give_kernel,
        "first_give",
        after(tokens, chip_2),
        gain,
        w_in,
        (struct((rows + 16, share), BF16), pltpu.VMEM((depth, share), BF16), struct((1, depth))),
    )
    far_1 = after(far_1, give_0)
    give_1, keep_1 = later_b(1, ready_1, far_1)

    ready_3, chip_3, note_3, far_3 = later_a(3, (crossed, last), give_1)
    far_2 = after(far_2, chip_3)
    give_2, keep_2 = later_b(2, ready_2, far_2)
    *gives_3, keep_3 = later_b(3, ready_3, give_2)
    nears_0, nears_1, nears_2, nears_3 = send(0, [give_0]), send(1, [give_1]), send(2, [give_2]), send(3, gives_3)
    gains = small(
        lambda *refs: all_gains_kernel(rows, *refs),
        "all_gains",
        struct((8, share)),
        after(keep_gain, keep_3),
        *nears_0,
        far_0,
    )
    parts = [
        pool(width, 0, keep_0, nears_0, far_0, far_0, bias, gains, note_0),
        pool(width, 3, keep_1, nears_1, far_1, far_2, bias, gains, note_1),
        pool(width, 0, keep_2, nears_2, far_2, far_2, bias, gains, note_2),
    ]
    pooled = pool_all(width, keep_3, nears_3, far_3, bias, gains, note_3, parts)

    core, across, both = other_core("core_pool", pooled), other_chip("chip_pool", pooled), other_both("both_pool", pooled)
    mixed = mix(rows, ((0, 0), (0, 1)), (pooled, core), resid, w_out)
    across, both = after(across, mixed), after(both, mixed)
    mixed = mix(rows, ((1, 0),), (across,), mixed, w_out)
    mixed = mix(rows, ((1, 1),), (after(both, mixed),), mixed, w_out)
    own = mixed + along("swap_mixed", mixed, SWAP) + along("skip_mixed", mixed, SKIP) + along("ends_mixed", mixed, ENDS)
    text_vals = captions.astype(F32)
    text_scale = lax.rsqrt(jnp.mean(text_vals * text_vals, axis=1) + 1e-06)
    scores = score(
        own,
        other_core("core_embed", own),
        other_chip("chip_embed", own),
        other_both("both_embed", own),
        b_out.reshape(1, -1),
        captions,
        text_scale.reshape(1, -1),
        pairs.reshape(1, -1),
    )
    return scores.reshape(-1)


def solution(mesh):
    sizes = dict(mesh.shape)

    def shards(tokens, ln_gain, w_in, *rest):
        rows, depth = tokens.shape
        fits = (
            (sizes["mrow"], sizes["mcol"], sizes["sub"]) == (4, 2, 2)
            and rows == 128
            and PATCHES % rows == 0
            and depth % 256 == 0
            and w_in.shape[1] % 1024 == 0
            and w_in.shape[1] >= 16 * rows
        )
        return (staged if fits else plain)(tokens, ln_gain, w_in, *rest)

    placed = (
        P(("group", "mrow"), ("mcol", "sub")),
        P(("mcol", "sub")),
        P(("mcol", "sub"), "mrow"),
        P("mrow"),
        P("mrow", ("mcol", "sub")),
        P(),
        P(("group", "mrow", "mcol", "sub"), None),
        P(("group", "mrow", "mcol", "sub")),
    )
    return jax.shard_map(
        shards,
        mesh=mesh,
        in_specs=placed,
        out_specs=P(("group", "mrow", "mcol", "sub")),
        check_vma=False,
    )
```
